256 devices in a mesh: table: 32 (over z, x), task: 4 (over y), fsdp: 2 (over core).
Axes of the slice: x: 4, y: 4, z: 8, core: 2. Of those that a mesh axis runs over, the one named last changes fastest.
Arguments:
- raw_ids: int32 [16384, 4, 16], P(('table', 'fsdp'), 'task'), may hold values from 0 to 524287, as said below
- bag_len: int32 [16384, 4], P(('table', 'fsdp'), 'task'), may hold values from 1 to 16, as said below
- labels: int32 [16384, 4], P(('table', 'fsdp'), 'task'), may hold values 0 or 1
- emb_table: bfloat16 [4, 262144, 128], P('task', ('table', 'fsdp')), may hold values from -6 to 6
- bucket_map: int32 [4, 524288], P('task', ('table', 'fsdp')), may hold values from 0 to 4095, as said below
- spec_weight: bfloat16 [4, 512, 4096], P('task', 'fsdp'), may hold values from -0.25 to 0.25
- shared_weight: bfloat16 [4, 512, 4096], P('task', 'fsdp'), may hold values from -0.25 to 0.25
- gate_weight: bfloat16 [4, 512, 5], replicated, may hold values from -1 to 1
- tower_weight: bfloat16 [4, 4096, 256], P('task', 'fsdp'), may hold values from -0.09375 to 0.09375
- head_vector: bfloat16 [4, 256], P('task'), may hold values from -1.5 to 1.5
Outputs:
- logits: float32 [16384, 4], P(('table', 'fsdp'), 'task')
- table_grad: float32 [4, 262144, 128], P('task', ('table', 'fsdp'))
The draws below stay inside these ranges and needn't reach their ends.
Inputs may be any that keep to these rules, and one draw needn't show every extreme that they name: `raw_ids`: raw id r belongs to block r // 8192. For each field, the samples of one device along table and fsdp name raw ids of one block in exactly 192 live slots and in no dead slot; that block is the same for all devices of a field. Counting all 16 slots of every bag, they name every other block at most 192 times, the remaining slots spread as evenly as possible over the other blocks. `bag_len`: most bags are nearly full; some hold a single live slot. bucket_map[f, r] is a row within the block of r. In each block and field, the rows from 16 up are named by exactly one raw id each; all other raw ids of the block name rows below 16, the shared default buckets.
All inputs are finite; a program needn't handle non-finite values. No bound on the sum of `labels` on one device may be relied on, other than what follows from the above.
Results may differ from the reference program's by a relative error of at most 0.02.
Values may be sent and summed in bfloat16 or wider, within the bound.
No kernel may reach another device: no remote copies, remote signals or barrier semaphores. Data moves between devices by JAX's collectives and lax.ppermute only.
A program may use at most 128 MiB of HBM per device.

```python
import jax
import jax.numpy as jnp
from jax import lax

SAMP_DEV = 256
BAG = 16
EMB = 128
D = 4096
TH = 256
ROWS_DEV = 4096
NDEF = 16
TASKS = 4
FIELDS = 4
GATE_WAYS = 5
IN = 512
OWNERS = 64
SAMPLES = 16384
RAW_DEV = 8192
ROWS = 262144


def bag_lengths(key):
    key_len, key_one = jax.random.split(key)
    lengths = jax.random.randint(key_len, (SAMPLES, FIELDS), BAG - 3, BAG + 1).astype(jnp.int32)
    odd_sample = (jnp.arange(SAMPLES, dtype=jnp.int32) % 2 == 1)[:, None]
    planted = jax.random.randint(key_one, (SAMPLES, FIELDS), 0, 8) == 0
    return jnp.where(odd_sample & planted, 1, lengths).astype(jnp.int32)


def draw_bag_len(key, part):
    return bag_lengths(key)


def draw_bucket_map(key, part):
    key = jax.random.fold_in(key, 11)
    subkeys = jax.random.split(key, FIELDS * OWNERS)
    permuted = jax.vmap(lambda subkey: jax.random.permutation(subkey, RAW_DEV))(subkeys)
    frequent = ROWS_DEV - NDEF
    row_vals = jnp.where(permuted < frequent, NDEF + permuted, permuted % NDEF)
    return row_vals.reshape(FIELDS, OWNERS * RAW_DEV).astype(jnp.int32)


def draw_raw_ids(key, part):
    lengths = bag_lengths(key)
    key = jax.random.fold_in(key, 23)
    positions = SAMP_DEV * BAG
    capacity = 3 * positions // OWNERS
    others = OWNERS - 1
    key_hot, key_order, key_local = jax.random.split(key, 3)
    hot_owner = jax.random.randint(key_hot, (FIELDS,), 0, OWNERS).astype(jnp.int32)
    order_keys = jax.random.split(key_order, OWNERS * FIELDS)
    shuffled = jax.vmap(lambda subkey: jax.random.permutation(subkey, positions))(order_keys)
    shuffled = shuffled.reshape(OWNERS, FIELDS, positions).astype(jnp.int32)
    length_block = lengths.reshape(OWNERS, SAMP_DEV, FIELDS).transpose(0, 2, 1)
    slot_live = jnp.arange(BAG, dtype=jnp.int32)[None, None, None, :] < length_block[..., None]
    slot_live = slot_live.reshape(OWNERS, FIELDS, positions)
    score = jnp.where(slot_live, 0, positions).astype(jnp.int32) + shuffled
    order = jnp.argsort(score, axis=2, stable=True)
    ranks = jnp.argsort(order, axis=2, stable=True).astype(jnp.int32)
    rotation = (others - 1 - (positions - 1 - capacity)) % others
    low_rank = capacity + -rotation % others
    spare_index = (ranks - capacity + rotation) % others
    hot_wide = hot_owner[None, :, None]
    other_owner = spare_index + (spare_index >= hot_wide).astype(jnp.int32)
    owner_ids = jnp.where(ranks < capacity, hot_wide, other_owner)
    local_ids = jax.random.randint(key_local, (OWNERS, FIELDS, positions), 0, RAW_DEV).astype(jnp.int32)
    local_ids = jnp.where((ranks == 0) | (ranks == positions - 1), RAW_DEV - 1, local_ids)
    local_ids = jnp.where((ranks == 1) | (ranks == low_rank), 0, local_ids)
    raw_all = owner_ids * RAW_DEV + local_ids
    raw_all = raw_all.reshape(OWNERS, FIELDS, SAMP_DEV, BAG).transpose(0, 2, 1, 3)
    return raw_all.reshape(SAMPLES, FIELDS, BAG).astype(jnp.int32)


def set_ends(values, own_key, low, largest):
    extent = values.shape
    spot = [jax.random.randint(jax.random.fold_in(own_key, axis), (), 0, extent[axis]) for axis in range(len(extent))]
    values = values.at[tuple(spot)].set(low)
    longest = extent.index(max(extent))
    spot[longest] = (spot[longest] + 1) % extent[longest]
    return values.at[tuple(spot)].set(largest)


def steps_of(stream_key, shape, pieces, low, high):
    level = 1.0
    for position, blocks in pieces:
        steps = jax.random.uniform(jax.random.fold_in(jax.random.fold_in(stream_key, 6), position), (blocks,), jnp.float32, low / len(pieces), high / len(pieces))
        level = level * jnp.repeat(jnp.exp(steps), shape[position] // blocks).reshape((-1,) + (1,) * (len(shape) - 1 - position))
    return level


def noise(key, dims, width, limit, cuts=(), held_as=jnp.bfloat16):
    values = jax.random.normal(key, dims, jnp.float32) * width
    if len(cuts) > 0:
        values = steps_of(key, dims, cuts, -0.22, 0.18) * values
    return jnp.clip(values, min=-limit, max=limit).astype(held_as)


def setup_inputs(seed: int = 0) -> dict:
    arg_keys = jax.random.split(jax.random.key(seed), 11)
    return {
        "raw_ids": draw_raw_ids(jax.random.fold_in(arg_keys[10], 71), 0),
        "bag_len": draw_bag_len(jax.random.fold_in(arg_keys[10], 71), 0),
        "labels": set_ends((jax.random.randint(arg_keys[2], (SAMPLES, TASKS), 0, 4) < 1).astype(jnp.int32), jax.random.fold_in(arg_keys[2], 1), 0, 1),
        "emb_table": noise(arg_keys[3], (FIELDS, ROWS, EMB), 1.0, 6.0, ((0, 4), (1, 64))),
        "bucket_map": draw_bucket_map(jax.random.fold_in(arg_keys[10], 71), 0),
        "spec_weight": noise(arg_keys[5], (TASKS, IN, D), IN ** -0.5, 0.25, ((0, 4), (1, 2))),
        "shared_weight": noise(arg_keys[6], (TASKS, IN, D), IN ** -0.5, 0.25, ((0, 4), (1, 2))),
        "gate_weight": noise(arg_keys[7], (TASKS, IN, GATE_WAYS), (IN // 16) ** -0.5, 1.0),
        "tower_weight": noise(arg_keys[8], (TASKS, D, TH), D ** -0.5, 0.09375, ((0, 4), (1, 2))),
        "head_vector": noise(arg_keys[9], (TASKS, TH), (TH // 16) ** -0.5, 1.5, ((0, 4),)),
    }


loss_scale = 1024.0
highest = lax.Precision.HIGHEST


def swish_slope(value):
    sigmoid_val = jax.nn.sigmoid(value)
    return sigmoid_val * (1.0 + value * (1.0 - sigmoid_val))


def rounded(value):
    return lax.optimization_barrier(value.astype(jnp.bfloat16)).astype(jnp.float32)


def dense_block(inputs, emb_table, spec_wide, shared_wide, gate_wide, tower_wide, head_wide):
    row_ids, live_slot, bag_count, targets = inputs
    field_count = row_ids.shape[1]
    picked = emb_table[jnp.arange(field_count, dtype=jnp.int32)[None, :, None], row_ids]
    summed = jnp.sum(jnp.where(live_slot[..., None], picked.astype(jnp.float32), 0.0), axis=2)
    pooled = (summed / bag_count[..., None]).astype(jnp.bfloat16)
    features = pooled.reshape(pooled.shape[0], -1).astype(jnp.float32)
    spec_input = jnp.einsum("si,tid->tsd", features, spec_wide, precision=highest)
    shared_input = jnp.einsum("si,kid->ksd", features, shared_wide, precision=highest)
    spec_out = rounded(jax.nn.silu(spec_input))
    shared_out = rounded(jax.nn.silu(shared_input))
    scores = jnp.einsum("si,tig->tsg", features, gate_wide, precision=highest)
    raised = jnp.exp(scores)
    gate_mix = raised / jnp.sum(raised, axis=2, keepdims=True)
    spec_proj = jnp.einsum("tsd,tdh->tsh", spec_out, tower_wide, precision=highest)
    shared_proj = jnp.einsum("ksd,tdh->tksh", shared_out, tower_wide, precision=highest)
    shared_gate = jnp.transpose(gate_mix[:, :, 1:], (0, 2, 1))[..., None]
    tower_pre = gate_mix[:, :, 0:1] * spec_proj + jnp.sum(shared_gate * shared_proj, axis=1)
    logits = jnp.einsum("tsh,th->st", jax.nn.silu(tower_pre), head_wide, precision=highest)
    logit_grad = loss_scale * (jax.nn.sigmoid(logits) - targets.astype(jnp.float32))
    pre_grad = rounded(logit_grad.T[:, :, None] * head_wide[:, None, :] * swish_slope(tower_pre))
    gate_grad = jnp.concatenate(
        [jnp.sum(pre_grad * spec_proj, axis=2)[..., None],
         jnp.transpose(jnp.sum(pre_grad[:, None] * shared_proj, axis=3), (0, 2, 1))], axis=2)
    score_grad = gate_mix * (gate_grad - jnp.sum(gate_mix * gate_grad, axis=2, keepdims=True))
    back_grad = jnp.einsum("tsh,tdh->tsd", pre_grad, tower_wide, precision=highest)
    spec_grad = rounded(gate_mix[:, :, 0:1] * back_grad)
    shared_grad = jnp.sum(rounded(shared_gate * back_grad[:, None]), axis=0)
    spec_inner = rounded(spec_grad * swish_slope(spec_input))
    shared_inner = rounded(shared_grad * swish_slope(shared_input))
    field_grad = jnp.einsum("tsd,tid->si", spec_inner, spec_wide, precision=highest)
    field_grad = field_grad + jnp.einsum("ksd,kid->si", shared_inner, shared_wide, precision=highest)
    field_grad = field_grad + jnp.einsum("tsg,tig->si", score_grad, gate_wide, precision=highest)
    lookup_grad = (field_grad.reshape(bag_count.shape[0], field_count, -1) / bag_count[..., None]).astype(jnp.bfloat16)
    return logits, lookup_grad


def reference(raw_ids, bag_len, labels, emb_table, bucket_map, spec_weight, shared_weight, gate_weight, tower_weight, head_vector):
    sample_count = raw_ids.shape[0]
    field_count = raw_ids.shape[1]
    slot_count = raw_ids.shape[2]
    block_of = (raw_ids // RAW_DEV).astype(jnp.int32)
    local_row = bucket_map[jnp.arange(field_count, dtype=jnp.int32)[None, :, None], raw_ids]
    row_ids = (block_of * ROWS_DEV + local_row).astype(jnp.int32)
    live_slot = jnp.arange(slot_count, dtype=jnp.int32)[None, None, :] < bag_len[:, :, None]
    bag_count = bag_len.astype(jnp.float32)
    block_rows = min(sample_count, 512)
    block_total = sample_count // block_rows
    spec_wide = spec_weight.astype(jnp.float32)
    shared_wide = shared_weight.astype(jnp.float32)
    gate_wide = gate_weight.astype(jnp.float32)
    tower_wide = tower_weight.astype(jnp.float32)
    head_wide = head_vector.astype(jnp.float32)

    def run_block(inputs):
        return dense_block(inputs, emb_table, spec_wide, shared_wide, gate_wide, tower_wide, head_wide)

    logits, lookup_grad = lax.map(run_block, (
        row_ids.reshape(block_total, block_rows, field_count, slot_count),
        live_slot.reshape(block_total, block_rows, field_count, slot_count),
        bag_count.reshape(block_total, block_rows, field_count),
        labels.reshape(block_total, block_rows, -1)))
    logits = logits.reshape(sample_count, -1)
    lookup_grad = lookup_grad.reshape(sample_count, field_count, -1)
    gradients = []
    for field in range(field_count):
        slot_terms = jnp.where(live_slot[:, field, :, None], lookup_grad[:, field, None, :].astype(jnp.float32), 0.0)
        gradients.append(jax.ops.segment_sum(
            slot_terms.reshape(sample_count * slot_count, -1),
            row_ids[:, field, :].reshape(-1), num_segments=emb_table.shape[1]))
    return logits, jnp.stack(gradients)
```

```python
import functools

import jax
import jax.numpy as jnp
from jax import lax
from jax.experimental import pallas as pl
from jax.experimental.pallas import tpu as pltpu
from jax.sharding import PartitionSpec as P

loss_scale = 1024.0
highest = lax.Precision.HIGHEST
contract_last = (((1,), (1,)), ((), ()))
bf16 = jnp.bfloat16
f32 = jnp.float32
i32 = jnp.int32
OWNERS = 64
CAP = 64
HOT_CAP = 192
HOT_LANES = 256
RAW_BITS = 13
PIECE_ROWS = 528
VMEM = pl.BlockSpec(memory_space=pltpu.VMEM)
SMEM = pl.BlockSpec(memory_space=pltpu.SMEM)


def params(mib):
    return pltpu.CompilerParams(vmem_limit_bytes=mib * 1024 * 1024)


def iota(shape, dim):
    return lax.broadcasted_iota(i32, shape, dim)


def dot(left, right):
    return jnp.dot(left, right, preferred_element_type=f32)


def dot_last(left, right):
    return lax.dot_general(left, right, contract_last, preferred_element_type=f32)


def one_hot(mask):
    return jnp.where(mask, 1.0, 0.0).astype(bf16)


def bucket_kernel(ids_ref, len_ref, req_ref, hot_ref):
    slots, samples = ids_ref.shape
    owner_row = iota((OWNERS, samples), 0)
    sample1 = (iota((1, samples), 1) + 1).astype(f32)
    before = one_hot(iota((samples, samples), 0) < iota((samples, samples), 1))
    rank_row = iota((HOT_CAP, samples), 0)
    lens = len_ref[...]
    base = jnp.zeros((OWNERS, 1), f32)
    total = jnp.zeros((3 * OWNERS, HOT_CAP), f32)
    for slot in range(slots):
        ids = ids_ref[slot : slot + 1, :]
        owner = jnp.where(lens > slot, ids >> RAW_BITS, -1)
        hit = owner_row == owner
        hit_f = jnp.where(hit, 1.0, 0.0)
        seen = dot(hit_f.astype(bf16), before) + base
        base = base + jnp.sum(hit_f, axis=1, keepdims=True)
        rank = jnp.sum(hit_f * seen, axis=0, keepdims=True).astype(i32)
        raw = ids & ((1 << RAW_BITS) - 1)
        planes = jnp.concatenate(
            [
                hit_f * (raw >> 7).astype(f32),
                hit_f * (raw & 127).astype(f32),
                hit_f * sample1,
            ],
            axis=0,
        ).astype(bf16)
        total = total + dot_last(planes, one_hot(rank_row == rank))
    hot = base > float(CAP)
    high, low, samp = total[:OWNERS], total[OWNERS : 2 * OWNERS], total[2 * OWNERS :]
    cold = jnp.where(hot, 0.0, 1.0)
    warm = 1.0 - cold
    raw_all = high * 128.0 + low
    req_ref[...] = ((samp * cold)[:, :CAP].astype(i32) << 16) + (raw_all * cold)[:, :CAP].astype(
        i32
    )
    hot_samp = jnp.sum(samp * warm, axis=0, keepdims=True).astype(i32)
    hot_raw = jnp.sum(raw_all * warm, axis=0, keepdims=True).astype(i32)
    index = jnp.sum(warm * iota((OWNERS, 1), 0).astype(f32), axis=0, keepdims=True)
    pad = jnp.broadcast_to(index.astype(i32), (1, HOT_LANES - HOT_CAP))
    hot_ref[...] = jnp.concatenate([(hot_samp << 16) + hot_raw, pad], axis=1)


def map_rows(code, map_t):
    lanes = code.shape[1]
    raw = code & 0xFFFF
    spread = one_hot(iota((64, lanes), 0) == (raw >> 7))
    both = dot(map_t, spread)
    wide = both[:128] * 64.0 + both[128:]
    return jnp.sum(
        jnp.where(iota((128, lanes), 0) == (raw & 127), wide, 0.0), axis=0, keepdims=True
    )


def as_column(row):
    return jnp.broadcast_to(row, (128, row.shape[1])).T


def low_one_hot(low):
    lane = iota(low.shape, 1)
    return jnp.concatenate([one_hot(low == lane), one_hot(low == lane + 128)], axis=1)


def pick_rows(spread, high, table_pair, pairs):
    found = jnp.zeros((spread.shape[0], 128), f32)
    for pair in range(pairs):
        both = dot(spread, table_pair(pair))
        found = jnp.where(high == 2 * pair, both[:, :128], found)
        found = jnp.where(high == 2 * pair + 1, both[:, 128:], found)
    return found


def gather_kernel(req_ref, map_ref, table_ref, out_ref, spread_ref, high_ref):
    map_t = map_ref[...]
    chunks = req_ref.shape[0]

    @pl.loop(0, chunks // 4)
    def _(group):
        for part in range(4):
            chunk = group * 4 + part
            code = req_ref[pl.ds(chunk, 1), :]
            row = jnp.where(code >= 65536, map_rows(code, map_t), -1.0)
            column = as_column(row).astype(i32)
            place = pl.ds(pl.multiple_of(chunk * 128, 128), 128)
            spread_ref[place, :] = low_one_hot(column & 255)
            high_ref[place, :] = column >> 8

    block = 512

    @pl.loop(0, out_ref.shape[0] // block)
    def _(step):
        place = pl.ds(pl.multiple_of(step * block, block), block)

        def table_pair(pair):
            return jnp.concatenate(
                [
                    table_ref[pair * 512 : pair * 512 + 256, :],
                    table_ref[pair * 512 + 256 : pair * 512 + 512, :],
                ],
                axis=1,
            )

        out_ref[place, :] = pick_rows(
            spread_ref[place, :], high_ref[place, :], table_pair, 8
        ).astype(bf16)


def map_kernel(code_ref, map_ref, row_ref, samp_ref):
    map_t = map_ref[...]

    @pl.loop(0, code_ref.shape[0] // 4)
    def _(group):
        for part in range(4):
            place = pl.ds(group * 4 + part, 1)
            code = code_ref[place, :]
            row_ref[place, :] = map_rows(code, map_t).astype(i32)
            samp_ref[place, :] = (code >> 16) - 1


def pool_kernel(place_ref, req_ref, hot_ref, rows_ref, own_ref, sib_ref, len_ref, out_ref):
    samples = out_ref.shape[0]
    sample_col = iota((samples, 128), 0)
    summed = jnp.zeros((samples, 128), f32)
    for pair in range(req_ref.shape[0] // 2):
        parts = [
            one_hot(sample_col == (req_ref[2 * pair + half : 2 * pair + half + 1, :] >> 16) - 1)
            for half in range(2)
        ]
        summed = summed + dot(
            jnp.concatenate(parts, axis=1), rows_ref[pair * 256 : pair * 256 + 256, :]
        )
    across, core = place_ref[1], place_ref[2]

    def piece(index, start, size):
        half, slot = index // 4, (across - index % 4) & 3
        own = own_ref[slot, start : start + size, :].astype(f32)
        sib = sib_ref[slot, start : start + size, :].astype(f32)
        return jnp.where(core == half, own, sib)

    planes = [
        jnp.concatenate([piece(4 * plane + part, 512, 16) for part in range(4)], axis=0).T
        for plane in range(2)
    ]
    map_t = jnp.concatenate(planes, axis=0).astype(bf16)
    code = jnp.where(iota((1, HOT_LANES), 1) < HOT_CAP, hot_ref[...], 0)
    row = jnp.where(code >= 65536, map_rows(code, map_t), -1.0)
    column = as_column(row).astype(i32)

    def table_pair(pair):
        return jnp.concatenate(
            [piece(pair, 0, 256), piece(pair, 256, 256)], axis=1
        ).astype(bf16)

    hot_rows = pick_rows(low_one_hot(column & 255), column >> 8, table_pair, 8).astype(bf16)
    spread = one_hot(iota((samples, HOT_LANES), 0) == (code >> 16) - 1)
    summed = summed + dot(spread, hot_rows)
    out_ref[...] = (summed / len_ref[...].astype(f32)).astype(bf16)


def scatter_kernel(steps, place_ref, row_ref, samp_ref, *refs):
    count = len(steps)
    grads = refs[: 2 * count]
    if len(refs) == 2 * count + 3:
        out_ref, wide_ref, spread_ref = refs[2 * count :]
        out_ref[...] = jnp.zeros_like(out_ref)
    else:
        seen_ref, out_ref, wide_ref, spread_ref = refs[2 * count :]
        out_ref[...] = seen_ref[...]
    depth, across, core, chunks = place_ref[0], place_ref[1], place_ref[2], place_ref[3]
    lane = iota((1, 128), 1)
    offset = jnp.where(lane < 64, core * 256, (1 - core) * 256)
    lane_wide = iota((128, 128), 1)
    low_row = iota((256, 128), 0)
    for index, step in enumerate(steps):
        own_ref, sib_ref = grads[2 * index], grads[2 * index + 1]
        level = ((depth - step) & 7) * 4

        @pl.loop(0, chunks)
        def _(chunk):
            for shift in range(4):
                block = level + ((across - shift) & 3)
                row = row_ref[block, pl.ds(chunk, 1), :]
                samp = samp_ref[block, pl.ds(chunk, 1), :]
                samp = jnp.where(samp < 0, -1, samp + offset)
                samp_col = as_column(samp.astype(f32)).astype(i32)
                high_col = as_column((row >> 8).astype(f32)).astype(i32)
                picks = jnp.concatenate(
                    [one_hot(samp_col == lane_wide + 128 * part) for part in range(4)], axis=1
                )
                source = jnp.concatenate([own_ref[shift], sib_ref[shift]], axis=0)
                slots = dot(picks, source)
                place = slice(shift * 128, shift * 128 + 128)
                for high in range(16):
                    wide_ref[place, high * 128 : high * 128 + 128] = jnp.where(
                        high_col == high, slots, 0.0
                    ).astype(bf16)
                spread_ref[:, place] = one_hot(low_row == (row & 255))
            spread = spread_ref[...]
            for pair in range(8):
                both = dot(spread, wide_ref[:, pair * 256 : pair * 256 + 256])
                start = pair * 512
                out_ref[start : start + 256, :] += both[:, :128]
                out_ref[start + 256 : start + 512, :] += both[:, 128:]


def scatter_call(steps, place, rows, samps, grads, seen):
    operands = [place, rows, samps, *grads]
    aliases = {}
    if seen is not None:
        operands.append(seen)
        aliases = {len(operands) - 1: 0}
    return pl.pallas_call(
        functools.partial(scatter_kernel, steps),
        out_shape=jax.ShapeDtypeStruct((4096, 128), f32),
        in_specs=[SMEM] + [VMEM] * (len(operands) - 1),
        out_specs=VMEM,
        scratch_shapes=[pltpu.VMEM((512, 2048), bf16), pltpu.VMEM((256, 512), bf16)],
        input_output_aliases=aliases,
        compiler_params=params(32),
    )(*operands)


def swish_slope(value):
    sigmoid_val = jax.nn.sigmoid(value)
    return sigmoid_val * (1.0 + value * (1.0 - sigmoid_val))


def ring(size, shift):
    return [(i, (i + shift) % size) for i in range(size)]


def along_task(value, shift):
    return lax.ppermute(value, "task", ring(4, shift))


def across_core(value):
    return lax.ppermute(value, "fsdp", [(0, 1), (1, 0)])


def along_x(value, shift):
    return lax.ppermute(
        value, "table", [(z * 4 + x, z * 4 + (x + shift) % 4) for z in range(8) for x in range(4)]
    )


def along_z(value, shift):
    return lax.ppermute(
        value,
        "table",
        [(z * 4 + x, (z + shift) % 8 * 4 + x) for z in range(8) for x in range(4)],
    )


def at(stack, index):
    return lax.dynamic_index_in_dim(stack, index, 0, keepdims=False)


def local(
    raw_ids,
    bag_len,
    labels,
    emb_table,
    bucket_map,
    spec_weight,
    shared_weight,
    gate_weight,
    tower_weight,
    head_vector,
):
    task = lax.axis_index("task")
    core = lax.axis_index("fsdp")
    table_index = lax.axis_index("table")
    depth, across = table_index // 4, table_index % 4
    me = table_index * 2 + core
    samples = raw_ids.shape[0]
    lookups = OWNERS * CAP

    tower_all = lax.all_gather(tower_weight[0], ("task", "fsdp"), axis=0, tiled=True)
    tower_all = tower_all.reshape(4, 4096, 256)
    spec_sib = across_core(spec_weight[0])
    shared_sib = across_core(shared_weight[0])

    def joined(own, sib):
        return jnp.concatenate(
            [jnp.where(core == 0, own, sib), jnp.where(core == 0, sib, own)], axis=0
        )

    ids_t = raw_ids[:, 0, :].T
    req, hot_row = pl.pallas_call(
        bucket_kernel,
        out_shape=(
            jax.ShapeDtypeStruct((OWNERS, CAP), i32),
            jax.ShapeDtypeStruct((1, HOT_LANES), i32),
        ),
        in_specs=[VMEM] * 2,
        out_specs=(VMEM, VMEM),
        compiler_params=params(16),
    )(ids_t, bag_len.reshape(1, samples))
    hot_index = hot_row[0, HOT_CAP]
    hot_z, hot_x, hot_c = hot_index // 8, hot_index // 2 % 4, hot_index % 2
    away_z, away_x = (depth - hot_z) % 8, (across - hot_x) % 4

    row_map = bucket_map[0].reshape(64, 128)
    planes = jnp.concatenate([row_map >> 6, row_map & 63], axis=0).astype(bf16)
    map_t = jnp.concatenate([(row_map >> 6).T, (row_map & 63).T], axis=0).astype(bf16)
    shard_rows = emb_table[0]

    pieces = jnp.concatenate(
        [shard_rows.reshape(8, 512, 128), planes.reshape(8, 16, 128)], axis=1
    ).reshape(2, 4, PIECE_ROWS, 128)
    half = jnp.where(hot_c == core, at(pieces, core), across_core(at(pieces, 1 - core)))

    asked = lax.all_to_all(req, ("table", "fsdp"), split_axis=0, concat_axis=0, tiled=True)
    asked = asked.reshape(lookups // 128, 128)

    quarters = [at(half, across)] + [
        along_x(at(half, (across + shift) % 4), shift) for shift in (1, 2, 3)
    ]
    part = lax.select_n(away_x, *quarters)
    part = lax.select_n(
        jnp.where(away_z == 1, 1, jnp.where(away_z == 7, 2, 0)),
        part,
        along_z(part, 1),
        along_z(part, 7),
    )
    part = lax.select_n(
        jnp.where((away_z >= 2) & (away_z <= 4), 1, jnp.where((away_z == 5) | (away_z == 6), 2, 0)),
        part,
        along_z(part, 3),
        along_z(part, 5),
    )
    hot_own = jnp.stack([part] + [along_x(part, shift) for shift in (1, 2, 3)])
    hot_sib = across_core(hot_own)

    fetched = pl.pallas_call(
        gather_kernel,
        out_shape=jax.ShapeDtypeStruct((lookups, 128), bf16),
        in_specs=[VMEM] * 3,
        out_specs=VMEM,
        scratch_shapes=[pltpu.VMEM((lookups, 256), bf16), pltpu.VMEM((lookups, 128), i32)],
        compiler_params=params(32),
    )(asked, map_t, shard_rows)
    returned = lax.all_to_all(
        fetched.reshape(OWNERS, CAP, 128),
        ("table", "fsdp"),
        split_axis=0,
        concat_axis=0,
        tiled=True,
    ).reshape(lookups, 128)

    place = jnp.stack([depth, across, core]).astype(i32)
    pooled = pl.pallas_call(
        pool_kernel,
        out_shape=jax.ShapeDtypeStruct((samples, 128), bf16),
        in_specs=[SMEM] + [VMEM] * 6,
        out_specs=VMEM,
        compiler_params=params(32),
    )(place, req.reshape(lookups // 128, 128), hot_row, returned, hot_own, hot_sib, bag_len)

    hot_all = lax.all_gather(hot_row[0, :HOT_CAP], ("table", "fsdp"), axis=0, tiled=False)
    is_hot = hot_index == me
    hot_codes = hot_all.reshape(32, 2, 3, 64).transpose(0, 2, 1, 3).reshape(32, 3, 128)
    cold_codes = jnp.pad(asked[:, None, :], ((0, 0), (0, 2), (0, 0)))
    codes = jnp.where(is_hot, hot_codes, cold_codes).reshape(96, 128)
    rows, samps = pl.pallas_call(
        map_kernel,
        out_shape=(jax.ShapeDtypeStruct((96, 128), i32),) * 2,
        in_specs=[VMEM] * 2,
        out_specs=(VMEM, VMEM),
        compiler_params=params(16),
    )(codes, map_t)
    rows, samps = rows.reshape(32, 3, 128), samps.reshape(32, 3, 128)

    felt = jnp.stack([pooled] + [along_task(pooled, shift) for shift in (1, 2, 3)])
    features = jnp.concatenate([at(felt, (task - field) % 4) for field in range(4)], axis=1)
    spec_full = joined(spec_weight[0], spec_sib)
    shared_full = joined(shared_weight[0], shared_sib)
    tower_own = at(tower_all, task)
    targets = labels[:, 0].astype(f32)
    head_row = head_vector[0].astype(f32)

    spec_input = dot(features, spec_full)
    shared_input = dot(features, shared_full)
    spec_out = jax.nn.silu(spec_input).astype(bf16)
    shared_out = jax.nn.silu(shared_input).astype(bf16)
    scores = jnp.einsum("si,tig->tsg", features, gate_weight, preferred_element_type=f32)
    raised = jnp.exp(scores)
    gate_mix = raised / jnp.sum(raised, axis=-1, keepdims=True)
    mix_shared = lax.dynamic_index_in_dim(gate_mix, task + 1, 2, keepdims=True)
    mix_own = at(gate_mix, task)
    spec_proj = dot(spec_out, tower_own)
    shared_proj = jnp.einsum("sd,tdh->tsh", shared_out, tower_all, preferred_element_type=f32)
    partial = mix_shared * shared_proj
    own_partial = at(partial, task) + mix_own[:, 0:1] * spec_proj
    sent = partial.astype(bf16)
    tower_pre = own_partial
    for shift in (1, 2, 3):
        tower_pre = tower_pre + along_task(at(sent, (task + shift) % 4), shift).astype(f32)
    logit_own = jnp.sum(jax.nn.silu(tower_pre) * head_row[None, :], axis=1)
    logit_grad = loss_scale * (jax.nn.sigmoid(logit_own) - targets)
    pre_grad = (logit_grad[:, None] * head_row[None, :] * swish_slope(tower_pre)).astype(bf16)
    pre_rel = jnp.stack([pre_grad] + [along_task(pre_grad, shift) for shift in (1, 2, 3)])
    pre_all = jnp.stack([at(pre_rel, (task - other) % 4) for other in range(4)])
    pre_wide = pre_grad.astype(f32)
    balance = jnp.sum(pre_wide * tower_pre, axis=1, keepdims=True)
    shared_score = mix_shared[:, :, 0].T * jnp.sum(pre_all.astype(f32) * shared_proj, axis=2).T
    spec_score = mix_own[:, 0:1] * jnp.sum(pre_wide * spec_proj, axis=1, keepdims=True)
    spec_grad = dot_last((mix_own[:, 0:1] * pre_wide).astype(bf16), tower_own)
    weighted = (mix_shared * pre_all.astype(f32)).astype(bf16)
    shared_grad = jnp.einsum("tsh,tdh->sd", weighted, tower_all, preferred_element_type=f32)
    spec_inner = (spec_grad * swish_slope(spec_input)).astype(bf16)
    shared_inner = (shared_grad * swish_slope(shared_input)).astype(bf16)
    gate_f = gate_weight.astype(f32)
    gate_own = at(gate_f, task)
    gate_shared = lax.dynamic_index_in_dim(gate_f, task + 1, 2, keepdims=False)
    score_grad = jnp.concatenate(
        [shared_score, spec_score, -mix_own * balance], axis=1
    )
    score_weight = jnp.concatenate([gate_shared, gate_own[:, 0:1].T, gate_own.T], axis=0)
    field_parts = (
        dot_last(spec_inner, spec_full)
        + dot_last(shared_inner, shared_full)
        + jnp.dot(score_grad, score_weight, precision=highest, preferred_element_type=f32)
    )
    blocks = field_parts.reshape(samples, 4, 128)
    blocks = jnp.moveaxis(blocks, 1, 0)
    field_grad = at(blocks, task)
    sent_blocks = blocks.astype(bf16)
    for shift in (1, 2, 3):
        field_grad = field_grad + along_task(at(sent_blocks, (task + shift) % 4), shift).astype(f32)
    lookup_grad = (field_grad / bag_len.astype(f32)).astype(bf16)

    place4 = jnp.stack([depth, across, core, jnp.where(is_hot, 3, 1)]).astype(i32)
    near = jnp.stack([lookup_grad] + [along_x(lookup_grad, shift) for shift in (1, 2, 3)])
    near_sib = across_core(near)
    table_grad = scatter_call((0,), place4, rows, samps, [near, near_sib], None)
    up, down = near, near
    for step in (1, 2, 3):
        up, down = along_z(up, 1), along_z(down, 7)
        up_sib, down_sib = across_core(up), across_core(down)
        table_grad = scatter_call(
            (step, -step), place4, rows, samps, [up, up_sib, down, down_sib], table_grad
        )
    far = jnp.concatenate([along_z(up[:2], 1), along_z(down[2:], 7)], axis=0)
    far_sib = across_core(far)
    table_grad = scatter_call((4,), place4, rows, samps, [far, far_sib], table_grad)
    return (logit_own[:, None], table_grad[None])


def solution(mesh):
    return jax.shard_map(
        local,
        mesh=mesh,
        in_specs=(
            P(("table", "fsdp"), "task", None),
            P(("table", "fsdp"), "task"),
            P(("table", "fsdp"), "task"),
            P("task", ("table", "fsdp"), None),
            P("task", ("table", "fsdp")),
            P("task", "fsdp", None),
            P("task", "fsdp", None),
            P(),
            P("task", "fsdp", None),
            P("task", None),
        ),
        out_specs=(P(("table", "fsdp"), "task"), P("task", ("table", "fsdp"), None)),
        check_vma=False,
    )
```

```python
import functools

import jax
import jax.numpy as jnp
from jax import lax
from jax.experimental import pallas as pl
from jax.experimental.pallas import tpu as pltpu
from jax.sharding import PartitionSpec as P

loss_scale = 1024.0
highest = lax.Precision.HIGHEST
contract_last = (((1,), (1,)), ((), ()))
bf16 = jnp.bfloat16
f32 = jnp.float32
i32 = jnp.int32
OWNERS = 64
CAP = 64
HOT_CAP = 192
HOT_LANES = 256
RAW_BITS = 13
PIECE_ROWS = 528
VMEM = pl.BlockSpec(memory_space=pltpu.VMEM)
SMEM = pl.BlockSpec(memory_space=pltpu.SMEM)


def params(mib):
    return pltpu.CompilerParams(vmem_limit_bytes=mib * 1024 * 1024)


def cost(flops):
    return pl.CostEstimate(flops=int(flops), bytes_accessed=4194304, transcendentals=0)


def iota(shape, dim):
    return lax.broadcasted_iota(i32, shape, dim)


def dot(left, right):
    return jnp.dot(left, right, preferred_element_type=f32)


def dot_last(left, right):
    return lax.dot_general(left, right, contract_last, preferred_element_type=f32)


def one_hot(mask):
    return jnp.where(mask, 1.0, 0.0).astype(bf16)


def bucket_kernel(ids_ref, len_ref, req_ref, hot_ref):
    slots, samples = ids_ref.shape
    owner_row = iota((OWNERS, samples), 0)
    sample1 = (iota((1, samples), 1) + 1).astype(f32)
    before = one_hot(iota((samples, samples), 0) < iota((samples, samples), 1))
    rank_row = iota((HOT_CAP, samples), 0)
    lens = len_ref[...]
    base = jnp.zeros((OWNERS, 1), f32)
    total = jnp.zeros((3 * OWNERS, HOT_CAP), f32)
    for slot in range(slots):
        ids = ids_ref[slot : slot + 1, :]
        owner = jnp.where(lens > slot, ids >> RAW_BITS, -1)
        hit = owner_row == owner
        hit_f = jnp.where(hit, 1.0, 0.0)
        seen = dot(hit_f.astype(bf16), before) + base
        base = base + jnp.sum(hit_f, axis=1, keepdims=True)
        rank = jnp.sum(hit_f * seen, axis=0, keepdims=True).astype(i32)
        raw = ids & ((1 << RAW_BITS) - 1)
        planes = jnp.concatenate(
            [
                hit_f * (raw >> 7).astype(f32),
                hit_f * (raw & 127).astype(f32),
                hit_f * sample1,
            ],
            axis=0,
        ).astype(bf16)
        total = total + dot_last(planes, one_hot(rank_row == rank))
    hot = base > float(CAP)
    high, low, samp = total[:OWNERS], total[OWNERS : 2 * OWNERS], total[2 * OWNERS :]
    cold = jnp.where(hot, 0.0, 1.0)
    warm = 1.0 - cold
    raw_all = high * 128.0 + low
    req_ref[...] = ((samp * cold)[:, :CAP].astype(i32) << 16) + (raw_all * cold)[:, :CAP].astype(
        i32
    )
    hot_samp = jnp.sum(samp * warm, axis=0, keepdims=True).astype(i32)
    hot_raw = jnp.sum(raw_all * warm, axis=0, keepdims=True).astype(i32)
    index = jnp.sum(warm * iota((OWNERS, 1), 0).astype(f32), axis=0, keepdims=True)
    pad = jnp.broadcast_to(index.astype(i32), (1, HOT_LANES - HOT_CAP))
    hot_ref[...] = jnp.concatenate([(hot_samp << 16) + hot_raw, pad], axis=1)


def map_rows(code, map_t):
    lanes = code.shape[1]
    raw = code & 0xFFFF
    spread = one_hot(iota((64, lanes), 0) == (raw >> 7))
    both = dot(map_t, spread)
    wide = both[:128] * 64.0 + both[128:]
    return jnp.sum(
        jnp.where(iota((128, lanes), 0) == (raw & 127), wide, 0.0), axis=0, keepdims=True
    )


def as_column(row):
    return jnp.broadcast_to(row, (128, row.shape[1])).T


def low_one_hot(low):
    lane = iota(low.shape, 1)
    return jnp.concatenate([one_hot(low == lane), one_hot(low == lane + 128)], axis=1)


def pick_rows(spread, high, table_pair, pairs):
    found = jnp.zeros((spread.shape[0], 128), f32)
    for pair in range(pairs):
        both = dot(spread, table_pair(pair))
        found = jnp.where(high == 2 * pair, both[:, :128], found)
        found = jnp.where(high == 2 * pair + 1, both[:, 128:], found)
    return found


def gather_kernel(req_ref, map_ref, table_ref, out_ref, spread_ref, high_ref):
    map_t = map_ref[...]
    chunks = req_ref.shape[0]

    @pl.loop(0, chunks // 4)
    def _(group):
        for part in range(4):
            chunk = group * 4 + part
            code = req_ref[pl.ds(chunk, 1), :]
            row = jnp.where(code >= 65536, map_rows(code, map_t), -1.0)
            column = as_column(row).astype(i32)
            place = pl.ds(pl.multiple_of(chunk * 128, 128), 128)
            spread_ref[place, :] = low_one_hot(column & 255)
            high_ref[place, :] = column >> 8

    block = 512

    @pl.loop(0, out_ref.shape[0] // block)
    def _(step):
        place = pl.ds(pl.multiple_of(step * block, block), block)

        def table_pair(pair):
            return jnp.concatenate(
                [
                    table_ref[pair * 512 : pair * 512 + 256, :],
                    table_ref[pair * 512 + 256 : pair * 512 + 512, :],
                ],
                axis=1,
            )

        out_ref[place, :] = pick_rows(
            spread_ref[place, :], high_ref[place, :], table_pair, 8
        ).astype(bf16)


def map_kernel(code_ref, map_ref, row_ref, samp_ref):
    map_t = map_ref[...]

    @pl.loop(0, code_ref.shape[0] // 4)
    def _(group):
        for part in range(4):
            place = pl.ds(group * 4 + part, 1)
            code = code_ref[place, :]
            row_ref[place, :] = map_rows(code, map_t).astype(i32)
            samp_ref[place, :] = (code >> 16) - 1


def pool_kernel(place_ref, req_ref, hot_ref, rows_ref, own_ref, sib_ref, len_ref, out_ref):
    samples = out_ref.shape[0]
    sample_col = iota((samples, 128), 0)
    summed = jnp.zeros((samples, 128), f32)
    for pair in range(req_ref.shape[0] // 2):
        parts = [
            one_hot(sample_col == (req_ref[2 * pair + half : 2 * pair + half + 1, :] >> 16) - 1)
            for half in range(2)
        ]
        summed = summed + dot(
            jnp.concatenate(parts, axis=1), rows_ref[pair * 256 : pair * 256 + 256, :]
        )
    across, core = place_ref[1], place_ref[2]

    def piece(index, start, size):
        half, slot = index // 4, (across - index % 4) & 3
        own = own_ref[slot, start : start + size, :].astype(f32)
        sib = sib_ref[slot, start : start + size, :].astype(f32)
        return jnp.where(core == half, own, sib)

    planes = [
        jnp.concatenate([piece(4 * plane + part, 512, 16) for part in range(4)], axis=0).T
        for plane in range(2)
    ]
    map_t = jnp.concatenate(planes, axis=0).astype(bf16)
    code = jnp.where(iota((1, HOT_LANES), 1) < HOT_CAP, hot_ref[...], 0)
    row = jnp.where(code >= 65536, map_rows(code, map_t), -1.0)
    column = as_column(row).astype(i32)

    def table_pair(pair):
        return jnp.concatenate(
            [piece(pair, 0, 256), piece(pair, 256, 256)], axis=1
        ).astype(bf16)

    hot_rows = pick_rows(low_one_hot(column & 255), column >> 8, table_pair, 8).astype(bf16)
    spread = one_hot(iota((samples, HOT_LANES), 0) == (code >> 16) - 1)
    summed = summed + dot(spread, hot_rows)
    out_ref[...] = (summed / len_ref[...].astype(f32)).astype(bf16)


def scatter_kernel(steps, place_ref, row_ref, samp_ref, *refs):
    count = len(steps)
    grads = refs[: 2 * count]
    if len(refs) == 2 * count + 3:
        out_ref, wide_ref, spread_ref = refs[2 * count :]
        out_ref[...] = jnp.zeros_like(out_ref)
    else:
        seen_ref, out_ref, wide_ref, spread_ref = refs[2 * count :]
        out_ref[...] = seen_ref[...]
    depth, across, core, chunks = place_ref[0], place_ref[1], place_ref[2], place_ref[3]
    lane = iota((1, 128), 1)
    offset = jnp.where(lane < 64, core * 256, (1 - core) * 256)
    lane_wide = iota((128, 128), 1)
    low_row = iota((256, 128), 0)
    for index, step in enumerate(steps):
        own_ref, sib_ref = grads[2 * index], grads[2 * index + 1]
        level = ((depth - step) & 7) * 4

        @pl.loop(0, chunks)
        def _(chunk):
            for shift in range(4):
                block = level + ((across - shift) & 3)
                row = row_ref[block, pl.ds(chunk, 1), :]
                samp = samp_ref[block, pl.ds(chunk, 1), :]
                samp = jnp.where(samp < 0, -1, samp + offset)
                samp_col = as_column(samp.astype(f32)).astype(i32)
                high_col = as_column((row >> 8).astype(f32)).astype(i32)
                picks = jnp.concatenate(
                    [one_hot(samp_col == lane_wide + 128 * part) for part in range(4)], axis=1
                )
                source = jnp.concatenate([own_ref[shift], sib_ref[shift]], axis=0)
                slots = dot(picks, source)
                place = slice(shift * 128, shift * 128 + 128)
                for high in range(16):
                    wide_ref[place, high * 128 : high * 128 + 128] = jnp.where(
                        high_col == high, slots, 0.0
                    ).astype(bf16)
                spread_ref[:, place] = one_hot(low_row == (row & 255))
            spread = spread_ref[...]
            for pair in range(8):
                both = dot(spread, wide_ref[:, pair * 256 : pair * 256 + 256])
                start = pair * 512
                out_ref[start : start + 256, :] += both[:, :128]
                out_ref[start + 256 : start + 512, :] += both[:, 128:]


def scatter_call(steps, place, rows, samps, grads, seen):
    operands = [place, rows, samps, *grads]
    aliases = {}
    if seen is not None:
        operands.append(seen)
        aliases = {len(operands) - 1: 0}
    return pl.pallas_call(
        functools.partial(scatter_kernel, steps),
        out_shape=jax.ShapeDtypeStruct((4096, 128), f32),
        in_specs=[SMEM] + [VMEM] * (len(operands) - 1),
        out_specs=VMEM,
        scratch_shapes=[pltpu.VMEM((512, 2048), bf16), pltpu.VMEM((256, 512), bf16)],
        input_output_aliases=aliases,
        cost_estimate=cost(4e9 * len(steps)),
        compiler_params=params(32),
    )(*operands)


def swish_slope(value):
    sigmoid_val = jax.nn.sigmoid(value)
    return sigmoid_val * (1.0 + value * (1.0 - sigmoid_val))


def ring(size, shift):
    return [(i, (i + shift) % size) for i in range(size)]


def along_task(value, shift):
    return lax.ppermute(value, "task", ring(4, shift))


def across_core(value):
    return lax.ppermute(value, "fsdp", [(0, 1), (1, 0)])


def along_x(value, shift):
    return lax.ppermute(
        value, "table", [(z * 4 + x, z * 4 + (x + shift) % 4) for z in range(8) for x in range(4)]
    )


def along_z(value, shift):
    return lax.ppermute(
        value,
        "table",
        [(z * 4 + x, (z + shift) % 8 * 4 + x) for z in range(8) for x in range(4)],
    )


def at(stack, index):
    return lax.dynamic_index_in_dim(stack, index, 0, keepdims=False)


def local(
    raw_ids,
    bag_len,
    labels,
    emb_table,
    bucket_map,
    spec_weight,
    shared_weight,
    gate_weight,
    tower_weight,
    head_vector,
):
    task = lax.axis_index("task")
    core = lax.axis_index("fsdp")
    table_index = lax.axis_index("table")
    depth, across = table_index // 4, table_index % 4
    me = table_index * 2 + core
    samples = raw_ids.shape[0]
    lookups = OWNERS * CAP

    tower_all = lax.all_gather(tower_weight[0], ("task", "fsdp"), axis=0, tiled=True)
    tower_all = tower_all.reshape(4, 4096, 256)
    spec_sib = across_core(spec_weight[0])
    shared_sib = across_core(shared_weight[0])

    def joined(own, sib):
        return jnp.concatenate(
            [jnp.where(core == 0, own, sib), jnp.where(core == 0, sib, own)], axis=0
        )

    ids_t = raw_ids[:, 0, :].T
    req, hot_row = pl.pallas_call(
        bucket_kernel,
        out_shape=(
            jax.ShapeDtypeStruct((OWNERS, CAP), i32),
            jax.ShapeDtypeStruct((1, HOT_LANES), i32),
        ),
        in_specs=[VMEM] * 2,
        out_specs=(VMEM, VMEM),
        compiler_params=params(16),
    )(ids_t, bag_len.reshape(1, samples))
    hot_index = hot_row[0, HOT_CAP]
    hot_z, hot_x, hot_c = hot_index // 8, hot_index // 2 % 4, hot_index % 2
    away_z, away_x = (depth - hot_z) % 8, (across - hot_x) % 4

    row_map = bucket_map[0].reshape(64, 128)
    planes = jnp.concatenate([row_map >> 6, row_map & 63], axis=0).astype(bf16)
    map_t = jnp.concatenate([(row_map >> 6).T, (row_map & 63).T], axis=0).astype(bf16)
    shard_rows = emb_table[0]

    pieces = jnp.concatenate(
        [shard_rows.reshape(8, 512, 128), planes.reshape(8, 16, 128)], axis=1
    ).reshape(2, 4, PIECE_ROWS, 128)
    half = jnp.where(hot_c == core, at(pieces, core), across_core(at(pieces, 1 - core)))

    req, half = lax.optimization_barrier((req, half))
    asked = lax.all_to_all(req, ("table", "fsdp"), split_axis=0, concat_axis=0, tiled=True)
    asked = asked.reshape(lookups // 128, 128)

    quarters = [at(half, across)] + [
        along_x(at(half, (across + shift) % 4), shift) for shift in (1, 2, 3)
    ]
    part = lax.select_n(away_x, *quarters)
    part, asked = lax.optimization_barrier((part, asked))
    part = lax.select_n(
        jnp.where(away_z == 1, 1, jnp.where(away_z == 7, 2, 0)),
        part,
        along_z(part, 1),
        along_z(part, 7),
    )

    fetched = pl.pallas_call(
        gather_kernel,
        out_shape=jax.ShapeDtypeStruct((lookups, 128), bf16),
        in_specs=[VMEM] * 3,
        out_specs=VMEM,
        scratch_shapes=[pltpu.VMEM((lookups, 256), bf16), pltpu.VMEM((lookups, 128), i32)],
        cost_estimate=cost(9e9),
        compiler_params=params(32),
    )(asked, map_t, shard_rows)
    fetched, part = lax.optimization_barrier((fetched, part))
    part = lax.select_n(
        jnp.where((away_z >= 2) & (away_z <= 4), 1, jnp.where((away_z == 5) | (away_z == 6), 2, 0)),
        part,
        along_z(part, 3),
        along_z(part, 5),
    )
    hot_own = jnp.stack([part] + [along_x(part, shift) for shift in (1, 2, 3)])
    hot_sib = across_core(hot_own)
    returned = lax.all_to_all(
        fetched.reshape(OWNERS, CAP, 128),
        ("table", "fsdp"),
        split_axis=0,
        concat_axis=0,
        tiled=True,
    ).reshape(lookups, 128)

    spec_full = joined(spec_weight[0], spec_sib)
    shared_full = joined(shared_weight[0], shared_sib)
    returned, spec_full, shared_full = lax.optimization_barrier(
        (returned, spec_full, shared_full)
    )
    place = jnp.stack([depth, across, core]).astype(i32)
    pooled = pl.pallas_call(
        pool_kernel,
        out_shape=jax.ShapeDtypeStruct((samples, 128), bf16),
        in_specs=[SMEM] + [VMEM] * 6,
        out_specs=VMEM,
        compiler_params=params(32),
    )(place, req.reshape(lookups // 128, 128), hot_row, returned, hot_own, hot_sib, bag_len)

    hot_wide = jnp.pad(hot_row, ((0, 15), (0, 0))).reshape(16 * HOT_LANES)
    hot_all = lax.all_gather(hot_wide, ("table", "fsdp"), axis=0, tiled=False)[:, :HOT_CAP]
    is_hot = hot_index == me
    hot_codes = hot_all.reshape(32, 2, 3, 64).transpose(0, 2, 1, 3).reshape(32, 3, 128)
    cold_codes = jnp.pad(asked[:, None, :], ((0, 0), (0, 2), (0, 0)))
    codes = jnp.where(is_hot, hot_codes, cold_codes).reshape(96, 128)
    rows, samps = pl.pallas_call(
        map_kernel,
        out_shape=(jax.ShapeDtypeStruct((96, 128), i32),) * 2,
        in_specs=[VMEM] * 2,
        out_specs=(VMEM, VMEM),
        compiler_params=params(16),
    )(codes, map_t)
    rows, samps = rows.reshape(32, 3, 128), samps.reshape(32, 3, 128)

    felt = jnp.stack([pooled] + [along_task(pooled, shift) for shift in (1, 2, 3)])
    features = jnp.concatenate([at(felt, (task - field) % 4) for field in range(4)], axis=1)
    tower_own = at(tower_all, task)
    targets = labels[:, 0].astype(f32)
    head_row = head_vector[0].astype(f32)

    spec_input = dot(features, spec_full)
    shared_input = dot(features, shared_full)
    spec_out = jax.nn.silu(spec_input).astype(bf16)
    shared_out = jax.nn.silu(shared_input).astype(bf16)
    scores = jnp.einsum("si,tig->tsg", features, gate_weight, preferred_element_type=f32)
    raised = jnp.exp(scores)
    gate_mix = raised / jnp.sum(raised, axis=-1, keepdims=True)
    mix_shared = lax.dynamic_index_in_dim(gate_mix, task + 1, 2, keepdims=True)
    mix_own = at(gate_mix, task)
    spec_proj = dot(spec_out, tower_own)
    shared_proj = jnp.einsum("sd,tdh->tsh", shared_out, tower_all, preferred_element_type=f32)
    partial = mix_shared * shared_proj
    own_partial = at(partial, task) + mix_own[:, 0:1] * spec_proj
    sent = partial.astype(bf16)
    tower_pre = own_partial
    for shift in (1, 2, 3):
        tower_pre = tower_pre + along_task(at(sent, (task + shift) % 4), shift).astype(f32)
    logit_own = jnp.sum(jax.nn.silu(tower_pre) * head_row[None, :], axis=1)
    logit_grad = loss_scale * (jax.nn.sigmoid(logit_own) - targets)
    pre_grad = (logit_grad[:, None] * head_row[None, :] * swish_slope(tower_pre)).astype(bf16)
    pre_rel = jnp.stack([pre_grad] + [along_task(pre_grad, shift) for shift in (1, 2, 3)])
    pre_all = jnp.stack([at(pre_rel, (task - other) % 4) for other in range(4)])
    pre_wide = pre_grad.astype(f32)
    balance = jnp.sum(pre_wide * tower_pre, axis=1, keepdims=True)
    shared_score = mix_shared[:, :, 0].T * jnp.sum(pre_all.astype(f32) * shared_proj, axis=2).T
    spec_score = mix_own[:, 0:1] * jnp.sum(pre_wide * spec_proj, axis=1, keepdims=True)
    spec_grad = dot_last((mix_own[:, 0:1] * pre_wide).astype(bf16), tower_own)
    weighted = (mix_shared * pre_all.astype(f32)).astype(bf16)
    shared_grad = jnp.einsum("tsh,tdh->sd", weighted, tower_all, preferred_element_type=f32)
    spec_inner = (spec_grad * swish_slope(spec_input)).astype(bf16)
    shared_inner = (shared_grad * swish_slope(shared_input)).astype(bf16)
    gate_f = gate_weight.astype(f32)
    gate_own = at(gate_f, task)
    gate_shared = lax.dynamic_index_in_dim(gate_f, task + 1, 2, keepdims=False)
    score_grad = jnp.concatenate(
        [shared_score, spec_score, -mix_own * balance], axis=1
    )
    score_weight = jnp.concatenate([gate_shared, gate_own[:, 0:1].T, gate_own.T], axis=0)
    field_parts = (
        dot_last(spec_inner, spec_full)
        + dot_last(shared_inner, shared_full)
        + jnp.dot(score_grad, score_weight, precision=highest, preferred_element_type=f32)
    )
    blocks = field_parts.reshape(samples, 4, 128)
    blocks = jnp.moveaxis(blocks, 1, 0)
    field_grad = at(blocks, task)
    sent_blocks = blocks.astype(bf16)
    for shift in (1, 2, 3):
        field_grad = field_grad + along_task(at(sent_blocks, (task + shift) % 4), shift).astype(f32)
    lookup_grad = (field_grad / bag_len.astype(f32)).astype(bf16)

    place4 = jnp.stack([depth, across, core, jnp.where(is_hot, 3, 1)]).astype(i32)
    near = jnp.stack([lookup_grad] + [along_x(lookup_grad, shift) for shift in (1, 2, 3)])
    near_sib = across_core(near)
    table_grad = None
    up, down = near, near
    steps, ready = (0,), [near, near_sib]
    for step in (1, 2, 3):
        up, down = along_z(up, 1), along_z(down, 7)
        table_grad = scatter_call(steps, place4, rows, samps, ready, table_grad)
        table_grad, up, down = lax.optimization_barrier((table_grad, up, down))
        steps, ready = (step, -step), [up, across_core(up), down, across_core(down)]
    far = [along_z(up[:2], 1), along_z(down[2:], 7)]
    table_grad = scatter_call(steps, place4, rows, samps, ready, table_grad)
    table_grad, *far = lax.optimization_barrier((table_grad, *far))
    far = jnp.concatenate(far, axis=0)
    table_grad = scatter_call((4,), place4, rows, samps, [far, across_core(far)], table_grad)
    return (logit_own[:, None], table_grad[None])


def solution(mesh):
    return jax.shard_map(
        local,
        mesh=mesh,
        in_specs=(
            P(("table", "fsdp"), "task", None),
            P(("table", "fsdp"), "task"),
            P(("table", "fsdp"), "task"),
            P("task", ("table", "fsdp"), None),
            P("task", ("table", "fsdp")),
            P("task", "fsdp", None),
            P("task", "fsdp", None),
            P(),
            P("task", "fsdp", None),
            P("task", None),
        ),
        out_specs=(P(("table", "fsdp"), "task"), P("task", ("table", "fsdp"), None)),
        check_vma=False,
    )
```

```python
import functools

import jax
import jax.numpy as jnp
from jax import lax
from jax.experimental import pallas as pl
from jax.experimental.pallas import tpu as pltpu
from jax.sharding import PartitionSpec as P

loss_scale = 1024.0
highest = lax.Precision.HIGHEST
contract_last = (((1,), (1,)), ((), ()))
bf16 = jnp.bfloat16
f32 = jnp.float32
i32 = jnp.int32
OWNERS = 64
CAP = 64
HOT_CAP = 192
HOT_LANES = 256
RAW_BITS = 13
PIECE_ROWS = 528
HIGHS = 8
LOW_ROWS = 512
LOW_BITS = 9
TILE = 512
VMEM = pl.BlockSpec(memory_space=pltpu.VMEM)
SMEM = pl.BlockSpec(memory_space=pltpu.SMEM)


def params(mib):
    return pltpu.CompilerParams(vmem_limit_bytes=mib * 1024 * 1024)


def cost(flops):
    return pl.CostEstimate(flops=int(flops), bytes_accessed=4194304, transcendentals=0)


def iota(shape, dim):
    return lax.broadcasted_iota(i32, shape, dim)


def dot(left, right):
    return jnp.dot(left, right, preferred_element_type=f32)


def dot_last(left, right):
    return lax.dot_general(left, right, contract_last, preferred_element_type=f32)


def one_hot(mask):
    return jnp.where(mask, 1.0, 0.0).astype(bf16)


def packed_hot(mask):
    return jnp.where(mask, jnp.ones((), bf16), jnp.zeros((), bf16))


def bucket_kernel(ids_ref, len_ref, req_ref, hot_ref):
    slots, samples = ids_ref.shape
    owner_row = iota((OWNERS, samples), 0)
    sample1 = (iota((1, samples), 1) + 1).astype(f32)
    before = one_hot(iota((samples, samples), 0) < iota((samples, samples), 1))
    rank_row = iota((HOT_CAP, samples), 0)
    lens = len_ref[...]
    base = jnp.zeros((OWNERS, 1), f32)
    total = jnp.zeros((3 * OWNERS, HOT_CAP), f32)
    for slot in range(slots):
        ids = ids_ref[slot : slot + 1, :]
        owner = jnp.where(lens > slot, ids >> RAW_BITS, -1)
        hit = owner_row == owner
        hit_f = jnp.where(hit, 1.0, 0.0)
        seen = dot(hit_f.astype(bf16), before) + base
        base = base + jnp.sum(hit_f, axis=1, keepdims=True)
        rank = jnp.sum(hit_f * seen, axis=0, keepdims=True).astype(i32)
        raw = ids & ((1 << RAW_BITS) - 1)
        planes = jnp.concatenate(
            [
                hit_f * (raw >> 7).astype(f32),
                hit_f * (raw & 127).astype(f32),
                hit_f * sample1,
            ],
            axis=0,
        ).astype(bf16)
        total = total + dot_last(planes, one_hot(rank_row == rank))
    hot = base > float(CAP)
    high, low, samp = total[:OWNERS], total[OWNERS : 2 * OWNERS], total[2 * OWNERS :]
    cold = jnp.where(hot, 0.0, 1.0)
    warm = 1.0 - cold
    raw_all = high * 128.0 + low
    req_ref[...] = ((samp * cold)[:, :CAP].astype(i32) << 16) + (raw_all * cold)[:, :CAP].astype(
        i32
    )
    hot_samp = jnp.sum(samp * warm, axis=0, keepdims=True).astype(i32)
    hot_raw = jnp.sum(raw_all * warm, axis=0, keepdims=True).astype(i32)
    index = jnp.sum(warm * iota((OWNERS, 1), 0).astype(f32), axis=0, keepdims=True)
    pad = jnp.broadcast_to(index.astype(i32), (1, HOT_LANES - HOT_CAP))
    hot_ref[...] = jnp.concatenate([(hot_samp << 16) + hot_raw, pad], axis=1)


def map_rows(code, map_t):
    lanes = code.shape[1]
    raw = code & 0xFFFF
    spread = one_hot(iota((64, lanes), 0) == (raw >> 7))
    both = dot(map_t, spread)
    wide = both[:128] * 64.0 + both[128:]
    return jnp.sum(
        jnp.where(iota((128, lanes), 0) == (raw & 127), wide, 0.0), axis=0, keepdims=True
    )


def as_column(row):
    return jnp.broadcast_to(row, (128, row.shape[1])).T


def low_one_hot(low):
    lane = iota(low.shape, 1)
    narrow = low.astype(f32).astype(bf16)
    return jnp.concatenate(
        [
            packed_hot(narrow == (lane + 128 * part).astype(f32).astype(bf16))
            for part in range(2)
        ],
        axis=1,
    )


def pick_rows(spread, high, table_pair, pairs):
    found = jnp.zeros((spread.shape[0], 128), f32)
    for pair in range(pairs):
        both = dot(spread, table_pair(pair))
        found = jnp.where(high == 2 * pair, both[:, :128], found)
        found = jnp.where(high == 2 * pair + 1, both[:, 128:], found)
    return found


def gather_kernel(req_ref, map_ref, table_ref, *refs):
    out_ref, spread_ref, high_ref = refs[-3:]
    map_t = map_ref[...]
    chunks = req_ref.shape[0]

    @pl.loop(0, chunks // 4)
    def _(group):
        for part in range(4):
            chunk = group * 4 + part
            code = req_ref[pl.ds(chunk, 1), :]
            row = jnp.where(code >= 65536, map_rows(code, map_t), -1.0)
            column = as_column(row).astype(i32)
            place = pl.ds(pl.multiple_of(chunk * 128, 128), 128)
            spread_ref[place, :] = low_one_hot(column & 255)
            high_ref[place, :] = column >> 8

    block = 512

    @pl.loop(0, out_ref.shape[0] // block)
    def _(step):
        place = pl.ds(pl.multiple_of(step * block, block), block)

        def table_pair(pair):
            return jnp.concatenate(
                [
                    table_ref[pair * 512 : pair * 512 + 256, :],
                    table_ref[pair * 512 + 256 : pair * 512 + 512, :],
                ],
                axis=1,
            )

        out_ref[place, :] = pick_rows(
            spread_ref[place, :], high_ref[place, :], table_pair, 8
        ).astype(bf16)


def gather_call(asked, map_t, table, half, before):
    chunks = asked.shape[0] // 2
    rows = chunks * 128
    operands = [asked, map_t, table]
    specs = [
        pl.BlockSpec((chunks, 128), lambda i: (half, 0)),
        whole_spec(*map_t.shape),
        whole_spec(*table.shape),
    ]
    aliases = {}
    if before is not None:
        operands.append(before)
        specs.append(pl.BlockSpec(memory_space=pl.ANY))
        aliases = {3: 0}
    return pl.pallas_call(
        gather_kernel,
        grid=(1,),
        out_shape=jax.ShapeDtypeStruct((2 * rows, 128), bf16),
        in_specs=specs,
        out_specs=pl.BlockSpec((rows, 128), lambda i: (half, 0)),
        scratch_shapes=[pltpu.VMEM((rows, 256), bf16), pltpu.VMEM((rows, 128), i32)],
        input_output_aliases=aliases,
        cost_estimate=cost(5e9),
        compiler_params=params(16),
    )(*operands)


def map_kernel(code_ref, map_ref, row_ref, samp_ref):
    map_t = map_ref[...]

    @pl.loop(0, code_ref.shape[0] // 8)
    def _(group):
        place = pl.ds(pl.multiple_of(group * 8, 8), 8)
        code = code_ref[place, :]
        samp_ref[place, :] = (code >> 16) - 1
        for half in range(2):
            wide = jnp.concatenate(
                [code[half * 4 + part : half * 4 + part + 1, :] for part in range(4)], axis=1
            )
            row = map_rows(wide, map_t).astype(i32)
            for part in range(4):
                row_ref[pl.ds(group * 8 + half * 4 + part, 1), :] = row[
                    :, part * 128 : part * 128 + 128
                ]


def pool_kernel(place_ref, req_ref, hot_ref, rows_ref, own_ref, sib_ref, len_ref, out_ref):
    samples = out_ref.shape[0]
    sample_col = iota((samples, 128), 0)
    summed = jnp.zeros((samples, 128), f32)
    for pair in range(req_ref.shape[0] // 2):
        parts = [
            one_hot(sample_col == (req_ref[2 * pair + half : 2 * pair + half + 1, :] >> 16) - 1)
            for half in range(2)
        ]
        summed = summed + dot(
            jnp.concatenate(parts, axis=1), rows_ref[pair * 256 : pair * 256 + 256, :]
        )
    across, core = place_ref[1], place_ref[2]

    def piece(index, start, size):
        half, slot = index // 4, (across - index % 4) & 3
        own = own_ref[slot, start : start + size, :].astype(f32)
        sib = sib_ref[slot, start : start + size, :].astype(f32)
        return jnp.where(core == half, own, sib)

    planes = [
        jnp.concatenate([piece(4 * plane + part, 512, 16) for part in range(4)], axis=0).T
        for plane in range(2)
    ]
    map_t = jnp.concatenate(planes, axis=0).astype(bf16)
    code = jnp.where(iota((1, HOT_LANES), 1) < HOT_CAP, hot_ref[...], 0)
    row = jnp.where(code >= 65536, map_rows(code, map_t), -1.0)
    column = as_column(row).astype(i32)

    def table_pair(pair):
        return jnp.concatenate(
            [piece(pair, 0, 256), piece(pair, 256, 256)], axis=1
        ).astype(bf16)

    hot_rows = pick_rows(low_one_hot(column & 255), column >> 8, table_pair, 8).astype(bf16)
    spread = one_hot(iota((samples, HOT_LANES), 0) == (code >> 16) - 1)
    summed = summed + dot(spread, hot_rows)
    out_ref[...] = (summed / len_ref[...].astype(f32)).astype(bf16)


def scatter_block(chunks, level, shifts, across, offset, row_ref, samp_ref, own_ref, sib_ref,
                  out_ref, wide_ref, spread_ref):
    lane = iota((128, 128), 1).astype(f32).astype(bf16)
    sub = iota((128, 128), 0).astype(f32).astype(bf16)
    span = 128 * chunks
    for order, shift in enumerate(shifts):
        block = level + ((across - shift) & 3)
        highs, picks = [], []
        for chunk in range(chunks):
            row = row_ref[block, chunk : chunk + 1, :]
            samp = samp_ref[block, chunk : chunk + 1, :]
            samp = as_column(jnp.where(samp < 0, -1, samp + offset).astype(f32))
            low = row & (LOW_ROWS - 1)
            start = order * span + chunk * 128
            place = slice(start, start + 128)
            highs.append(as_column((row >> LOW_BITS).astype(f32)).astype(bf16))
            picks.append(
                jnp.concatenate(
                    [packed_hot((samp - 128.0 * part).astype(bf16) == lane) for part in range(4)],
                    axis=1,
                )
            )
            for part in range(LOW_ROWS // 128):
                shifted = (low - 128 * part).astype(f32)
                shifted = jnp.broadcast_to(shifted, (128, 128)).astype(bf16)
                spread_ref[part * 128 : part * 128 + 128, place] = packed_hot(shifted == sub)
        picked = jnp.concatenate(picks, axis=0) if chunks > 1 else picks[0]
        source = jnp.concatenate([own_ref[order], sib_ref[order]], axis=0)
        slots = dot(picked, source).astype(bf16)
        for chunk in range(chunks):
            start = order * span + chunk * 128
            part = slots[chunk * 128 : chunk * 128 + 128, :]
            for high in range(HIGHS):
                wide_ref[start : start + 128, high * 128 : high * 128 + 128] = jnp.where(
                    highs[chunk] == jnp.asarray(high, bf16), part, jnp.zeros((), bf16)
                )
    used = len(shifts) * span
    for pair in range(HIGHS // 2):
        both = dot(spread_ref[:, :used], wide_ref[:used, pair * 256 : pair * 256 + 256])
        start = 2 * pair * LOW_ROWS
        out_ref[start : start + LOW_ROWS, :] += both[:, :128]
        out_ref[start + LOW_ROWS : start + 2 * LOW_ROWS, :] += both[:, 128:]


def scatter_kernel(steps, place_ref, row_ref, samp_ref, *refs):
    count = len(steps)
    grads = refs[: 2 * count]
    if len(refs) == 2 * count + 3:
        out_ref, wide_ref, spread_ref = refs[2 * count :]
        out_ref[...] = jnp.zeros_like(out_ref)
    else:
        seen_ref, out_ref, wide_ref, spread_ref = refs[2 * count :]
        out_ref[...] = seen_ref[...]
    depth, across, core, chunks = place_ref[0], place_ref[1], place_ref[2], place_ref[3]
    offset = jnp.where(iota((1, 128), 1) < 64, core * 256, (1 - core) * 256)

    def every(count_chunks):
        for index, (step, shifts) in enumerate(steps):
            level = ((depth - step) & 7) * 4
            scatter_block(
                count_chunks, level, shifts, across, offset, row_ref, samp_ref,
                grads[2 * index], grads[2 * index + 1], out_ref, wide_ref, spread_ref,
            )

    @pl.when(chunks == 1)
    def _():
        every(1)

    @pl.when(chunks != 1)
    def _():
        every(3)


def scatter_call(steps, place, rows, samps, grads, seen):
    operands = [place, rows, samps, *grads]
    aliases = {}
    if seen is not None:
        operands.append(seen)
        aliases = {len(operands) - 1: 0}
    return pl.pallas_call(
        functools.partial(scatter_kernel, steps),
        out_shape=jax.ShapeDtypeStruct((4096, 128), f32),
        in_specs=[SMEM] + [VMEM] * (len(operands) - 1),
        out_specs=VMEM,
        scratch_shapes=[
            pltpu.VMEM((1536, HIGHS * 128), bf16),
            pltpu.VMEM((LOW_ROWS, 1536), bf16),
        ],
        input_output_aliases=aliases,
        cost_estimate=cost(4e9 * len(steps)),
        compiler_params=params(24),
    )(*operands)


def forward_kernel(place_ref, felt_ref, spec_own, spec_sib, shared_own, shared_sib, tower_ref,
                   gate_ref, sent_ref, partial_ref, proj_ref, mix_ref, spec_slope, shared_slope,
                   acc_ref):
    step = pl.program_id(0)
    task, core = place_ref[0], place_ref[1]
    first = (task - 2 * core) & 3
    own = jnp.concatenate([felt_ref[first], felt_ref[(first - 1) & 3]], axis=1)
    sib = jnp.concatenate([felt_ref[(first - 2) & 3], felt_ref[(first - 3) & 3]], axis=1)

    @pl.when(step == 0)
    def _():
        acc_ref[...] = jnp.zeros_like(acc_ref)
        scores = dot(own, gate_ref[pl.ds(pl.multiple_of(core * 256, 256), 256), :]) + dot(
            sib, gate_ref[pl.ds(pl.multiple_of(256 - core * 256, 256), 256), :]
        )
        lane = iota(scores.shape, 1)
        raised = jnp.where(lane % 8 < 5, jnp.exp(scores), 0.0)
        bottom = jnp.ones_like(raised)
        for other in range(4):
            group = lane // 8 == other
            whole = jnp.sum(jnp.where(group, raised, 0.0), axis=1, keepdims=True)
            bottom = jnp.where(group, whole, bottom)
        mix_ref[...] = raised / bottom

    def activate(value, slope_ref):
        sig = 1.0 / (1.0 + jnp.exp(-value))
        slope_ref[...] = (sig * (1.0 + value * (1.0 - sig))).astype(bf16)
        return (value * sig).astype(bf16)

    spec_out = activate(dot(own, spec_own[...]) + dot(sib, spec_sib[...]), spec_slope)
    shared_out = activate(dot(own, shared_own[...]) + dot(sib, shared_sib[...]), shared_slope)
    for other in range(4):
        acc_ref[other] += dot(shared_out, tower_ref[other])
    acc_ref[4] += dot(spec_out, tower_ref[task])

    @pl.when(step == pl.num_programs(0) - 1)
    def _():
        mix = mix_ref[...]
        lane = iota(mix.shape, 1)

        def column(index):
            return jnp.sum(jnp.where(lane == index, mix, 0.0), axis=1, keepdims=True)

        proj_ref[...] = acc_ref[...]
        for shift in range(4):
            other = (task + shift) & 3
            part = column(other * 8 + 1 + task) * acc_ref[other]
            if shift == 0:
                partial_ref[...] = part + column(task * 8) * acc_ref[4]
            else:
                sent_ref[shift - 1] = part.astype(bf16)


def middle_kernel(partial_ref, one_ref, two_ref, three_ref, head_ref, label_ref, logit_ref,
                  pre_ref, balance_ref):
    value = partial_ref[...] + (
        one_ref[...].astype(f32) + two_ref[...].astype(f32) + three_ref[...].astype(f32)
    )
    head = head_ref[...].astype(f32)
    sig = 1.0 / (1.0 + jnp.exp(-value))
    logit = jnp.sum(value * sig * head, axis=1, keepdims=True)
    logit_ref[...] = logit
    grad = loss_scale * (1.0 / (1.0 + jnp.exp(-logit)) - label_ref[...].astype(f32))
    pre = (grad * head * (sig * (1.0 + value * (1.0 - sig)))).astype(bf16)
    pre_ref[...] = pre
    balance_ref[...] = jnp.sum(pre.astype(f32) * value, axis=1, keepdims=True)


def backward_kernel(place_ref, pre_own, pre_one, pre_two, pre_three, proj_ref, mix_ref,
                    balance_ref, gate_ref, spec_own, spec_sib, shared_own, shared_sib, tower_ref,
                    spec_slope, shared_slope, sent_ref, field_ref, scaled_ref, score_ref, acc_ref):
    step = pl.program_id(0)
    task, core = place_ref[0], place_ref[1]

    @pl.when(step == 0)
    def _():
        acc_ref[...] = jnp.zeros_like(acc_ref)
        mix = mix_ref[...]
        lane = iota(mix.shape, 1)

        def column(index):
            return jnp.sum(jnp.where(lane == index, mix, 0.0), axis=1, keepdims=True)

        score = jnp.where(lane // 8 == task, -mix * balance_ref[...], 0.0)
        for shift, pre_ref in enumerate((pre_own, pre_one, pre_two, pre_three)):
            other = (task - shift) & 3
            index = other * 8 + 1 + task
            scaled = column(index) * pre_ref[...].astype(f32)
            scaled_ref[shift] = scaled.astype(bf16)
            gained = jnp.sum(scaled * proj_ref[other], axis=1, keepdims=True)
            score = score + jnp.where(lane == index, gained, 0.0)
        scaled = column(task * 8) * pre_own[...].astype(f32)
        scaled_ref[4] = scaled.astype(bf16)
        gained = jnp.sum(scaled * proj_ref[4], axis=1, keepdims=True)
        score_ref[...] = score + jnp.where(lane == task * 8, gained, 0.0)

    shared_back = dot_last(scaled_ref[0], tower_ref[task])
    for shift in (1, 2, 3):
        shared_back = shared_back + dot_last(scaled_ref[shift], tower_ref[(task - shift) & 3])
    spec_back = dot_last(scaled_ref[4], tower_ref[task])
    spec_inner = (spec_back * spec_slope[...].astype(f32)).astype(bf16)
    shared_inner = (shared_back * shared_slope[...].astype(f32)).astype(bf16)
    acc_ref[0] += dot_last(spec_inner, spec_own[...]) + dot_last(shared_inner, shared_own[...])
    acc_ref[1] += dot_last(spec_inner, spec_sib[...]) + dot_last(shared_inner, shared_sib[...])

    @pl.when(step == pl.num_programs(0) - 1)
    def _():
        score = score_ref[...]
        parts = []
        for _ in range(3):
            parts.append(score.astype(bf16))
            score = score - parts[-1].astype(f32)
        for rel in range(2):
            half = core if rel == 0 else 1 - core
            gate = gate_ref[pl.ds(pl.multiple_of(half * 256, 256), 256), :]
            total = acc_ref[rel] + dot_last(parts[2], gate)
            total = total + dot_last(parts[1], gate) + dot_last(parts[0], gate)
            for side in range(2):
                block = total[:, side * 128 : side * 128 + 128]
                slot = (2 * half + side - task) & 3
                sent_ref[slot] = block.astype(bf16)

                @pl.when(slot == 0)
                def _():
                    field_ref[...] = block


def dense_specs(tile):
    weight = pl.BlockSpec((256, tile), lambda i: (0, i))
    tower = pl.BlockSpec((4, tile, 256), lambda i: (0, i, 0))
    return weight, tower


def whole_spec(*shape):
    return pl.BlockSpec(shape, lambda i: (0,) * len(shape))


def ring(size, shift):
    return [(i, (i + shift) % size) for i in range(size)]


def along_task(value, shift):
    return lax.ppermute(value, "task", ring(4, shift))


def across_core(value):
    return lax.ppermute(value, "fsdp", [(0, 1), (1, 0)])


def along_x(value, shift):
    return lax.ppermute(
        value, "table", [(z * 4 + x, z * 4 + (x + shift) % 4) for z in range(8) for x in range(4)]
    )


def along_z(value, shift):
    return lax.ppermute(
        value,
        "table",
        [(z * 4 + x, (z + shift) % 8 * 4 + x) for z in range(8) for x in range(4)],
    )


def at(stack, index):
    return lax.dynamic_index_in_dim(stack, index, 0, keepdims=False)


def local(
    raw_ids,
    bag_len,
    labels,
    emb_table,
    bucket_map,
    spec_weight,
    shared_weight,
    gate_weight,
    tower_weight,
    head_vector,
):
    task = lax.axis_index("task")
    core = lax.axis_index("fsdp")
    table_index = lax.axis_index("table")
    depth, across = table_index // 4, table_index % 4
    me = table_index * 2 + core
    samples = raw_ids.shape[0]
    lookups = OWNERS * CAP

    tower_all = lax.all_gather(tower_weight[0], ("task", "fsdp"), axis=0, tiled=True)
    tower_all = tower_all.reshape(4, 4096, 256)
    spec_sib = across_core(spec_weight[0])
    shared_sib = across_core(shared_weight[0])

    ids_t = raw_ids[:, 0, :].T
    req, hot_row = pl.pallas_call(
        bucket_kernel,
        out_shape=(
            jax.ShapeDtypeStruct((OWNERS, CAP), i32),
            jax.ShapeDtypeStruct((1, HOT_LANES), i32),
        ),
        in_specs=[VMEM] * 2,
        out_specs=(VMEM, VMEM),
        compiler_params=params(16),
    )(ids_t, bag_len.reshape(1, samples))
    hot_index = hot_row[0, HOT_CAP]
    hot_z, hot_x, hot_c = hot_index // 8, hot_index // 2 % 4, hot_index % 2
    away_z, away_x = (depth - hot_z) % 8, (across - hot_x) % 4

    row_map = bucket_map[0].reshape(64, 128)
    planes = jnp.concatenate([row_map >> 6, row_map & 63], axis=0).astype(bf16)
    map_t = jnp.concatenate([(row_map >> 6).T, (row_map & 63).T], axis=0).astype(bf16)
    shard_rows = emb_table[0]

    pieces = jnp.concatenate(
        [shard_rows.reshape(8, 512, 128), planes.reshape(8, 16, 128)], axis=1
    ).reshape(2, 4, PIECE_ROWS, 128)
    half = jnp.where(hot_c == core, at(pieces, core), across_core(at(pieces, 1 - core)))

    asked = lax.all_to_all(req, ("table", "fsdp"), split_axis=0, concat_axis=0, tiled=True)
    asked = asked.reshape(lookups // 128, 128)

    quarters = [at(half, across)] + [
        along_x(at(half, (across + shift) % 4), shift) for shift in (1, 2, 3)
    ]
    part = lax.select_n(away_x, *quarters)
    part, asked = lax.optimization_barrier((part, asked))
    part = lax.select_n(
        jnp.where(away_z == 1, 1, jnp.where(away_z == 7, 2, 0)),
        part,
        along_z(part, 1),
        along_z(part, 7),
    )

    fetched = gather_call(asked, map_t, shard_rows, 0, None)
    fetched, part = lax.optimization_barrier((fetched, part))
    part = lax.select_n(
        jnp.where((away_z >= 2) & (away_z <= 4), 1, jnp.where((away_z == 5) | (away_z == 6), 2, 0)),
        part,
        along_z(part, 3),
        along_z(part, 5),
    )
    fetched = gather_call(asked, map_t, shard_rows, 1, fetched)
    fetched, part = lax.optimization_barrier((fetched, part))
    hot_own = jnp.stack([part] + [along_x(part, shift) for shift in (1, 2, 3)])
    returned = lax.all_to_all(
        fetched.reshape(OWNERS, CAP, 128),
        ("table", "fsdp"),
        split_axis=0,
        concat_axis=0,
        tiled=True,
    )
    returned, hot_own = lax.optimization_barrier((returned, hot_own))
    returned = returned.reshape(lookups, 128)
    hot_sib = across_core(hot_own)

    place = jnp.stack([depth, across, core]).astype(i32)
    pooled = pl.pallas_call(
        pool_kernel,
        out_shape=jax.ShapeDtypeStruct((samples, 128), bf16),
        in_specs=[SMEM] + [VMEM] * 6,
        out_specs=VMEM,
        compiler_params=params(32),
    )(place, req.reshape(lookups // 128, 128), hot_row, returned, hot_own, hot_sib, bag_len)

    hot_wide = jnp.pad(hot_row, ((0, 15), (0, 0))).reshape(16 * HOT_LANES)
    hot_all = lax.all_gather(hot_wide, ("table", "fsdp"), axis=0, tiled=False)[:, :HOT_CAP]
    is_hot = hot_index == me
    hot_codes = hot_all.reshape(32, 2, 3, 64).transpose(0, 2, 1, 3).reshape(32, 3, 128)
    cold_codes = jnp.pad(asked[:, None, :], ((0, 0), (0, 2), (0, 0)))
    codes = jnp.where(is_hot, hot_codes, cold_codes).reshape(96, 128)
    rows, samps = pl.pallas_call(
        map_kernel,
        out_shape=(jax.ShapeDtypeStruct((96, 128), i32),) * 2,
        in_specs=[VMEM] * 2,
        out_specs=(VMEM, VMEM),
        compiler_params=params(16),
    )(codes, map_t)
    rows, samps = rows.reshape(32, 3, 128), samps.reshape(32, 3, 128)

    felt = jnp.stack([pooled] + [along_task(pooled, shift) for shift in (1, 2, 3)])
    gate_cat = jnp.pad(gate_weight, ((0, 0), (0, 0), (0, 3))).transpose(1, 0, 2)
    gate_cat = jnp.pad(gate_cat.reshape(512, 32), ((0, 0), (0, 96)))
    dense_place = jnp.stack([task, core]).astype(i32)
    weight, tower = dense_specs(TILE)
    wide = spec_weight.shape[2]
    grid = (wide // TILE,)
    sent, partial, proj, mix, spec_slope, shared_slope = pl.pallas_call(
        forward_kernel,
        grid=grid,
        out_shape=(
            jax.ShapeDtypeStruct((3, samples, 256), bf16),
            jax.ShapeDtypeStruct((samples, 256), f32),
            jax.ShapeDtypeStruct((5, samples, 256), f32),
            jax.ShapeDtypeStruct((samples, 128), f32),
            jax.ShapeDtypeStruct((samples, wide), bf16),
            jax.ShapeDtypeStruct((samples, wide), bf16),
        ),
        in_specs=[SMEM, whole_spec(4, samples, 128)]
        + [weight] * 4
        + [tower, whole_spec(512, 128)],
        out_specs=(
            whole_spec(3, samples, 256),
            whole_spec(samples, 256),
            whole_spec(5, samples, 256),
            whole_spec(samples, 128),
            weight,
            weight,
        ),
        scratch_shapes=[pltpu.VMEM((5, samples, 256), f32)],
        compiler_params=params(32),
    )(dense_place, felt, spec_weight[0], spec_sib, shared_weight[0], shared_sib, tower_all,
      gate_cat)
    received = [along_task(sent[shift - 1], shift) for shift in (1, 2, 3)]
    logit_own, pre_grad, balance = pl.pallas_call(
        middle_kernel,
        out_shape=(
            jax.ShapeDtypeStruct((samples, 1), f32),
            jax.ShapeDtypeStruct((samples, 256), bf16),
            jax.ShapeDtypeStruct((samples, 1), f32),
        ),
        in_specs=[VMEM] * 6,
        out_specs=(VMEM,) * 3,
        compiler_params=params(16),
    )(partial, *received, head_vector, labels)
    others = [along_task(pre_grad, shift) for shift in (1, 2, 3)]
    sent_blocks, field_grad = pl.pallas_call(
        backward_kernel,
        grid=grid,
        out_shape=(
            jax.ShapeDtypeStruct((4, samples, 128), bf16),
            jax.ShapeDtypeStruct((samples, 128), f32),
        ),
        in_specs=[SMEM]
        + [whole_spec(samples, 256)] * 4
        + [
            whole_spec(5, samples, 256),
            whole_spec(samples, 128),
            whole_spec(samples, 1),
            whole_spec(512, 128),
        ]
        + [weight] * 4
        + [tower, weight, weight],
        out_specs=(whole_spec(4, samples, 128), whole_spec(samples, 128)),
        scratch_shapes=[
            pltpu.VMEM((5, samples, 256), bf16),
            pltpu.VMEM((samples, 128), f32),
            pltpu.VMEM((2, samples, 256), f32),
        ],
        compiler_params=params(32),
    )(dense_place, pre_grad, *others, proj, mix, balance, gate_cat, spec_weight[0], spec_sib,
      shared_weight[0], shared_sib, tower_all, spec_slope, shared_slope)
    blocks = [along_task(sent_blocks[shift], shift).astype(f32) for shift in (1, 2, 3)]
    field_grad = field_grad + (blocks[0] + blocks[1] + blocks[2])
    lookup_grad = (field_grad / bag_len.astype(f32)).astype(bf16)
    lookup_grad, rows, samps = lax.optimization_barrier((lookup_grad, rows, samps))

    place4 = jnp.stack([depth, across, core, jnp.where(is_hot, 3, 1)]).astype(i32)
    near = jnp.stack([lookup_grad] + [along_x(lookup_grad, shift) for shift in (1, 2, 3)])
    near_sib = across_core(near)
    table_grad = None
    up, down = near, near
    every = (0, 1, 2, 3)
    steps, ready = ((0, every),), [near, near_sib]
    for step in (1, 2, 3):
        up, down = along_z(up, 1), along_z(down, 7)
        table_grad = scatter_call(steps, place4, rows, samps, ready, table_grad)
        table_grad, up, down = lax.optimization_barrier((table_grad, up, down))
        steps = ((step, every), (-step, every))
        ready = [up, across_core(up), down, across_core(down)]
    far = [along_z(up[:2], 1), along_z(down[2:], 7)]
    table_grad = scatter_call(steps, place4, rows, samps, ready, table_grad)
    table_grad, *far = lax.optimization_barrier((table_grad, *far))
    table_grad = scatter_call(
        ((4, (0, 1)), (4, (2, 3))),
        place4,
        rows,
        samps,
        [far[0], across_core(far[0]), far[1], across_core(far[1])],
        table_grad,
    )
    return (logit_own, table_grad[None])


def solution(mesh):
    return jax.shard_map(
        local,
        mesh=mesh,
        in_specs=(
            P(("table", "fsdp"), "task", None),
            P(("table", "fsdp"), "task"),
            P(("table", "fsdp"), "task"),
            P("task", ("table", "fsdp"), None),
            P("task", ("table", "fsdp")),
            P("task", "fsdp", None),
            P("task", "fsdp", None),
            P(),
            P("task", "fsdp", None),
            P("task", None),
        ),
        out_specs=(P(("table", "fsdp"), "task"), P("task", ("table", "fsdp"), None)),
        check_vma=False,
    )
```

```python
import functools

import jax
import jax.numpy as jnp
from jax import lax
from jax.experimental import pallas as pl
from jax.experimental.pallas import tpu as pltpu
from jax.sharding import PartitionSpec as P

loss_scale = 1024.0
highest = lax.Precision.HIGHEST
contract_last = (((1,), (1,)), ((), ()))
bf16 = jnp.bfloat16
f32 = jnp.float32
i32 = jnp.int32
OWNERS = 64
CAP = 64
HOT_CAP = 192
HOT_LANES = 256
RAW_BITS = 13
PIECE_ROWS = 528
HIGHS = 8
LOW_ROWS = 512
LOW_BITS = 9
TILE = 512
VMEM = pl.BlockSpec(memory_space=pltpu.VMEM)
SMEM = pl.BlockSpec(memory_space=pltpu.SMEM)


def params(mib):
    return pltpu.CompilerParams(vmem_limit_bytes=mib * 1024 * 1024)


def sigmoid(value):
    return 0.5 * jnp.tanh(0.5 * value) + 0.5


def cost(flops):
    return pl.CostEstimate(flops=int(flops), bytes_accessed=4194304, transcendentals=0)


def iota(shape, dim):
    return lax.broadcasted_iota(i32, shape, dim)


def dot(left, right):
    return jnp.dot(left, right, preferred_element_type=f32)


def dot_last(left, right):
    return lax.dot_general(left, right, contract_last, preferred_element_type=f32)


def one_hot(mask):
    return jnp.where(mask, 1.0, 0.0).astype(bf16)


def packed_hot(mask):
    return jnp.where(mask, jnp.ones((), bf16), jnp.zeros((), bf16))


def bucket_kernel(ids_ref, len_ref, req_ref, hot_ref):
    slots, samples = ids_ref.shape
    owner_row = iota((OWNERS, samples), 0)
    sample1 = (iota((1, samples), 1) + 1).astype(f32)
    before = one_hot(iota((samples, samples), 0) < iota((samples, samples), 1))
    rank_row = iota((HOT_CAP, samples), 0)
    lens = len_ref[...]
    base = jnp.zeros((OWNERS, 1), f32)
    total = jnp.zeros((3 * OWNERS, HOT_CAP), f32)
    for slot in range(slots):
        ids = ids_ref[slot : slot + 1, :]
        owner = jnp.where(lens > slot, ids >> RAW_BITS, -1)
        hit = owner_row == owner
        hit_f = jnp.where(hit, 1.0, 0.0)
        seen = dot(hit_f.astype(bf16), before) + base
        base = base + jnp.sum(hit_f, axis=1, keepdims=True)
        rank = jnp.sum(hit_f * seen, axis=0, keepdims=True).astype(i32)
        raw = ids & ((1 << RAW_BITS) - 1)
        planes = jnp.concatenate(
            [
                hit_f * (raw >> 7).astype(f32),
                hit_f * (raw & 127).astype(f32),
                hit_f * sample1,
            ],
            axis=0,
        ).astype(bf16)
        total = total + dot_last(planes, one_hot(rank_row == rank))
    hot = base > float(CAP)
    high, low, samp = total[:OWNERS], total[OWNERS : 2 * OWNERS], total[2 * OWNERS :]
    cold = jnp.where(hot, 0.0, 1.0)
    warm = 1.0 - cold
    raw_all = high * 128.0 + low
    req_ref[...] = ((samp * cold)[:, :CAP].astype(i32) << 16) + (raw_all * cold)[:, :CAP].astype(
        i32
    )
    hot_samp = jnp.sum(samp * warm, axis=0, keepdims=True).astype(i32)
    hot_raw = jnp.sum(raw_all * warm, axis=0, keepdims=True).astype(i32)
    index = jnp.sum(warm * iota((OWNERS, 1), 0).astype(f32), axis=0, keepdims=True)
    pad = jnp.broadcast_to(index.astype(i32), (1, HOT_LANES - HOT_CAP))
    hot_ref[...] = jnp.concatenate([(hot_samp << 16) + hot_raw, pad], axis=1)


def map_rows(code, map_t):
    lanes = code.shape[1]
    raw = code & 0xFFFF
    spread = one_hot(iota((64, lanes), 0) == (raw >> 7))
    both = dot(map_t, spread)
    wide = both[:128] * 64.0 + both[128:]
    return jnp.sum(
        jnp.where(iota((128, lanes), 0) == (raw & 127), wide, 0.0), axis=0, keepdims=True
    )


def as_column(row):
    return jnp.broadcast_to(row, (128, row.shape[1])).T


def low_one_hot(low):
    lane = iota(low.shape, 1)
    narrow = low.astype(f32).astype(bf16)
    return jnp.concatenate(
        [
            packed_hot(narrow == (lane + 128 * part).astype(f32).astype(bf16))
            for part in range(2)
        ],
        axis=1,
    )


def pick_rows(spread, high, table_pair, pairs):
    found = jnp.zeros((spread.shape[0], 128), f32)
    for pair in range(pairs):
        both = dot(spread, table_pair(pair))
        found = jnp.where(high == 2 * pair, both[:, :128], found)
        found = jnp.where(high == 2 * pair + 1, both[:, 128:], found)
    return found


def gather_kernel(req_ref, map_ref, table_ref, *refs):
    out_ref, spread_ref, high_ref = refs[-3:]
    map_t = map_ref[...]
    chunks = req_ref.shape[0]

    @pl.loop(0, chunks // 4)
    def _(group):
        for part in range(4):
            chunk = group * 4 + part
            code = req_ref[pl.ds(chunk, 1), :]
            row = jnp.where(code >= 65536, map_rows(code, map_t), -1.0)
            column = as_column(row).astype(i32)
            place = pl.ds(pl.multiple_of(chunk * 128, 128), 128)
            spread_ref[place, :] = low_one_hot(column & 255)
            high_ref[place, :] = column >> 8

    block = 512

    @pl.loop(0, out_ref.shape[0] // block)
    def _(step):
        place = pl.ds(pl.multiple_of(step * block, block), block)

        def table_pair(pair):
            return jnp.concatenate(
                [
                    table_ref[pair * 512 : pair * 512 + 256, :],
                    table_ref[pair * 512 + 256 : pair * 512 + 512, :],
                ],
                axis=1,
            )

        out_ref[place, :] = pick_rows(
            spread_ref[place, :], high_ref[place, :], table_pair, 8
        ).astype(bf16)


def gather_call(asked, map_t, table, half, before):
    chunks = asked.shape[0] // 2
    rows = chunks * 128
    operands = [asked, map_t, table]
    specs = [
        pl.BlockSpec((chunks, 128), lambda i: (half, 0)),
        whole_spec(*map_t.shape),
        whole_spec(*table.shape),
    ]
    aliases = {}
    if before is not None:
        operands.append(before)
        specs.append(pl.BlockSpec(memory_space=pl.ANY))
        aliases = {3: 0}
    return pl.pallas_call(
        gather_kernel,
        grid=(1,),
        out_shape=jax.ShapeDtypeStruct((2 * rows, 128), bf16),
        in_specs=specs,
        out_specs=pl.BlockSpec((rows, 128), lambda i: (half, 0)),
        scratch_shapes=[pltpu.VMEM((rows, 256), bf16), pltpu.VMEM((rows, 128), i32)],
        input_output_aliases=aliases,
        cost_estimate=cost(5e9),
        compiler_params=params(16),
    )(*operands)


def map_kernel(code_ref, map_ref, row_ref, samp_ref):
    map_t = map_ref[...]

    @pl.loop(0, code_ref.shape[0] // 8)
    def _(group):
        place = pl.ds(pl.multiple_of(group * 8, 8), 8)
        code = code_ref[place, :]
        samp_ref[place, :] = (code >> 16) - 1
        for half in range(2):
            wide = jnp.concatenate(
                [code[half * 4 + part : half * 4 + part + 1, :] for part in range(4)], axis=1
            )
            row = map_rows(wide, map_t).astype(i32)
            for part in range(4):
                row_ref[pl.ds(group * 8 + half * 4 + part, 1), :] = row[
                    :, part * 128 : part * 128 + 128
                ]


def pool_kernel(place_ref, req_ref, hot_ref, rows_ref, own_ref, sib_ref, len_ref, out_ref):
    samples = out_ref.shape[0]
    sample_col = iota((samples, 128), 0)
    summed = jnp.zeros((samples, 128), f32)
    for pair in range(req_ref.shape[0] // 2):
        parts = [
            one_hot(sample_col == (req_ref[2 * pair + half : 2 * pair + half + 1, :] >> 16) - 1)
            for half in range(2)
        ]
        summed = summed + dot(
            jnp.concatenate(parts, axis=1), rows_ref[pair * 256 : pair * 256 + 256, :]
        )
    across, core = place_ref[1], place_ref[2]

    def piece(index, start, size):
        half, slot = index // 4, (across - index % 4) & 3
        own = own_ref[slot, start : start + size, :].astype(f32)
        sib = sib_ref[slot, start : start + size, :].astype(f32)
        return jnp.where(core == half, own, sib)

    planes = [
        jnp.concatenate([piece(4 * plane + part, 512, 16) for part in range(4)], axis=0).T
        for plane in range(2)
    ]
    map_t = jnp.concatenate(planes, axis=0).astype(bf16)
    code = jnp.where(iota((1, HOT_LANES), 1) < HOT_CAP, hot_ref[...], 0)
    row = jnp.where(code >= 65536, map_rows(code, map_t), -1.0)
    column = as_column(row).astype(i32)

    def table_pair(pair):
        return jnp.concatenate(
            [piece(pair, 0, 256), piece(pair, 256, 256)], axis=1
        ).astype(bf16)

    hot_rows = pick_rows(low_one_hot(column & 255), column >> 8, table_pair, 8).astype(bf16)
    spread = one_hot(iota((samples, HOT_LANES), 0) == (code >> 16) - 1)
    summed = summed + dot(spread, hot_rows)
    out_ref[...] = (summed / len_ref[...].astype(f32)).astype(bf16)


def scatter_block(chunks, level, shifts, across, offset, row_ref, samp_ref, own_ref, sib_ref,
                  out_ref, wide_ref, spread_ref):
    lane = iota((128, 128), 1).astype(f32).astype(bf16)
    sub = iota((128, 128), 0).astype(f32).astype(bf16)
    span = 128 * chunks
    for order, shift in enumerate(shifts):
        block = level + ((across - shift) & 3)
        highs, picks = [], []
        for chunk in range(chunks):
            row = row_ref[block, chunk : chunk + 1, :]
            samp = samp_ref[block, chunk : chunk + 1, :]
            samp = as_column(jnp.where(samp < 0, -1, samp + offset).astype(f32))
            low = row & (LOW_ROWS - 1)
            start = order * span + chunk * 128
            place = slice(start, start + 128)
            highs.append(as_column((row >> LOW_BITS).astype(f32)).astype(bf16))
            picks.append(
                jnp.concatenate(
                    [packed_hot((samp - 128.0 * part).astype(bf16) == lane) for part in range(4)],
                    axis=1,
                )
            )
            for part in range(LOW_ROWS // 128):
                shifted = (low - 128 * part).astype(f32)
                shifted = jnp.broadcast_to(shifted, (128, 128)).astype(bf16)
                spread_ref[part * 128 : part * 128 + 128, place] = packed_hot(shifted == sub)
        picked = jnp.concatenate(picks, axis=0) if chunks > 1 else picks[0]
        source = jnp.concatenate([own_ref[order], sib_ref[order]], axis=0)
        slots = dot(picked, source).astype(bf16)
        for chunk in range(chunks):
            start = order * span + chunk * 128
            part = slots[chunk * 128 : chunk * 128 + 128, :]
            for high in range(HIGHS):
                wide_ref[start : start + 128, high * 128 : high * 128 + 128] = jnp.where(
                    highs[chunk] == jnp.asarray(high, bf16), part, jnp.zeros((), bf16)
                )
    used = len(shifts) * span
    for pair in range(HIGHS // 2):
        both = dot(spread_ref[:, :used], wide_ref[:used, pair * 256 : pair * 256 + 256])
        start = 2 * pair * LOW_ROWS
        out_ref[start : start + LOW_ROWS, :] += both[:, :128]
        out_ref[start + LOW_ROWS : start + 2 * LOW_ROWS, :] += both[:, 128:]


def scatter_kernel(steps, place_ref, row_ref, samp_ref, *refs):
    count = len(steps)
    grads = refs[: 2 * count]
    if len(refs) == 2 * count + 3:
        out_ref, wide_ref, spread_ref = refs[2 * count :]
        out_ref[...] = jnp.zeros_like(out_ref)
    else:
        seen_ref, out_ref, wide_ref, spread_ref = refs[2 * count :]
        out_ref[...] = seen_ref[...]
    depth, across, core, chunks = place_ref[0], place_ref[1], place_ref[2], place_ref[3]
    offset = jnp.where(iota((1, 128), 1) < 64, core * 256, (1 - core) * 256)

    def every(count_chunks):
        for index, (step, shifts) in enumerate(steps):
            level = ((depth - step) & 7) * 4
            scatter_block(
                count_chunks, level, shifts, across, offset, row_ref, samp_ref,
                grads[2 * index], grads[2 * index + 1], out_ref, wide_ref, spread_ref,
            )

    @pl.when(chunks == 1)
    def _():
        every(1)

    @pl.when(chunks != 1)
    def _():
        every(3)


def scatter_call(steps, place, rows, samps, grads, seen):
    operands = [place, rows, samps, *grads]
    aliases = {}
    if seen is not None:
        operands.append(seen)
        aliases = {len(operands) - 1: 0}
    return pl.pallas_call(
        functools.partial(scatter_kernel, steps),
        out_shape=jax.ShapeDtypeStruct((4096, 128), f32),
        in_specs=[SMEM] + [VMEM] * (len(operands) - 1),
        out_specs=VMEM,
        scratch_shapes=[
            pltpu.VMEM((1536, HIGHS * 128), bf16),
            pltpu.VMEM((LOW_ROWS, 1536), bf16),
        ],
        input_output_aliases=aliases,
        cost_estimate=cost(4e9 * len(steps)),
        compiler_params=params(16),
    )(*operands)


def forward_kernel(place_ref, felt_ref, spec_own, spec_sib, shared_own, shared_sib, tower_ref,
                   gate_ref, sent_ref, partial_ref, proj_ref, mix_ref, spec_slope, shared_slope,
                   acc_ref):
    step = pl.program_id(0)
    task, core = place_ref[0], place_ref[1]
    first = (task - 2 * core) & 3
    own = jnp.concatenate([felt_ref[first], felt_ref[(first - 1) & 3]], axis=1)
    sib = jnp.concatenate([felt_ref[(first - 2) & 3], felt_ref[(first - 3) & 3]], axis=1)

    @pl.when(step == 0)
    def _():
        acc_ref[...] = jnp.zeros_like(acc_ref)
        scores = dot(own, gate_ref[pl.ds(pl.multiple_of(core * 256, 256), 256), :]) + dot(
            sib, gate_ref[pl.ds(pl.multiple_of(256 - core * 256, 256), 256), :]
        )
        lane = iota(scores.shape, 1)
        raised = jnp.where(lane % 8 < 5, jnp.exp(scores), 0.0)
        bottom = jnp.ones_like(raised)
        for other in range(4):
            group = lane // 8 == other
            whole = jnp.sum(jnp.where(group, raised, 0.0), axis=1, keepdims=True)
            bottom = jnp.where(group, whole, bottom)
        mix_ref[...] = raised / bottom

    def activate(value, slope_ref):
        sig = sigmoid(value)
        out = value * sig
        slope_ref[...] = (sig + out * (1.0 - sig)).astype(bf16)
        return out.astype(bf16)

    spec_out = activate(dot(own, spec_own[...]) + dot(sib, spec_sib[...]), spec_slope)
    shared_out = activate(dot(own, shared_own[...]) + dot(sib, shared_sib[...]), shared_slope)
    for other in range(4):
        acc_ref[other] += dot(shared_out, tower_ref[other])
    acc_ref[4] += dot(spec_out, tower_ref[task])

    @pl.when(step == pl.num_programs(0) - 1)
    def _():
        mix = mix_ref[...]
        lane = iota(mix.shape, 1)

        def column(index):
            return jnp.sum(jnp.where(lane == index, mix, 0.0), axis=1, keepdims=True)

        proj_ref[...] = acc_ref[...]
        for shift in range(4):
            other = (task + shift) & 3
            part = column(other * 8 + 1 + task) * acc_ref[other]
            if shift == 0:
                partial_ref[...] = part + column(task * 8) * acc_ref[4]
            else:
                sent_ref[shift - 1] = part.astype(bf16)


def middle_kernel(partial_ref, one_ref, two_ref, three_ref, head_ref, label_ref, logit_ref,
                  pre_ref, balance_ref):
    value = partial_ref[...] + (
        one_ref[...].astype(f32) + two_ref[...].astype(f32) + three_ref[...].astype(f32)
    )
    head = head_ref[...].astype(f32)
    sig = sigmoid(value)
    logit = jnp.sum(value * sig * head, axis=1, keepdims=True)
    logit_ref[...] = logit
    grad = loss_scale * (sigmoid(logit) - label_ref[...].astype(f32))
    pre = (grad * head * (sig * (1.0 + value * (1.0 - sig)))).astype(bf16)
    pre_ref[...] = pre
    balance_ref[...] = jnp.sum(pre.astype(f32) * value, axis=1, keepdims=True)


def backward_kernel(place_ref, pre_own, pre_one, pre_two, pre_three, proj_ref, mix_ref,
                    balance_ref, gate_ref, spec_own, spec_sib, shared_own, shared_sib, tower_ref,
                    spec_slope, shared_slope, sent_ref, field_ref, scaled_ref, score_ref, acc_ref):
    step = pl.program_id(0)
    task, core = place_ref[0], place_ref[1]

    @pl.when(step == 0)
    def _():
        acc_ref[...] = jnp.zeros_like(acc_ref)
        mix = mix_ref[...]
        lane = iota(mix.shape, 1)

        def column(index):
            return jnp.sum(jnp.where(lane == index, mix, 0.0), axis=1, keepdims=True)

        score = jnp.where(lane // 8 == task, -mix * balance_ref[...], 0.0)
        for shift, pre_ref in enumerate((pre_own, pre_one, pre_two, pre_three)):
            other = (task - shift) & 3
            index = other * 8 + 1 + task
            scaled = column(index) * pre_ref[...].astype(f32)
            scaled_ref[shift] = scaled.astype(bf16)
            gained = jnp.sum(scaled * proj_ref[other], axis=1, keepdims=True)
            score = score + jnp.where(lane == index, gained, 0.0)
        scaled = column(task * 8) * pre_own[...].astype(f32)
        scaled_ref[4] = scaled.astype(bf16)
        gained = jnp.sum(scaled * proj_ref[4], axis=1, keepdims=True)
        score_ref[...] = score + jnp.where(lane == task * 8, gained, 0.0)

    shared_back = dot_last(scaled_ref[0], tower_ref[task])
    for shift in (1, 2, 3):
        shared_back = shared_back + dot_last(scaled_ref[shift], tower_ref[(task - shift) & 3])
    spec_back = dot_last(scaled_ref[4], tower_ref[task])
    spec_inner = (spec_back * spec_slope[...].astype(f32)).astype(bf16)
    shared_inner = (shared_back * shared_slope[...].astype(f32)).astype(bf16)
    acc_ref[0] += dot_last(spec_inner, spec_own[...]) + dot_last(shared_inner, shared_own[...])
    acc_ref[1] += dot_last(spec_inner, spec_sib[...]) + dot_last(shared_inner, shared_sib[...])

    @pl.when(step == pl.num_programs(0) - 1)
    def _():
        score = score_ref[...]
        parts = []
        for _ in range(3):
            parts.append(score.astype(bf16))
            score = score - parts[-1].astype(f32)
        for rel in range(2):
            half = core if rel == 0 else 1 - core
            gate = gate_ref[pl.ds(pl.multiple_of(half * 256, 256), 256), :]
            total = acc_ref[rel] + dot_last(parts[2], gate)
            total = total + dot_last(parts[1], gate) + dot_last(parts[0], gate)
            for side in range(2):
                block = total[:, side * 128 : side * 128 + 128]
                slot = (2 * half + side - task) & 3
                sent_ref[slot] = block.astype(bf16)

                @pl.when(slot == 0)
                def _():
                    field_ref[...] = block


def dense_specs(tile):
    weight = pl.BlockSpec((256, tile), lambda i: (0, i))
    tower = pl.BlockSpec((4, tile, 256), lambda i: (0, i, 0))
    return weight, tower


def whole_spec(*shape):
    return pl.BlockSpec(shape, lambda i: (0,) * len(shape))


def ring(size, shift):
    return [(i, (i + shift) % size) for i in range(size)]


def along_task(value, shift):
    return lax.ppermute(value, "task", ring(4, shift))


def across_core(value):
    return lax.ppermute(value, "fsdp", [(0, 1), (1, 0)])


def along_x(value, shift):
    return lax.ppermute(
        value, "table", [(z * 4 + x, z * 4 + (x + shift) % 4) for z in range(8) for x in range(4)]
    )


def along_z(value, shift):
    return lax.ppermute(
        value,
        "table",
        [(z * 4 + x, (z + shift) % 8 * 4 + x) for z in range(8) for x in range(4)],
    )


def at(stack, index):
    return lax.dynamic_index_in_dim(stack, index, 0, keepdims=False)


def local(
    raw_ids,
    bag_len,
    labels,
    emb_table,
    bucket_map,
    spec_weight,
    shared_weight,
    gate_weight,
    tower_weight,
    head_vector,
):
    task = lax.axis_index("task")
    core = lax.axis_index("fsdp")
    table_index = lax.axis_index("table")
    depth, across = table_index // 4, table_index % 4
    me = table_index * 2 + core
    samples = raw_ids.shape[0]
    lookups = OWNERS * CAP

    tower_all = lax.all_gather(tower_weight[0], ("task", "fsdp"), axis=0, tiled=True)
    tower_all = tower_all.reshape(4, 4096, 256)
    spec_sib = across_core(spec_weight[0])
    shared_sib = across_core(shared_weight[0])

    ids_t = raw_ids[:, 0, :].T
    req, hot_row = pl.pallas_call(
        bucket_kernel,
        out_shape=(
            jax.ShapeDtypeStruct((OWNERS, CAP), i32),
            jax.ShapeDtypeStruct((1, HOT_LANES), i32),
        ),
        in_specs=[VMEM] * 2,
        out_specs=(VMEM, VMEM),
        compiler_params=params(16),
    )(ids_t, bag_len.reshape(1, samples))
    hot_index = hot_row[0, HOT_CAP]
    hot_z, hot_x, hot_c = hot_index // 8, hot_index // 2 % 4, hot_index % 2
    away_z, away_x = (depth - hot_z) % 8, (across - hot_x) % 4

    row_map = bucket_map[0].reshape(64, 128)
    planes = jnp.concatenate([row_map >> 6, row_map & 63], axis=0).astype(bf16)
    map_t = jnp.concatenate([(row_map >> 6).T, (row_map & 63).T], axis=0).astype(bf16)
    shard_rows = emb_table[0]

    pieces = jnp.concatenate(
        [shard_rows.reshape(8, 512, 128), planes.reshape(8, 16, 128)], axis=1
    ).reshape(2, 4, PIECE_ROWS, 128)
    half = jnp.where(hot_c == core, at(pieces, core), across_core(at(pieces, 1 - core)))

    asked = lax.all_to_all(req, ("table", "fsdp"), split_axis=0, concat_axis=0, tiled=True)
    asked = asked.reshape(lookups // 128, 128)

    quarters = [at(half, across)] + [
        along_x(at(half, (across + shift) % 4), shift) for shift in (1, 2, 3)
    ]
    part = lax.select_n(away_x, *quarters)
    part, asked = lax.optimization_barrier((part, asked))
    part = lax.select_n(
        jnp.where(away_z == 1, 1, jnp.where(away_z == 7, 2, 0)),
        part,
        along_z(part, 1),
        along_z(part, 7),
    )

    fetched = gather_call(asked, map_t, shard_rows, 0, None)
    fetched, part = lax.optimization_barrier((fetched, part))
    part = lax.select_n(
        jnp.where((away_z >= 2) & (away_z <= 4), 1, jnp.where((away_z == 5) | (away_z == 6), 2, 0)),
        part,
        along_z(part, 3),
        along_z(part, 5),
    )
    fetched = gather_call(asked, map_t, shard_rows, 1, fetched)
    fetched, part = lax.optimization_barrier((fetched, part))
    hot_own = jnp.stack([part] + [along_x(part, shift) for shift in (1, 2, 3)])
    returned = lax.all_to_all(
        fetched.reshape(OWNERS, CAP, 128),
        ("table", "fsdp"),
        split_axis=0,
        concat_axis=0,
        tiled=True,
    )
    gate_cat = jnp.pad(gate_weight, ((0, 0), (0, 0), (0, 3))).transpose(1, 0, 2)
    gate_cat = jnp.pad(gate_cat.reshape(512, 32), ((0, 0), (0, 96)))
    req_wide = req.reshape(lookups // 128, 128)
    returned, hot_own, gate_cat, req_wide = lax.optimization_barrier(
        (returned, hot_own, gate_cat, req_wide)
    )
    returned = returned.reshape(lookups, 128)
    hot_sib = across_core(hot_own)

    place = jnp.stack([depth, across, core]).astype(i32)
    pooled = pl.pallas_call(
        pool_kernel,
        out_shape=jax.ShapeDtypeStruct((samples, 128), bf16),
        in_specs=[SMEM] + [VMEM] * 6,
        out_specs=VMEM,
        compiler_params=params(16),
    )(place, req_wide, hot_row, returned, hot_own, hot_sib, bag_len)

    hot_wide = jnp.pad(hot_row, ((0, 15), (0, 0))).reshape(16 * HOT_LANES)
    hot_all = lax.all_gather(hot_wide, ("table", "fsdp"), axis=0, tiled=False)[:, :HOT_CAP]
    is_hot = hot_index == me
    hot_codes = hot_all.reshape(32, 2, 3, 64).transpose(0, 2, 1, 3).reshape(32, 3, 128)
    cold_codes = jnp.pad(asked[:, None, :], ((0, 0), (0, 2), (0, 0)))
    codes = jnp.where(is_hot, hot_codes, cold_codes).reshape(96, 128)
    rows, samps = pl.pallas_call(
        map_kernel,
        out_shape=(jax.ShapeDtypeStruct((96, 128), i32),) * 2,
        in_specs=[VMEM] * 2,
        out_specs=(VMEM, VMEM),
        compiler_params=params(16),
    )(codes, map_t)
    rows, samps = rows.reshape(32, 3, 128), samps.reshape(32, 3, 128)

    felt = jnp.stack([pooled] + [along_task(pooled, shift) for shift in (1, 2, 3)])
    dense_place = jnp.stack([task, core]).astype(i32)
    weight, tower = dense_specs(TILE)
    wide = spec_weight.shape[2]
    grid = (wide // TILE,)
    sent, partial, proj, mix, spec_slope, shared_slope = pl.pallas_call(
        forward_kernel,
        grid=grid,
        out_shape=(
            jax.ShapeDtypeStruct((3, samples, 256), bf16),
            jax.ShapeDtypeStruct((samples, 256), f32),
            jax.ShapeDtypeStruct((5, samples, 256), f32),
            jax.ShapeDtypeStruct((samples, 128), f32),
            jax.ShapeDtypeStruct((samples, wide), bf16),
            jax.ShapeDtypeStruct((samples, wide), bf16),
        ),
        in_specs=[SMEM, whole_spec(4, samples, 128)]
        + [weight] * 4
        + [tower, whole_spec(512, 128)],
        out_specs=(
            whole_spec(3, samples, 256),
            whole_spec(samples, 256),
            whole_spec(5, samples, 256),
            whole_spec(samples, 128),
            weight,
            weight,
        ),
        scratch_shapes=[pltpu.VMEM((5, samples, 256), f32)],
        compiler_params=params(16),
    )(dense_place, felt, spec_weight[0], spec_sib, shared_weight[0], shared_sib, tower_all,
      gate_cat)
    received = [along_task(sent[shift - 1], shift) for shift in (1, 2, 3)]
    logit_own, pre_grad, balance = pl.pallas_call(
        middle_kernel,
        out_shape=(
            jax.ShapeDtypeStruct((samples, 1), f32),
            jax.ShapeDtypeStruct((samples, 256), bf16),
            jax.ShapeDtypeStruct((samples, 1), f32),
        ),
        in_specs=[VMEM] * 6,
        out_specs=(VMEM,) * 3,
        compiler_params=params(16),
    )(partial, *received, head_vector, labels)
    others = [along_task(pre_grad, shift) for shift in (1, 2, 3)]
    sent_blocks, field_grad = pl.pallas_call(
        backward_kernel,
        grid=grid,
        out_shape=(
            jax.ShapeDtypeStruct((4, samples, 128), bf16),
            jax.ShapeDtypeStruct((samples, 128), f32),
        ),
        in_specs=[SMEM]
        + [whole_spec(samples, 256)] * 4
        + [
            whole_spec(5, samples, 256),
            whole_spec(samples, 128),
            whole_spec(samples, 1),
            whole_spec(512, 128),
        ]
        + [weight] * 4
        + [tower, weight, weight],
        out_specs=(whole_spec(4, samples, 128), whole_spec(samples, 128)),
        scratch_shapes=[
            pltpu.VMEM((5, samples, 256), bf16),
            pltpu.VMEM((samples, 128), f32),
            pltpu.VMEM((2, samples, 256), f32),
        ],
        compiler_params=params(16),
    )(dense_place, pre_grad, *others, proj, mix, balance, gate_cat, spec_weight[0], spec_sib,
      shared_weight[0], shared_sib, tower_all, spec_slope, shared_slope)
    blocks = [along_task(sent_blocks[shift], shift).astype(f32) for shift in (1, 2, 3)]
    field_grad = field_grad + (blocks[0] + blocks[1] + blocks[2])
    lookup_grad = (field_grad / bag_len.astype(f32)).astype(bf16)
    lookup_grad, rows, samps = lax.optimization_barrier((lookup_grad, rows, samps))

    place4 = jnp.stack([depth, across, core, jnp.where(is_hot, 3, 1)]).astype(i32)
    near = jnp.stack([lookup_grad] + [along_x(lookup_grad, shift) for shift in (1, 2, 3)])
    near_sib = across_core(near)
    table_grad = None
    up, down = near, near
    every = (0, 1, 2, 3)
    steps, ready = ((0, every),), [near, near_sib]
    for step in (1, 2, 3):
        up, down = along_z(up, 1), along_z(down, 7)
        table_grad = scatter_call(steps, place4, rows, samps, ready, table_grad)
        table_grad, up, down = lax.optimization_barrier((table_grad, up, down))
        steps = ((step, every), (-step, every))
        ready = [up, across_core(up), down, across_core(down)]
    far = [along_z(up[:2], 1), along_z(down[2:], 7)]
    table_grad = scatter_call(steps, place4, rows, samps, ready, table_grad)
    table_grad, *far = lax.optimization_barrier((table_grad, *far))
    table_grad = scatter_call(
        ((4, (0, 1)), (4, (2, 3))),
        place4,
        rows,
        samps,
        [far[0], across_core(far[0]), far[1], across_core(far[1])],
        table_grad,
    )
    return (logit_own, table_grad[None])


def solution(mesh):
    return jax.shard_map(
        local,
        mesh=mesh,
        in_specs=(
            P(("table", "fsdp"), "task", None),
            P(("table", "fsdp"), "task"),
            P(("table", "fsdp"), "task"),
            P("task", ("table", "fsdp"), None),
            P("task", ("table", "fsdp")),
            P("task", "fsdp", None),
            P("task", "fsdp", None),
            P(),
            P("task", "fsdp", None),
            P("task", None),
        ),
        out_specs=(P(("table", "fsdp"), "task"), P("task", ("table", "fsdp"), None)),
        check_vma=False,
    )
```

```python
import functools

import jax
import jax.numpy as jnp
from jax import lax
from jax.experimental import pallas as pl
from jax.experimental.pallas import tpu as pltpu
from jax.sharding import PartitionSpec as P

loss_scale = 1024.0
highest = lax.Precision.HIGHEST
contract_last = (((1,), (1,)), ((), ()))
bf16 = jnp.bfloat16
f32 = jnp.float32
i32 = jnp.int32
OWNERS = 64
CAP = 64
HOT_CAP = 192
HOT_LANES = 256
RAW_BITS = 13
PIECE_ROWS = 528
HIGHS = 8
LOW_ROWS = 512
LOW_BITS = 9
TILE = 512
VMEM = pl.BlockSpec(memory_space=pltpu.VMEM)
SMEM = pl.BlockSpec(memory_space=pltpu.SMEM)


def params(mib):
    return pltpu.CompilerParams(vmem_limit_bytes=mib * 1024 * 1024)


def sigmoid(value):
    return 0.5 * jnp.tanh(0.5 * value) + 0.5


def hbm(value):
    return pltpu.with_memory_space_constraint(value, pltpu.HBM)


def near_core(value):
    return pltpu.with_memory_space_constraint(value, pltpu.VMEM)


def cost(flops):
    return pl.CostEstimate(flops=int(flops), bytes_accessed=4194304, transcendentals=0)


def iota(shape, dim):
    return lax.broadcasted_iota(i32, shape, dim)


def dot(left, right):
    return jnp.dot(left, right, preferred_element_type=f32)


def dot_last(left, right):
    return lax.dot_general(left, right, contract_last, preferred_element_type=f32)


def one_hot(mask):
    return jnp.where(mask, 1.0, 0.0).astype(bf16)


def packed_hot(mask):
    return jnp.where(mask, jnp.ones((), bf16), jnp.zeros((), bf16))


def bucket_kernel(ids_ref, len_ref, req_ref, hot_ref):
    slots, samples = ids_ref.shape
    owner_row = iota((OWNERS, samples), 0)
    sample1 = (iota((1, samples), 1) + 1).astype(f32)
    before = one_hot(iota((samples, samples), 0) < iota((samples, samples), 1))
    rank_row = iota((HOT_CAP, samples), 0)
    lens = len_ref[...]
    base = jnp.zeros((OWNERS, 1), f32)
    total = jnp.zeros((3 * OWNERS, HOT_CAP), f32)
    for slot in range(slots):
        ids = ids_ref[slot : slot + 1, :]
        owner = jnp.where(lens > slot, ids >> RAW_BITS, -1)
        hit = owner_row == owner
        hit_f = jnp.where(hit, 1.0, 0.0)
        seen = dot(hit_f.astype(bf16), before) + base
        base = base + jnp.sum(hit_f, axis=1, keepdims=True)
        rank = jnp.sum(hit_f * seen, axis=0, keepdims=True).astype(i32)
        raw = ids & ((1 << RAW_BITS) - 1)
        planes = jnp.concatenate(
            [
                hit_f * (raw >> 7).astype(f32),
                hit_f * (raw & 127).astype(f32),
                hit_f * sample1,
            ],
            axis=0,
        ).astype(bf16)
        total = total + dot_last(planes, one_hot(rank_row == rank))
    hot = base > float(CAP)
    high, low, samp = total[:OWNERS], total[OWNERS : 2 * OWNERS], total[2 * OWNERS :]
    cold = jnp.where(hot, 0.0, 1.0)
    warm = 1.0 - cold
    raw_all = high * 128.0 + low
    req_ref[...] = ((samp * cold)[:, :CAP].astype(i32) << 16) + (raw_all * cold)[:, :CAP].astype(
        i32
    )
    hot_samp = jnp.sum(samp * warm, axis=0, keepdims=True).astype(i32)
    hot_raw = jnp.sum(raw_all * warm, axis=0, keepdims=True).astype(i32)
    index = jnp.sum(warm * iota((OWNERS, 1), 0).astype(f32), axis=0, keepdims=True)
    pad = jnp.broadcast_to(index.astype(i32), (1, HOT_LANES - HOT_CAP))
    hot_ref[...] = jnp.concatenate([(hot_samp << 16) + hot_raw, pad], axis=1)


def map_rows(code, map_t):
    lanes = code.shape[1]
    raw = code & 0xFFFF
    spread = one_hot(iota((64, lanes), 0) == (raw >> 7))
    both = dot(map_t, spread)
    wide = both[:128] * 64.0 + both[128:]
    return jnp.sum(
        jnp.where(iota((128, lanes), 0) == (raw & 127), wide, 0.0), axis=0, keepdims=True
    )


def as_column(row):
    return jnp.broadcast_to(row, (128, row.shape[1])).T


def low_one_hot(low):
    lane = iota(low.shape, 1)
    narrow = low.astype(f32).astype(bf16)
    return jnp.concatenate(
        [
            packed_hot(narrow == (lane + 128 * part).astype(f32).astype(bf16))
            for part in range(2)
        ],
        axis=1,
    )


def pick_rows(spread, high, table_pair, pairs):
    found = jnp.zeros((spread.shape[0], 128), f32)
    for pair in range(pairs):
        both = dot(spread, table_pair(pair))
        found = jnp.where(high == 2 * pair, both[:, :128], found)
        found = jnp.where(high == 2 * pair + 1, both[:, 128:], found)
    return found


def gather_kernel(req_ref, map_ref, table_ref, *refs):
    out_ref, spread_ref, high_ref = refs[-3:]
    map_t = map_ref[...]
    chunks = req_ref.shape[0]

    @pl.loop(0, chunks // 4)
    def _(group):
        for part in range(4):
            chunk = group * 4 + part
            code = req_ref[pl.ds(chunk, 1), :]
            row = jnp.where(code >= 65536, map_rows(code, map_t), -1.0)
            column = as_column(row).astype(i32)
            place = pl.ds(pl.multiple_of(chunk * 128, 128), 128)
            spread_ref[place, :] = low_one_hot(column & 255)
            high_ref[place, :] = column >> 8

    block = 512

    @pl.loop(0, out_ref.shape[0] // block)
    def _(step):
        place = pl.ds(pl.multiple_of(step * block, block), block)

        def table_pair(pair):
            return jnp.concatenate(
                [
                    table_ref[pair * 512 : pair * 512 + 256, :],
                    table_ref[pair * 512 + 256 : pair * 512 + 512, :],
                ],
                axis=1,
            )

        out_ref[place, :] = pick_rows(
            spread_ref[place, :], high_ref[place, :], table_pair, 8
        ).astype(bf16)


def gather_call(asked, map_t, table, half, before):
    chunks = asked.shape[0] // 2
    rows = chunks * 128
    operands = [asked, map_t, table]
    specs = [
        pl.BlockSpec((chunks, 128), lambda i: (half, 0)),
        whole_spec(*map_t.shape),
        whole_spec(*table.shape),
    ]
    aliases = {}
    if before is not None:
        operands.append(before)
        specs.append(pl.BlockSpec(memory_space=pl.ANY))
        aliases = {3: 0}
    return pl.pallas_call(
        gather_kernel,
        grid=(1,),
        out_shape=jax.ShapeDtypeStruct((2 * rows, 128), bf16),
        in_specs=specs,
        out_specs=pl.BlockSpec((rows, 128), lambda i: (half, 0)),
        scratch_shapes=[pltpu.VMEM((rows, 256), bf16), pltpu.VMEM((rows, 128), i32)],
        input_output_aliases=aliases,
        cost_estimate=cost(5e9),
        compiler_params=params(16),
    )(*operands)


def map_kernel(code_ref, map_ref, row_ref, samp_ref):
    map_t = map_ref[...]

    @pl.loop(0, code_ref.shape[0] // 8)
    def _(group):
        place = pl.ds(pl.multiple_of(group * 8, 8), 8)
        code = code_ref[place, :]
        samp_ref[place, :] = (code >> 16) - 1
        for half in range(2):
            wide = jnp.concatenate(
                [code[half * 4 + part : half * 4 + part + 1, :] for part in range(4)], axis=1
            )
            row = map_rows(wide, map_t).astype(i32)
            for part in range(4):
                row_ref[pl.ds(group * 8 + half * 4 + part, 1), :] = row[
                    :, part * 128 : part * 128 + 128
                ]


def pool_kernel(place_ref, req_ref, hot_ref, rows_ref, own_ref, sib_ref, len_ref, out_ref):
    samples = out_ref.shape[0]
    sample_col = iota((samples, 128), 0)
    summed = jnp.zeros((samples, 128), f32)
    for pair in range(req_ref.shape[0] // 2):
        parts = [
            one_hot(sample_col == (req_ref[2 * pair + half : 2 * pair + half + 1, :] >> 16) - 1)
            for half in range(2)
        ]
        summed = summed + dot(
            jnp.concatenate(parts, axis=1), rows_ref[pair * 256 : pair * 256 + 256, :]
        )
    across, core = place_ref[1], place_ref[2]

    def piece(index, start, size):
        half, slot = index // 4, (across - index % 4) & 3
        own = own_ref[slot, start : start + size, :].astype(f32)
        sib = sib_ref[slot, start : start + size, :].astype(f32)
        return jnp.where(core == half, own, sib)

    planes = [
        jnp.concatenate([piece(4 * plane + part, 512, 16) for part in range(4)], axis=0).T
        for plane in range(2)
    ]
    map_t = jnp.concatenate(planes, axis=0).astype(bf16)
    code = jnp.where(iota((1, HOT_LANES), 1) < HOT_CAP, hot_ref[...], 0)
    row = jnp.where(code >= 65536, map_rows(code, map_t), -1.0)
    column = as_column(row).astype(i32)

    def table_pair(pair):
        return jnp.concatenate(
            [piece(pair, 0, 256), piece(pair, 256, 256)], axis=1
        ).astype(bf16)

    hot_rows = pick_rows(low_one_hot(column & 255), column >> 8, table_pair, 8).astype(bf16)
    spread = one_hot(iota((samples, HOT_LANES), 0) == (code >> 16) - 1)
    summed = summed + dot(spread, hot_rows)
    out_ref[...] = (summed / len_ref[...].astype(f32)).astype(bf16)


def scatter_block(chunks, level, shifts, across, offset, row_ref, samp_ref, own_ref, sib_ref,
                  out_ref, wide_ref, spread_ref):
    lane = iota((128, 128), 1).astype(f32).astype(bf16)
    sub = iota((128, 128), 0).astype(f32).astype(bf16)
    span = 128 * chunks
    for order, shift in enumerate(shifts):
        block = level + ((across - shift) & 3)
        highs, picks = [], []
        for chunk in range(chunks):
            row = row_ref[block, chunk : chunk + 1, :]
            samp = samp_ref[block, chunk : chunk + 1, :]
            samp = as_column(jnp.where(samp < 0, -1, samp + offset).astype(f32))
            low = row & (LOW_ROWS - 1)
            start = order * span + chunk * 128
            place = slice(start, start + 128)
            highs.append(as_column((row >> LOW_BITS).astype(f32)).astype(bf16))
            picks.append(
                jnp.concatenate(
                    [packed_hot((samp - 128.0 * part).astype(bf16) == lane) for part in range(4)],
                    axis=1,
                )
            )
            for part in range(LOW_ROWS // 128):
                shifted = (low - 128 * part).astype(f32)
                shifted = jnp.broadcast_to(shifted, (128, 128)).astype(bf16)
                spread_ref[part * 128 : part * 128 + 128, place] = packed_hot(shifted == sub)
        picked = jnp.concatenate(picks, axis=0) if chunks > 1 else picks[0]
        source = jnp.concatenate([own_ref[order], sib_ref[order]], axis=0)
        slots = dot(picked, source).astype(bf16)
        for chunk in range(chunks):
            start = order * span + chunk * 128
            part = slots[chunk * 128 : chunk * 128 + 128, :]
            for high in range(HIGHS):
                wide_ref[start : start + 128, high * 128 : high * 128 + 128] = jnp.where(
                    highs[chunk] == jnp.asarray(high, bf16), part, jnp.zeros((), bf16)
                )
    used = len(shifts) * span
    for pair in range(HIGHS // 2):
        both = dot(spread_ref[:, :used], wide_ref[:used, pair * 256 : pair * 256 + 256])
        start = 2 * pair * LOW_ROWS
        out_ref[start : start + LOW_ROWS, :] += both[:, :128]
        out_ref[start + LOW_ROWS : start + 2 * LOW_ROWS, :] += both[:, 128:]


def scatter_kernel(steps, place_ref, row_ref, samp_ref, *refs):
    count = len(steps)
    grads = refs[: 2 * count]
    if len(refs) == 2 * count + 3:
        out_ref, wide_ref, spread_ref = refs[2 * count :]
        out_ref[...] = jnp.zeros_like(out_ref)
    else:
        seen_ref, out_ref, wide_ref, spread_ref = refs[2 * count :]
        out_ref[...] = seen_ref[...]
    depth, across, core, chunks = place_ref[0], place_ref[1], place_ref[2], place_ref[3]
    offset = jnp.where(iota((1, 128), 1) < 64, core * 256, (1 - core) * 256)

    def every(count_chunks):
        for index, (step, shifts) in enumerate(steps):
            level = ((depth - step) & 7) * 4
            scatter_block(
                count_chunks, level, shifts, across, offset, row_ref, samp_ref,
                grads[2 * index], grads[2 * index + 1], out_ref, wide_ref, spread_ref,
            )

    @pl.when(chunks == 1)
    def _():
        every(1)

    @pl.when(chunks != 1)
    def _():
        every(3)


def scatter_call(steps, place, rows, samps, grads, seen, last=False):
    operands = [place, rows, samps, *grads]
    if seen is not None:
        operands.append(near_core(seen))
    return pl.pallas_call(
        functools.partial(scatter_kernel, steps),
        out_shape=(pltpu.HBM if last else pltpu.VMEM)((4096, 128), f32),
        in_specs=[SMEM] + [VMEM] * (len(operands) - 1),
        out_specs=VMEM,
        scratch_shapes=[
            pltpu.VMEM((1536, HIGHS * 128), bf16),
            pltpu.VMEM((LOW_ROWS, 1536), bf16),
        ],
        cost_estimate=cost(4e9 * len(steps)),
        compiler_params=params(16),
    )(*operands)


def forward_kernel(place_ref, felt_ref, spec_own, spec_sib, shared_own, shared_sib, tower_ref,
                   gate_ref, sent_one, sent_two, sent_three, partial_ref, proj_ref, mix_ref, spec_slope, shared_slope,
                   acc_ref):
    step = pl.program_id(0)
    task, core = place_ref[0], place_ref[1]
    first = (task - 2 * core) & 3
    own = jnp.concatenate([felt_ref[first], felt_ref[(first - 1) & 3]], axis=1)
    sib = jnp.concatenate([felt_ref[(first - 2) & 3], felt_ref[(first - 3) & 3]], axis=1)

    @pl.when(step == 0)
    def _():
        acc_ref[...] = jnp.zeros_like(acc_ref)
        scores = dot(own, gate_ref[pl.ds(pl.multiple_of(core * 256, 256), 256), :]) + dot(
            sib, gate_ref[pl.ds(pl.multiple_of(256 - core * 256, 256), 256), :]
        )
        lane = iota(scores.shape, 1)
        raised = jnp.where(lane % 8 < 5, jnp.exp(scores), 0.0)
        bottom = jnp.ones_like(raised)
        for other in range(4):
            group = lane // 8 == other
            whole = jnp.sum(jnp.where(group, raised, 0.0), axis=1, keepdims=True)
            bottom = jnp.where(group, whole, bottom)
        mix_ref[...] = raised / bottom

    def activate(value, slope_ref):
        sig = sigmoid(value)
        out = value * sig
        slope_ref[...] = (sig + out * (1.0 - sig)).astype(bf16)
        return out.astype(bf16)

    spec_out = activate(dot(own, spec_own[...]) + dot(sib, spec_sib[...]), spec_slope)
    shared_out = activate(dot(own, shared_own[...]) + dot(sib, shared_sib[...]), shared_slope)
    for other in range(4):
        acc_ref[other] += dot(shared_out, tower_ref[other])
    acc_ref[4] += dot(spec_out, tower_ref[task])

    @pl.when(step == pl.num_programs(0) - 1)
    def _():
        mix = mix_ref[...]
        lane = iota(mix.shape, 1)

        def column(index):
            return jnp.sum(jnp.where(lane == index, mix, 0.0), axis=1, keepdims=True)

        proj_ref[...] = acc_ref[...]
        for shift in range(4):
            other = (task + shift) & 3
            part = column(other * 8 + 1 + task) * acc_ref[other]
            if shift == 0:
                partial_ref[...] = part + column(task * 8) * acc_ref[4]
            else:
                (sent_one, sent_two, sent_three)[shift - 1][...] = part.astype(bf16)


def middle_kernel(partial_ref, one_ref, two_ref, three_ref, head_ref, label_ref, logit_ref,
                  pre_ref, balance_ref):
    value = partial_ref[...] + (
        one_ref[...].astype(f32) + two_ref[...].astype(f32) + three_ref[...].astype(f32)
    )
    head = head_ref[...].astype(f32)
    sig = sigmoid(value)
    logit = jnp.sum(value * sig * head, axis=1, keepdims=True)
    logit_ref[...] = logit
    grad = loss_scale * (sigmoid(logit) - label_ref[...].astype(f32))
    pre = (grad * head * (sig * (1.0 + value * (1.0 - sig)))).astype(bf16)
    pre_ref[...] = pre
    balance_ref[...] = jnp.sum(pre.astype(f32) * value, axis=1, keepdims=True)


def backward_kernel(place_ref, pre_own, pre_one, pre_two, pre_three, proj_ref, mix_ref,
                    balance_ref, gate_ref, spec_own, spec_sib, shared_own, shared_sib, tower_ref,
                    spec_slope, shared_slope, sent_ref, field_ref, scaled_ref, score_ref, acc_ref):
    step = pl.program_id(0)
    task, core = place_ref[0], place_ref[1]

    @pl.when(step == 0)
    def _():
        acc_ref[...] = jnp.zeros_like(acc_ref)
        mix = mix_ref[...]
        lane = iota(mix.shape, 1)

        def column(index):
            return jnp.sum(jnp.where(lane == index, mix, 0.0), axis=1, keepdims=True)

        score = jnp.where(lane // 8 == task, -mix * balance_ref[...], 0.0)
        for shift, pre_ref in enumerate((pre_own, pre_one, pre_two, pre_three)):
            other = (task - shift) & 3
            index = other * 8 + 1 + task
            scaled = column(index) * pre_ref[...].astype(f32)
            scaled_ref[shift] = scaled.astype(bf16)
            gained = jnp.sum(scaled * proj_ref[other], axis=1, keepdims=True)
            score = score + jnp.where(lane == index, gained, 0.0)
        scaled = column(task * 8) * pre_own[...].astype(f32)
        scaled_ref[4] = scaled.astype(bf16)
        gained = jnp.sum(scaled * proj_ref[4], axis=1, keepdims=True)
        score_ref[...] = score + jnp.where(lane == task * 8, gained, 0.0)

    shared_back = dot_last(scaled_ref[0], tower_ref[task])
    for shift in (1, 2, 3):
        shared_back = shared_back + dot_last(scaled_ref[shift], tower_ref[(task - shift) & 3])
    spec_back = dot_last(scaled_ref[4], tower_ref[task])
    spec_inner = (spec_back * spec_slope[...].astype(f32)).astype(bf16)
    shared_inner = (shared_back * shared_slope[...].astype(f32)).astype(bf16)
    acc_ref[0] += dot_last(spec_inner, spec_own[...]) + dot_last(shared_inner, shared_own[...])
    acc_ref[1] += dot_last(spec_inner, spec_sib[...]) + dot_last(shared_inner, shared_sib[...])

    @pl.when(step == pl.num_programs(0) - 1)
    def _():
        score = score_ref[...]
        parts = []
        for _ in range(3):
            parts.append(score.astype(bf16))
            score = score - parts[-1].astype(f32)
        for rel in range(2):
            half = core if rel == 0 else 1 - core
            gate = gate_ref[pl.ds(pl.multiple_of(half * 256, 256), 256), :]
            total = acc_ref[rel] + dot_last(parts[2], gate)
            total = total + dot_last(parts[1], gate) + dot_last(parts[0], gate)
            for side in range(2):
                block = total[:, side * 128 : side * 128 + 128]
                slot = (2 * half + side - task) & 3
                sent_ref[slot] = block.astype(bf16)

                @pl.when(slot == 0)
                def _():
                    field_ref[...] = block


def dense_specs(tile):
    weight = pl.BlockSpec((256, tile), lambda i: (0, i))
    tower = pl.BlockSpec((4, tile, 256), lambda i: (0, i, 0))
    return weight, tower


def whole_spec(*shape):
    return pl.BlockSpec(shape, lambda i: (0,) * len(shape))


def ring(size, shift):
    return [(i, (i + shift) % size) for i in range(size)]


def along_task(value, shift):
    return lax.ppermute(value, "task", ring(4, shift))


def across_core(value):
    return lax.ppermute(value, "fsdp", [(0, 1), (1, 0)])


def along_x(value, shift):
    return lax.ppermute(
        value, "table", [(z * 4 + x, z * 4 + (x + shift) % 4) for z in range(8) for x in range(4)]
    )


def along_z(value, shift):
    return lax.ppermute(
        value,
        "table",
        [(z * 4 + x, (z + shift) % 8 * 4 + x) for z in range(8) for x in range(4)],
    )


def at(stack, index):
    return lax.dynamic_index_in_dim(stack, index, 0, keepdims=False)


def local(
    raw_ids,
    bag_len,
    labels,
    emb_table,
    bucket_map,
    spec_weight,
    shared_weight,
    gate_weight,
    tower_weight,
    head_vector,
):
    task = lax.axis_index("task")
    core = lax.axis_index("fsdp")
    table_index = lax.axis_index("table")
    depth, across = table_index // 4, table_index % 4
    me = table_index * 2 + core
    samples = raw_ids.shape[0]
    lookups = OWNERS * CAP

    tower_all = lax.all_gather(tower_weight[0], ("task", "fsdp"), axis=0, tiled=True)
    tower_all = tower_all.reshape(4, 4096, 256)
    spec_sib = across_core(spec_weight[0])
    shared_sib = across_core(shared_weight[0])

    ids_t = raw_ids[:, 0, :].T
    req, hot_row = pl.pallas_call(
        bucket_kernel,
        out_shape=(
            jax.ShapeDtypeStruct((OWNERS, CAP), i32),
            jax.ShapeDtypeStruct((1, HOT_LANES), i32),
        ),
        in_specs=[VMEM] * 2,
        out_specs=(VMEM, VMEM),
        compiler_params=params(16),
    )(ids_t, bag_len.reshape(1, samples))
    hot_index = hot_row[0, HOT_CAP]
    hot_z, hot_x, hot_c = hot_index // 8, hot_index // 2 % 4, hot_index % 2
    away_z, away_x = (depth - hot_z) % 8, (across - hot_x) % 4

    row_map = bucket_map[0].reshape(64, 128)
    planes = jnp.concatenate([row_map >> 6, row_map & 63], axis=0).astype(bf16)
    map_t = jnp.concatenate([(row_map >> 6).T, (row_map & 63).T], axis=0).astype(bf16)
    shard_rows = emb_table[0]

    pieces = jnp.concatenate(
        [shard_rows.reshape(8, 512, 128), planes.reshape(8, 16, 128)], axis=1
    ).reshape(2, 4, PIECE_ROWS, 128)
    half = jnp.where(hot_c == core, at(pieces, core), across_core(at(pieces, 1 - core)))

    asked = lax.all_to_all(req, ("table", "fsdp"), split_axis=0, concat_axis=0, tiled=True)
    asked = asked.reshape(lookups // 128, 128)

    quarters = [at(half, across)] + [
        along_x(at(half, (across + shift) % 4), shift) for shift in (1, 2, 3)
    ]
    part = lax.select_n(away_x, *quarters)
    part, asked = lax.optimization_barrier((part, asked))
    part = lax.select_n(
        jnp.where(away_z == 1, 1, jnp.where(away_z == 7, 2, 0)),
        part,
        along_z(part, 1),
        along_z(part, 7),
    )

    fetched = gather_call(asked, map_t, shard_rows, 0, None)
    fetched, part = lax.optimization_barrier((fetched, part))
    part = lax.select_n(
        jnp.where((away_z >= 2) & (away_z <= 4), 1, jnp.where((away_z == 5) | (away_z == 6), 2, 0)),
        part,
        along_z(part, 3),
        along_z(part, 5),
    )
    fetched = gather_call(asked, map_t, shard_rows, 1, fetched)
    fetched, part = lax.optimization_barrier((fetched, part))
    hot_own = jnp.stack([part] + [along_x(part, shift) for shift in (1, 2, 3)])
    returned = lax.all_to_all(
        fetched.reshape(OWNERS, CAP, 128),
        ("table", "fsdp"),
        split_axis=0,
        concat_axis=0,
        tiled=True,
    )
    gate_cat = jnp.pad(gate_weight, ((0, 0), (0, 0), (0, 3))).transpose(1, 0, 2)
    gate_cat = jnp.pad(gate_cat.reshape(512, 32), ((0, 0), (0, 96)))
    req_wide = req.reshape(lookups // 128, 128)
    returned, hot_own, gate_cat, req_wide = lax.optimization_barrier(
        (returned, hot_own, gate_cat, req_wide)
    )
    returned = returned.reshape(lookups, 128)
    hot_sib = across_core(hot_own)

    place = jnp.stack([depth, across, core]).astype(i32)
    pooled = pl.pallas_call(
        pool_kernel,
        out_shape=jax.ShapeDtypeStruct((samples, 128), bf16),
        in_specs=[SMEM] + [VMEM] * 6,
        out_specs=VMEM,
        compiler_params=params(16),
    )(place, req_wide, hot_row, returned, hbm(hot_own), hbm(hot_sib), bag_len)

    hot_wide = jnp.pad(hot_row, ((0, 15), (0, 0))).reshape(16 * HOT_LANES)
    hot_all = lax.all_gather(hot_wide, ("table", "fsdp"), axis=0, tiled=False)[:, :HOT_CAP]
    is_hot = hot_index == me
    hot_codes = hot_all.reshape(32, 2, 3, 64).transpose(0, 2, 1, 3).reshape(32, 3, 128)
    cold_codes = jnp.pad(asked[:, None, :], ((0, 0), (0, 2), (0, 0)))
    codes = jnp.where(is_hot, hot_codes, cold_codes).reshape(96, 128)
    rows, samps = pl.pallas_call(
        map_kernel,
        out_shape=(jax.ShapeDtypeStruct((96, 128), i32),) * 2,
        in_specs=[VMEM] * 2,
        out_specs=(VMEM, VMEM),
        compiler_params=params(16),
    )(codes, map_t)
    rows, samps = rows.reshape(32, 3, 128), samps.reshape(32, 3, 128)

    felt = jnp.stack([pooled] + [along_task(pooled, shift) for shift in (1, 2, 3)])
    dense_place = jnp.stack([task, core]).astype(i32)
    weight, tower = dense_specs(TILE)
    wide = spec_weight.shape[2]
    grid = (wide // TILE,)
    weights = [
        hbm(value)
        for value in (spec_weight[0], spec_sib, shared_weight[0], shared_sib, tower_all)
    ]
    *sent, partial, proj, mix, spec_slope, shared_slope = pl.pallas_call(
        forward_kernel,
        grid=grid,
        out_shape=(
            *[pltpu.HBM((samples, 256), bf16)] * 3,
            pltpu.HBM((samples, 256), f32),
            pltpu.HBM((5, samples, 256), f32),
            pltpu.HBM((samples, 128), f32),
            pltpu.HBM((samples, wide), bf16),
            pltpu.HBM((samples, wide), bf16),
        ),
        in_specs=[SMEM, whole_spec(4, samples, 128)]
        + [weight] * 4
        + [tower, whole_spec(512, 128)],
        out_specs=(
            *[whole_spec(samples, 256)] * 3,
            whole_spec(samples, 256),
            whole_spec(5, samples, 256),
            whole_spec(samples, 128),
            weight,
            weight,
        ),
        scratch_shapes=[pltpu.VMEM((5, samples, 256), f32)],
        compiler_params=params(16),
    )(dense_place, hbm(felt), *weights, hbm(gate_cat))
    received = [along_task(sent[shift - 1], shift) for shift in (1, 2, 3)]
    logit_own, pre_grad, balance = pl.pallas_call(
        middle_kernel,
        out_shape=(
            pltpu.HBM((samples, 1), f32),
            pltpu.HBM((samples, 256), bf16),
            pltpu.HBM((samples, 1), f32),
        ),
        in_specs=[VMEM] * 6,
        out_specs=(VMEM,) * 3,
        compiler_params=params(16),
    )(hbm(partial), *received, head_vector, labels)
    others = [along_task(pre_grad, shift) for shift in (1, 2, 3)]
    sent_blocks, field_grad = pl.pallas_call(
        backward_kernel,
        grid=grid,
        out_shape=(
            pltpu.HBM((4, samples, 128), bf16),
            pltpu.HBM((samples, 128), f32),
        ),
        in_specs=[SMEM]
        + [whole_spec(samples, 256)] * 4
        + [
            whole_spec(5, samples, 256),
            whole_spec(samples, 128),
            whole_spec(samples, 1),
            whole_spec(512, 128),
        ]
        + [weight] * 4
        + [tower, weight, weight],
        out_specs=(whole_spec(4, samples, 128), whole_spec(samples, 128)),
        scratch_shapes=[
            pltpu.VMEM((5, samples, 256), bf16),
            pltpu.VMEM((samples, 128), f32),
            pltpu.VMEM((2, samples, 256), f32),
        ],
        compiler_params=params(16),
    )(dense_place, hbm(pre_grad), *others, hbm(proj),
      hbm(mix), hbm(balance), hbm(gate_cat), *weights, hbm(spec_slope),
      hbm(shared_slope))
    blocks = [along_task(sent_blocks[shift], shift).astype(f32) for shift in (1, 2, 3)]
    field_grad = field_grad + (blocks[0] + blocks[1] + blocks[2])
    lookup_grad = (field_grad / bag_len.astype(f32)).astype(bf16)
    lookup_grad, rows, samps = lax.optimization_barrier((lookup_grad, rows, samps))

    place4 = jnp.stack([depth, across, core, jnp.where(is_hot, 3, 1)]).astype(i32)
    near = jnp.stack([lookup_grad] + [along_x(lookup_grad, shift) for shift in (1, 2, 3)])
    near_sib = across_core(near)
    table_grad = None
    up, down = near, near
    every = (0, 1, 2, 3)
    steps, ready = ((0, every),), [near, near_sib]
    for step in (1, 2, 3):
        up, down = along_z(up, 1), along_z(down, 7)
        table_grad = scatter_call(steps, place4, rows, samps, ready, table_grad)
        table_grad, up, down = lax.optimization_barrier((table_grad, up, down))
        steps = ((step, every), (-step, every))
        ready = [up, across_core(up), down, across_core(down)]
    far = [along_z(up[:2], 1), along_z(down[2:], 7)]
    table_grad = scatter_call(steps, place4, rows, samps, ready, table_grad)
    table_grad, *far = lax.optimization_barrier((table_grad, *far))
    table_grad = scatter_call(
        ((4, (0, 1)), (4, (2, 3))),
        place4,
        rows,
        samps,
        [far[0], across_core(far[0]), far[1], across_core(far[1])],
        table_grad,
        last=True,
    )
    return (logit_own, table_grad[None])


def solution(mesh):
    return jax.shard_map(
        local,
        mesh=mesh,
        in_specs=(
            P(("table", "fsdp"), "task", None),
            P(("table", "fsdp"), "task"),
            P(("table", "fsdp"), "task"),
            P("task", ("table", "fsdp"), None),
            P("task", ("table", "fsdp")),
            P("task", "fsdp", None),
            P("task", "fsdp", None),
            P(),
            P("task", "fsdp", None),
            P("task", None),
        ),
        out_specs=(P(("table", "fsdp"), "task"), P("task", ("table", "fsdp"), None)),
        check_vma=False,
    )
```

```python
import functools

import jax
import jax.numpy as jnp
from jax import lax
from jax.experimental import pallas as pl
from jax.experimental.pallas import tpu as pltpu
from jax.sharding import PartitionSpec as P

loss_scale = 1024.0
highest = lax.Precision.HIGHEST
contract_last = (((1,), (1,)), ((), ()))
bf16 = jnp.bfloat16
f32 = jnp.float32
i32 = jnp.int32
OWNERS = 64
CAP = 64
HOT_CAP = 192
HOT_LANES = 256
RAW_BITS = 13
PIECE_ROWS = 528
HIGHS = 8
LOW_ROWS = 512
LOW_BITS = 9
TILE = 512
VMEM = pl.BlockSpec(memory_space=pltpu.VMEM)
SMEM = pl.BlockSpec(memory_space=pltpu.SMEM)


def params(mib):
    return pltpu.CompilerParams(vmem_limit_bytes=mib * 1024 * 1024)


def sigmoid(value):
    return 0.5 * jnp.tanh(0.5 * value) + 0.5


def hbm(value):
    return pltpu.with_memory_space_constraint(value, pltpu.HBM)


def near_core(value):
    return pltpu.with_memory_space_constraint(value, pltpu.VMEM)


def cost(flops):
    return pl.CostEstimate(flops=int(flops), bytes_accessed=4194304, transcendentals=0)


def iota(shape, dim):
    return lax.broadcasted_iota(i32, shape, dim)


def dot(left, right):
    return jnp.dot(left, right, preferred_element_type=f32)


def dot_last(left, right):
    return lax.dot_general(left, right, contract_last, preferred_element_type=f32)


def one_hot(mask):
    return jnp.where(mask, 1.0, 0.0).astype(bf16)


def packed_hot(mask):
    return jnp.where(mask, jnp.ones((), bf16), jnp.zeros((), bf16))


def bucket_kernel(ids_ref, len_ref, req_ref, hot_ref):
    slots, samples = ids_ref.shape
    owner_row = iota((OWNERS, samples), 0)
    sample1 = (iota((1, samples), 1) + 1).astype(f32)
    before = one_hot(iota((samples, samples), 0) < iota((samples, samples), 1))
    rank_row = iota((HOT_CAP, samples), 0)
    lens = len_ref[...]
    base = jnp.zeros((OWNERS, 1), f32)
    total = jnp.zeros((3 * OWNERS, HOT_CAP), f32)
    for slot in range(slots):
        ids = ids_ref[slot : slot + 1, :]
        owner = jnp.where(lens > slot, ids >> RAW_BITS, -1)
        hit = owner_row == owner
        hit_f = jnp.where(hit, 1.0, 0.0)
        seen = dot(hit_f.astype(bf16), before) + base
        base = base + jnp.sum(hit_f, axis=1, keepdims=True)
        rank = jnp.sum(hit_f * seen, axis=0, keepdims=True).astype(i32)
        raw = ids & ((1 << RAW_BITS) - 1)
        planes = jnp.concatenate(
            [
                hit_f * (raw >> 7).astype(f32),
                hit_f * (raw & 127).astype(f32),
                hit_f * sample1,
            ],
            axis=0,
        ).astype(bf16)
        total = total + dot_last(planes, one_hot(rank_row == rank))
    hot = base > float(CAP)
    high, low, samp = total[:OWNERS], total[OWNERS : 2 * OWNERS], total[2 * OWNERS :]
    cold = jnp.where(hot, 0.0, 1.0)
    warm = 1.0 - cold
    raw_all = high * 128.0 + low
    req_ref[...] = ((samp * cold)[:, :CAP].astype(i32) << 16) + (raw_all * cold)[:, :CAP].astype(
        i32
    )
    hot_samp = jnp.sum(samp * warm, axis=0, keepdims=True).astype(i32)
    hot_raw = jnp.sum(raw_all * warm, axis=0, keepdims=True).astype(i32)
    index = jnp.sum(warm * iota((OWNERS, 1), 0).astype(f32), axis=0, keepdims=True)
    pad = jnp.broadcast_to(index.astype(i32), (1, HOT_LANES - HOT_CAP))
    hot_ref[...] = jnp.concatenate([(hot_samp << 16) + hot_raw, pad], axis=1)


def map_rows(code, map_t):
    lanes = code.shape[1]
    raw = code & 0xFFFF
    spread = one_hot(iota((64, lanes), 0) == (raw >> 7))
    both = dot(map_t, spread)
    wide = both[:128] * 64.0 + both[128:]
    return jnp.sum(
        jnp.where(iota((128, lanes), 0) == (raw & 127), wide, 0.0), axis=0, keepdims=True
    )


def as_column(row):
    return jnp.broadcast_to(row, (128, row.shape[1])).T


def low_one_hot(low):
    lane = iota(low.shape, 1)
    narrow = low.astype(f32).astype(bf16)
    return jnp.concatenate(
        [
            packed_hot(narrow == (lane + 128 * part).astype(f32).astype(bf16))
            for part in range(2)
        ],
        axis=1,
    )


def pick_rows(spread, high, table_pair, pairs):
    found = jnp.zeros((spread.shape[0], 128), f32)
    for pair in range(pairs):
        both = dot(spread, table_pair(pair))
        found = jnp.where(high == 2 * pair, both[:, :128], found)
        found = jnp.where(high == 2 * pair + 1, both[:, 128:], found)
    return found


def gather_kernel(req_ref, map_ref, table_ref, out_ref, spread_ref, high_ref):
    map_t = map_ref[...]
    chunks = req_ref.shape[0]

    @pl.loop(0, chunks // 4)
    def _(group):
        for part in range(4):
            chunk = group * 4 + part
            code = req_ref[pl.ds(chunk, 1), :]
            row = jnp.where(code >= 65536, map_rows(code, map_t), -1.0)
            column = as_column(row).astype(i32)
            place = pl.ds(pl.multiple_of(chunk * 128, 128), 128)
            spread_ref[place, :] = low_one_hot(column & 255)
            high_ref[place, :] = column >> 8

    block = 512

    @pl.loop(0, out_ref.shape[0] // block)
    def _(step):
        place = pl.ds(pl.multiple_of(step * block, block), block)

        def table_pair(pair):
            return jnp.concatenate(
                [
                    table_ref[pair * 512 : pair * 512 + 256, :],
                    table_ref[pair * 512 + 256 : pair * 512 + 512, :],
                ],
                axis=1,
            )

        out_ref[place, :] = pick_rows(
            spread_ref[place, :], high_ref[place, :], table_pair, 8
        ).astype(bf16)


def gather_call(asked, map_t, table):
    rows = asked.shape[0] * 128
    return pl.pallas_call(
        gather_kernel,
        out_shape=jax.ShapeDtypeStruct((rows, 128), bf16),
        in_specs=[VMEM] * 3,
        out_specs=VMEM,
        scratch_shapes=[pltpu.VMEM((rows, 256), bf16), pltpu.VMEM((rows, 128), i32)],
        cost_estimate=cost(9e9),
        compiler_params=params(16),
    )(asked, map_t, table)


def map_kernel(hot_ref, asked_ref, low_ref, high_ref, map_ref, row_ref, samp_ref, code_ref):
    map_t = map_ref[...]
    blocks = asked_ref.shape[0]
    is_hot = hot_ref[0] == 1
    code_ref[0:blocks, :] = asked_ref[...]

    @pl.when(is_hot)
    def _():
        for chunk in range(3):
            all_ref = low_ref if chunk < 2 else high_ref
            even = all_ref[pl.ds(0, blocks, stride=16), :]
            odd = all_ref[pl.ds(8, blocks, stride=16), :]
            lanes = slice(chunk % 2 * 64, chunk % 2 * 64 + 64)
            code_ref[chunk * blocks : (chunk + 1) * blocks, :] = jnp.concatenate(
                [even[:, lanes], odd[:, lanes]], axis=1
            )

    @pl.loop(0, jnp.where(is_hot, 3 * blocks // 8, blocks // 8))
    def _(group):
        place = pl.ds(pl.multiple_of(group * 8, 8), 8)
        code = code_ref[place, :]
        samp_ref[place, :] = (code >> 16) - 1
        for half in range(2):
            wide = jnp.concatenate(
                [code[half * 4 + part : half * 4 + part + 1, :] for part in range(4)], axis=1
            )
            row = map_rows(wide, map_t).astype(i32)
            for part in range(4):
                row_ref[pl.ds(group * 8 + half * 4 + part, 1), :] = row[
                    :, part * 128 : part * 128 + 128
                ]


def pool_kernel(place_ref, req_ref, hot_ref, rows_ref, own_ref, sib_ref, len_ref, out_ref):
    samples = out_ref.shape[0]
    sample_col = iota((samples, 128), 0)
    summed = jnp.zeros((samples, 128), f32)
    for pair in range(req_ref.shape[0] // 2):
        parts = [
            one_hot(sample_col == (req_ref[2 * pair + half : 2 * pair + half + 1, :] >> 16) - 1)
            for half in range(2)
        ]
        summed = summed + dot(
            jnp.concatenate(parts, axis=1), rows_ref[pair * 256 : pair * 256 + 256, :]
        )
    across, core = place_ref[1], place_ref[2]

    def piece(index, start, size):
        half, slot = index // 4, (across - index % 4) & 3
        own = own_ref[slot, start : start + size, :].astype(f32)
        sib = sib_ref[slot, start : start + size, :].astype(f32)
        return jnp.where(core == half, own, sib)

    planes = [
        jnp.concatenate([piece(4 * plane + part, 512, 16) for part in range(4)], axis=0).T
        for plane in range(2)
    ]
    map_t = jnp.concatenate(planes, axis=0).astype(bf16)
    code = jnp.where(iota((1, HOT_LANES), 1) < HOT_CAP, hot_ref[...], 0)
    row = jnp.where(code >= 65536, map_rows(code, map_t), -1.0)
    column = as_column(row).astype(i32)

    def table_pair(pair):
        return jnp.concatenate(
            [piece(pair, 0, 256), piece(pair, 256, 256)], axis=1
        ).astype(bf16)

    hot_rows = pick_rows(low_one_hot(column & 255), column >> 8, table_pair, 8).astype(bf16)
    spread = one_hot(iota((samples, HOT_LANES), 0) == (code >> 16) - 1)
    summed = summed + dot(spread, hot_rows)
    out_ref[...] = (summed / len_ref[...].astype(f32)).astype(bf16)


def scatter_block(chunks, level, shifts, across, offset, row_ref, samp_ref, own_ref, sib_ref,
                  out_ref, wide_ref, spread_ref):
    lane = iota((128, 128), 1).astype(f32).astype(bf16)
    sub = iota((128, 128), 0).astype(f32).astype(bf16)
    span = 128 * chunks
    for order, shift in enumerate(shifts):
        block = level + ((across - shift) & 3)
        highs, picks = [], []
        for chunk in range(chunks):
            line = pl.ds(chunk * 32 + block, 1)
            row, samp = row_ref[line, :], samp_ref[line, :]
            samp = as_column(jnp.where(samp < 0, -1, samp + offset).astype(f32))
            low = row & (LOW_ROWS - 1)
            start = order * span + chunk * 128
            place = slice(start, start + 128)
            highs.append(as_column((row >> LOW_BITS).astype(f32)).astype(bf16))
            picks.append(
                jnp.concatenate(
                    [packed_hot((samp - 128.0 * part).astype(bf16) == lane) for part in range(4)],
                    axis=1,
                )
            )
            for part in range(LOW_ROWS // 128):
                shifted = (low - 128 * part).astype(f32)
                shifted = jnp.broadcast_to(shifted, (128, 128)).astype(bf16)
                spread_ref[part * 128 : part * 128 + 128, place] = packed_hot(shifted == sub)
        picked = jnp.concatenate(picks, axis=0) if chunks > 1 else picks[0]
        source = jnp.concatenate([own_ref[order], sib_ref[order]], axis=0)
        slots = dot(picked, source).astype(bf16)
        for chunk in range(chunks):
            start = order * span + chunk * 128
            part = slots[chunk * 128 : chunk * 128 + 128, :]
            for high in range(HIGHS):
                wide_ref[start : start + 128, high * 128 : high * 128 + 128] = jnp.where(
                    highs[chunk] == jnp.asarray(high, bf16), part, jnp.zeros((), bf16)
                )
    used = len(shifts) * span
    for pair in range(HIGHS // 2):
        both = dot(spread_ref[:, :used], wide_ref[:used, pair * 256 : pair * 256 + 256])
        start = 2 * pair * LOW_ROWS
        out_ref[start : start + LOW_ROWS, :] += both[:, :128]
        out_ref[start + LOW_ROWS : start + 2 * LOW_ROWS, :] += both[:, 128:]


def scatter_kernel(steps, place_ref, row_ref, samp_ref, *refs):
    count = len(steps)
    grads = refs[: 2 * count]
    if len(refs) == 2 * count + 3:
        out_ref, wide_ref, spread_ref = refs[2 * count :]
        out_ref[...] = jnp.zeros_like(out_ref)
    else:
        seen_ref, out_ref, wide_ref, spread_ref = refs[2 * count :]
        out_ref[...] = seen_ref[...]
    depth, across, core, chunks = place_ref[0], place_ref[1], place_ref[2], place_ref[3]
    offset = jnp.where(iota((1, 128), 1) < 64, core * 256, (1 - core) * 256)

    def every(count_chunks):
        for index, (step, shifts) in enumerate(steps):
            level = ((depth - step) & 7) * 4
            scatter_block(
                count_chunks, level, shifts, across, offset, row_ref, samp_ref,
                grads[2 * index], grads[2 * index + 1], out_ref, wide_ref, spread_ref,
            )

    @pl.when(chunks == 1)
    def _():
        every(1)

    @pl.when(chunks != 1)
    def _():
        every(3)


def scatter_call(steps, place, rows, samps, grads, seen, last=False):
    operands = [place, rows, samps, *grads]
    if seen is not None:
        operands.append(near_core(seen))
    return pl.pallas_call(
        functools.partial(scatter_kernel, steps),
        out_shape=(pltpu.HBM if last else pltpu.VMEM)((4096, 128), f32),
        in_specs=[SMEM] + [VMEM] * (len(operands) - 1),
        out_specs=VMEM,
        scratch_shapes=[
            pltpu.VMEM((1536, HIGHS * 128), bf16),
            pltpu.VMEM((LOW_ROWS, 1536), bf16),
        ],
        cost_estimate=cost(4e9 * len(steps)),
        compiler_params=params(16),
    )(*operands)


def forward_kernel(place_ref, felt_ref, spec_own, spec_sib, shared_own, shared_sib, tower_ref,
                   gate_ref, sent_one, sent_two, sent_three, partial_ref, proj_ref, mix_ref, spec_slope, shared_slope,
                   acc_ref):
    step = pl.program_id(0)
    task, core = place_ref[0], place_ref[1]
    first = (task - 2 * core) & 3
    own = jnp.concatenate([felt_ref[first], felt_ref[(first - 1) & 3]], axis=1)
    sib = jnp.concatenate([felt_ref[(first - 2) & 3], felt_ref[(first - 3) & 3]], axis=1)

    @pl.when(step == 0)
    def _():
        acc_ref[...] = jnp.zeros_like(acc_ref)
        scores = dot(own, gate_ref[pl.ds(pl.multiple_of(core * 256, 256), 256), :]) + dot(
            sib, gate_ref[pl.ds(pl.multiple_of(256 - core * 256, 256), 256), :]
        )
        lane = iota(scores.shape, 1)
        raised = jnp.where(lane % 8 < 5, jnp.exp(scores), 0.0)
        bottom = jnp.ones_like(raised)
        for other in range(4):
            group = lane // 8 == other
            whole = jnp.sum(jnp.where(group, raised, 0.0), axis=1, keepdims=True)
            bottom = jnp.where(group, whole, bottom)
        mix_ref[...] = raised / bottom

    def activate(value, slope_ref):
        sig = sigmoid(value)
        out = value * sig
        slope_ref[...] = (sig + out * (1.0 - sig)).astype(bf16)
        return out.astype(bf16)

    spec_out = activate(dot(own, spec_own[...]) + dot(sib, spec_sib[...]), spec_slope)
    shared_out = activate(dot(own, shared_own[...]) + dot(sib, shared_sib[...]), shared_slope)
    for other in range(4):
        acc_ref[other] += dot(shared_out, tower_ref[other])
    acc_ref[4] += dot(spec_out, tower_ref[task])

    @pl.when(step == pl.num_programs(0) - 1)
    def _():
        mix = mix_ref[...]
        lane = iota(mix.shape, 1)

        def column(index):
            return jnp.sum(jnp.where(lane == index, mix, 0.0), axis=1, keepdims=True)

        proj_ref[...] = acc_ref[...]
        for shift in range(4):
            other = (task + shift) & 3
            part = column(other * 8 + 1 + task) * acc_ref[other]
            if shift == 0:
                partial_ref[...] = part + column(task * 8) * acc_ref[4]
            else:
                (sent_one, sent_two, sent_three)[shift - 1][...] = part.astype(bf16)


def middle_kernel(partial_ref, one_ref, two_ref, three_ref, head_ref, label_ref, logit_ref,
                  pre_ref, balance_ref):
    value = partial_ref[...] + (
        one_ref[...].astype(f32) + two_ref[...].astype(f32) + three_ref[...].astype(f32)
    )
    head = head_ref[...].astype(f32)
    sig = sigmoid(value)
    logit = jnp.sum(value * sig * head, axis=1, keepdims=True)
    logit_ref[...] = logit
    grad = loss_scale * (sigmoid(logit) - label_ref[...].astype(f32))
    pre = (grad * head * (sig * (1.0 + value * (1.0 - sig)))).astype(bf16)
    pre_ref[...] = pre
    balance_ref[...] = jnp.sum(pre.astype(f32) * value, axis=1, keepdims=True)


def backward_kernel(place_ref, pre_own, pre_one, pre_two, pre_three, proj_ref, mix_ref,
                    balance_ref, gate_ref, spec_own, spec_sib, shared_own, shared_sib, tower_ref,
                    spec_slope, shared_slope, sent_ref, field_ref, scaled_ref, score_ref, acc_ref):
    step = pl.program_id(0)
    task, core = place_ref[0], place_ref[1]

    @pl.when(step == 0)
    def _():
        acc_ref[...] = jnp.zeros_like(acc_ref)
        mix = mix_ref[...]
        lane = iota(mix.shape, 1)

        def column(index):
            return jnp.sum(jnp.where(lane == index, mix, 0.0), axis=1, keepdims=True)

        score = jnp.where(lane // 8 == task, -mix * balance_ref[...], 0.0)
        for shift, pre_ref in enumerate((pre_own, pre_one, pre_two, pre_three)):
            other = (task - shift) & 3
            index = other * 8 + 1 + task
            scaled = column(index) * pre_ref[...].astype(f32)
            scaled_ref[shift] = scaled.astype(bf16)
            gained = jnp.sum(scaled * proj_ref[other], axis=1, keepdims=True)
            score = score + jnp.where(lane == index, gained, 0.0)
        scaled = column(task * 8) * pre_own[...].astype(f32)
        scaled_ref[4] = scaled.astype(bf16)
        gained = jnp.sum(scaled * proj_ref[4], axis=1, keepdims=True)
        score_ref[...] = score + jnp.where(lane == task * 8, gained, 0.0)

    shared_back = dot_last(scaled_ref[0], tower_ref[task])
    for shift in (1, 2, 3):
        shared_back = shared_back + dot_last(scaled_ref[shift], tower_ref[(task - shift) & 3])
    spec_back = dot_last(scaled_ref[4], tower_ref[task])
    spec_inner = (spec_back * spec_slope[...].astype(f32)).astype(bf16)
    shared_inner = (shared_back * shared_slope[...].astype(f32)).astype(bf16)
    acc_ref[0] += dot_last(spec_inner, spec_own[...]) + dot_last(shared_inner, shared_own[...])
    acc_ref[1] += dot_last(spec_inner, spec_sib[...]) + dot_last(shared_inner, shared_sib[...])

    @pl.when(step == pl.num_programs(0) - 1)
    def _():
        score = score_ref[...]
        parts = []
        for _ in range(3):
            parts.append(score.astype(bf16))
            score = score - parts[-1].astype(f32)
        for rel in range(2):
            half = core if rel == 0 else 1 - core
            gate = gate_ref[pl.ds(pl.multiple_of(half * 256, 256), 256), :]
            total = acc_ref[rel] + dot_last(parts[2], gate)
            total = total + dot_last(parts[1], gate) + dot_last(parts[0], gate)
            for side in range(2):
                block = total[:, side * 128 : side * 128 + 128]
                slot = (2 * half + side - task) & 3
                sent_ref[slot] = block.astype(bf16)

                @pl.when(slot == 0)
                def _():
                    field_ref[...] = block


def dense_specs(tile):
    weight = pl.BlockSpec((256, tile), lambda i: (0, i))
    tower = pl.BlockSpec((4, tile, 256), lambda i: (0, i, 0))
    return weight, tower


def whole_spec(*shape):
    return pl.BlockSpec(shape, lambda i: (0,) * len(shape))


def ring(size, shift):
    return [(i, (i + shift) % size) for i in range(size)]


def along_task(value, shift):
    return lax.ppermute(value, "task", ring(4, shift))


def across_core(value):
    return lax.ppermute(value, "fsdp", [(0, 1), (1, 0)])


def along_x(value, shift):
    return lax.ppermute(
        value, "table", [(z * 4 + x, z * 4 + (x + shift) % 4) for z in range(8) for x in range(4)]
    )


def along_z(value, shift):
    return lax.ppermute(
        value,
        "table",
        [(z * 4 + x, (z + shift) % 8 * 4 + x) for z in range(8) for x in range(4)],
    )


def at(stack, index):
    return lax.dynamic_index_in_dim(stack, index, 0, keepdims=False)


def local(
    raw_ids,
    bag_len,
    labels,
    emb_table,
    bucket_map,
    spec_weight,
    shared_weight,
    gate_weight,
    tower_weight,
    head_vector,
):
    task = lax.axis_index("task")
    core = lax.axis_index("fsdp")
    table_index = lax.axis_index("table")
    depth, across = table_index // 4, table_index % 4
    me = table_index * 2 + core
    samples = raw_ids.shape[0]
    lookups = OWNERS * CAP

    tower_all = lax.all_gather(tower_weight[0], ("task", "fsdp"), axis=0, tiled=True)
    tower_all = tower_all.reshape(4, 4096, 256)
    spec_sib = across_core(spec_weight[0])
    shared_sib = across_core(shared_weight[0])

    ids_t = raw_ids[:, 0, :].T
    req, hot_row = pl.pallas_call(
        bucket_kernel,
        out_shape=(
            jax.ShapeDtypeStruct((OWNERS, CAP), i32),
            jax.ShapeDtypeStruct((1, HOT_LANES), i32),
        ),
        in_specs=[VMEM] * 2,
        out_specs=(VMEM, VMEM),
        compiler_params=params(16),
    )(ids_t, bag_len.reshape(1, samples))
    hot_index = hot_row[0, HOT_CAP]
    hot_z, hot_x, hot_c = hot_index // 8, hot_index // 2 % 4, hot_index % 2
    away_z, away_x = (depth - hot_z) % 8, (across - hot_x) % 4

    row_map = bucket_map[0].reshape(64, 128)
    planes = jnp.concatenate([row_map >> 6, row_map & 63], axis=0).astype(bf16)
    map_t = jnp.concatenate([(row_map >> 6).T, (row_map & 63).T], axis=0).astype(bf16)
    shard_rows = emb_table[0]

    pieces = jnp.concatenate(
        [shard_rows.reshape(8, 512, 128), planes.reshape(8, 16, 128)], axis=1
    ).reshape(2, 4, PIECE_ROWS, 128)
    half = jnp.where(hot_c == core, at(pieces, core), across_core(at(pieces, 1 - core)))

    asked = lax.all_to_all(req, ("table", "fsdp"), split_axis=0, concat_axis=0, tiled=True)
    asked = asked.reshape(lookups // 128, 128)

    quarters = [at(half, across)] + [
        along_x(at(half, (across + shift) % 4), shift) for shift in (1, 2, 3)
    ]
    part = lax.select_n(away_x, *quarters)
    part, asked = lax.optimization_barrier((part, asked))
    part = lax.select_n(
        jnp.where(away_z == 1, 1, jnp.where(away_z == 7, 2, 0)),
        part,
        along_z(part, 1),
        along_z(part, 7),
    )

    fetched = gather_call(asked, map_t, shard_rows)
    fetched, part = lax.optimization_barrier((fetched, part))
    part = lax.select_n(
        jnp.where((away_z >= 2) & (away_z <= 4), 1, jnp.where((away_z == 5) | (away_z == 6), 2, 0)),
        part,
        along_z(part, 3),
        along_z(part, 5),
    )
    hot_own = jnp.stack([part] + [along_x(part, shift) for shift in (1, 2, 3)])
    returned = lax.all_to_all(
        fetched.reshape(OWNERS, CAP, 128),
        ("table", "fsdp"),
        split_axis=0,
        concat_axis=0,
        tiled=True,
    )
    gate_cat = jnp.pad(gate_weight, ((0, 0), (0, 0), (0, 3))).transpose(1, 0, 2)
    gate_cat = jnp.pad(gate_cat.reshape(512, 32), ((0, 0), (0, 96)))
    req_wide = req.reshape(lookups // 128, 128)
    returned, hot_own, gate_cat, req_wide = lax.optimization_barrier(
        (returned, hot_own, gate_cat, req_wide)
    )
    returned = returned.reshape(lookups, 128)
    hot_sib = across_core(hot_own)

    place = jnp.stack([depth, across, core]).astype(i32)
    pooled = pl.pallas_call(
        pool_kernel,
        out_shape=jax.ShapeDtypeStruct((samples, 128), bf16),
        in_specs=[SMEM] + [VMEM] * 6,
        out_specs=VMEM,
        compiler_params=params(16),
    )(place, req_wide, hot_row, returned, hbm(hot_own), hbm(hot_sib), bag_len)

    hot_wide = jnp.pad(hot_row, ((0, 7), (0, 512 - HOT_LANES)))
    hot_all = lax.all_gather(hot_wide, ("table", "fsdp"), axis=0, tiled=True)
    is_hot = hot_index == me
    felt = jnp.stack([pooled] + [along_task(pooled, shift) for shift in (1, 2, 3)])
    dense_place = jnp.stack([task, core]).astype(i32)
    weight, tower = dense_specs(TILE)
    wide = spec_weight.shape[2]
    grid = (wide // TILE,)
    weights = [
        hbm(value)
        for value in (spec_weight[0], spec_sib, shared_weight[0], shared_sib, tower_all)
    ]
    *sent, partial, proj, mix, spec_slope, shared_slope = pl.pallas_call(
        forward_kernel,
        grid=grid,
        out_shape=(
            *[pltpu.HBM((samples, 256), bf16)] * 3,
            pltpu.HBM((samples, 256), f32),
            pltpu.HBM((5, samples, 256), f32),
            pltpu.HBM((samples, 128), f32),
            pltpu.HBM((samples, wide), bf16),
            pltpu.HBM((samples, wide), bf16),
        ),
        in_specs=[SMEM, whole_spec(4, samples, 128)]
        + [weight] * 4
        + [tower, whole_spec(512, 128)],
        out_specs=(
            *[whole_spec(samples, 256)] * 3,
            whole_spec(samples, 256),
            whole_spec(5, samples, 256),
            whole_spec(samples, 128),
            weight,
            weight,
        ),
        scratch_shapes=[pltpu.VMEM((5, samples, 256), f32)],
        compiler_params=params(16),
    )(dense_place, hbm(felt), *weights, hbm(gate_cat))
    received = [along_task(sent[shift - 1], shift) for shift in (1, 2, 3)]
    logit_own, pre_grad, balance = pl.pallas_call(
        middle_kernel,
        out_shape=(
            pltpu.HBM((samples, 1), f32),
            pltpu.HBM((samples, 256), bf16),
            pltpu.HBM((samples, 1), f32),
        ),
        in_specs=[VMEM] * 6,
        out_specs=(VMEM,) * 3,
        compiler_params=params(16),
    )(hbm(partial), *received, head_vector, labels)
    others = [along_task(pre_grad, shift) for shift in (1, 2, 3)]
    sent_blocks, field_grad = pl.pallas_call(
        backward_kernel,
        grid=grid,
        out_shape=(
            pltpu.HBM((4, samples, 128), bf16),
            pltpu.HBM((samples, 128), f32),
        ),
        in_specs=[SMEM]
        + [whole_spec(samples, 256)] * 4
        + [
            whole_spec(5, samples, 256),
            whole_spec(samples, 128),
            whole_spec(samples, 1),
            whole_spec(512, 128),
        ]
        + [weight] * 4
        + [tower, weight, weight],
        out_specs=(whole_spec(4, samples, 128), whole_spec(samples, 128)),
        scratch_shapes=[
            pltpu.VMEM((5, samples, 256), bf16),
            pltpu.VMEM((samples, 128), f32),
            pltpu.VMEM((2, samples, 256), f32),
        ],
        compiler_params=params(16),
    )(dense_place, hbm(pre_grad), *others, hbm(proj),
      hbm(mix), hbm(balance), hbm(gate_cat), *weights, hbm(spec_slope),
      hbm(shared_slope))
    later = (sent_blocks[0, 0, 0].astype(f32) * 0.0).astype(i32)
    hot_codes = hot_all[:, :HOT_LANES] + later
    rows, samps = pl.pallas_call(
        map_kernel,
        grid=(1,),
        out_shape=(jax.ShapeDtypeStruct((96, 128), i32),) * 2,
        in_specs=[
            SMEM,
            whole_spec(*asked.shape),
            pl.BlockSpec((8 * OWNERS, 128), lambda i: (0, 0)),
            pl.BlockSpec((8 * OWNERS, 128), lambda i: (0, 1)),
            whole_spec(*map_t.shape),
        ],
        out_specs=(whole_spec(96, 128),) * 2,
        scratch_shapes=[pltpu.VMEM((96, 128), i32)],
        cost_estimate=cost(4e9),
        compiler_params=params(16),
    )(is_hot.astype(i32).reshape(1), asked, hot_codes, hot_codes, map_t)
    blocks = [along_task(sent_blocks[shift], shift).astype(f32) for shift in (1, 2, 3)]
    field_grad = field_grad + (blocks[0] + blocks[1] + blocks[2])
    lookup_grad = (field_grad / bag_len.astype(f32)).astype(bf16)
    lookup_grad, rows, samps = lax.optimization_barrier((lookup_grad, rows, samps))

    place4 = jnp.stack([depth, across, core, jnp.where(is_hot, 3, 1)]).astype(i32)
    near = jnp.stack([lookup_grad] + [along_x(lookup_grad, shift) for shift in (1, 2, 3)])
    near_sib = across_core(near)
    table_grad = None
    up, down = near, near
    every = (0, 1, 2, 3)
    steps, ready = ((0, every),), [near, near_sib]
    for step in (1, 2, 3):
        up, down = along_z(up, 1), along_z(down, 7)
        table_grad = scatter_call(steps, place4, rows, samps, ready, table_grad)
        table_grad, up, down = lax.optimization_barrier((table_grad, up, down))
        steps = ((step, every), (-step, every))
        ready = [up, across_core(up), down, across_core(down)]
    far = [along_z(up[:2], 1), along_z(down[2:], 7)]
    table_grad = scatter_call(steps, place4, rows, samps, ready, table_grad)
    table_grad, *far = lax.optimization_barrier((table_grad, *far))
    table_grad = scatter_call(
        ((4, (0, 1)), (4, (2, 3))),
        place4,
        rows,
        samps,
        [far[0], across_core(far[0]), far[1], across_core(far[1])],
        table_grad,
        last=True,
    )
    return (logit_own, table_grad[None])


def solution(mesh):
    return jax.shard_map(
        local,
        mesh=mesh,
        in_specs=(
            P(("table", "fsdp"), "task", None),
            P(("table", "fsdp"), "task"),
            P(("table", "fsdp"), "task"),
            P("task", ("table", "fsdp"), None),
            P("task", ("table", "fsdp")),
            P("task", "fsdp", None),
            P("task", "fsdp", None),
            P(),
            P("task", "fsdp", None),
            P("task", None),
        ),
        out_specs=(P(("table", "fsdp"), "task"), P("task", ("table", "fsdp"), None)),
        check_vma=False,
    )
```

```python
import functools

import jax
import jax.numpy as jnp
from jax import lax
from jax.experimental import pallas as pl
from jax.experimental.pallas import tpu as pltpu
from jax.sharding import PartitionSpec as P

loss_scale = 1024.0
highest = lax.Precision.HIGHEST
contract_last = (((1,), (1,)), ((), ()))
bf16 = jnp.bfloat16
f32 = jnp.float32
i32 = jnp.int32
OWNERS = 64
CAP = 64
HOT_CAP = 192
HOT_LANES = 256
RAW_BITS = 13
PIECE_ROWS = 528
HIGHS = 8
LOW_ROWS = 512
LOW_BITS = 9
TILE = 1024
VMEM = pl.BlockSpec(memory_space=pltpu.VMEM)
SMEM = pl.BlockSpec(memory_space=pltpu.SMEM)


def params(mib):
    return pltpu.CompilerParams(vmem_limit_bytes=mib * 1024 * 1024)


def sigmoid(value):
    return 0.5 * jnp.tanh(0.5 * value) + 0.5


def hbm(value):
    return pltpu.with_memory_space_constraint(value, pltpu.HBM)


def near_core(value):
    return pltpu.with_memory_space_constraint(value, pltpu.VMEM)


def cost(flops):
    return pl.CostEstimate(flops=int(flops), bytes_accessed=4194304, transcendentals=0)


def iota(shape, dim):
    return lax.broadcasted_iota(i32, shape, dim)


def dot(left, right):
    return jnp.dot(left, right, preferred_element_type=f32)


def dot_last(left, right):
    return lax.dot_general(left, right, contract_last, preferred_element_type=f32)


def one_hot(mask):
    return jnp.where(mask, 1.0, 0.0).astype(bf16)


def packed_hot(mask):
    return jnp.where(mask, jnp.ones((), bf16), jnp.zeros((), bf16))


def bucket_kernel(ids_ref, len_ref, req_ref, hot_ref):
    slots, samples = ids_ref.shape
    owner_row = iota((OWNERS, samples), 0)
    sample1 = (iota((1, samples), 1) + 1).astype(f32)
    before = one_hot(iota((samples, samples), 0) < iota((samples, samples), 1))
    rank_row = iota((HOT_CAP, samples), 0)
    lens = len_ref[...]
    base = jnp.zeros((OWNERS, 1), f32)
    total = jnp.zeros((3 * OWNERS, HOT_CAP), f32)
    for slot in range(slots):
        ids = ids_ref[slot : slot + 1, :]
        owner = jnp.where(lens > slot, ids >> RAW_BITS, -1)
        hit = owner_row == owner
        hit_f = jnp.where(hit, 1.0, 0.0)
        seen = dot(hit_f.astype(bf16), before) + base
        base = base + jnp.sum(hit_f, axis=1, keepdims=True)
        rank = jnp.sum(hit_f * seen, axis=0, keepdims=True).astype(i32)
        raw = ids & ((1 << RAW_BITS) - 1)
        planes = jnp.concatenate(
            [
                hit_f * (raw >> 7).astype(f32),
                hit_f * (raw & 127).astype(f32),
                hit_f * sample1,
            ],
            axis=0,
        ).astype(bf16)
        total = total + dot_last(planes, one_hot(rank_row == rank))
    hot = base > float(CAP)
    high, low, samp = total[:OWNERS], total[OWNERS : 2 * OWNERS], total[2 * OWNERS :]
    cold = jnp.where(hot, 0.0, 1.0)
    warm = 1.0 - cold
    raw_all = high * 128.0 + low
    req_ref[...] = ((samp * cold)[:, :CAP].astype(i32) << 16) + (raw_all * cold)[:, :CAP].astype(
        i32
    )
    hot_samp = jnp.sum(samp * warm, axis=0, keepdims=True).astype(i32)
    hot_raw = jnp.sum(raw_all * warm, axis=0, keepdims=True).astype(i32)
    index = jnp.sum(warm * iota((OWNERS, 1), 0).astype(f32), axis=0, keepdims=True)
    pad = jnp.broadcast_to(index.astype(i32), (1, HOT_LANES - HOT_CAP))
    hot_ref[...] = jnp.concatenate([(hot_samp << 16) + hot_raw, pad], axis=1)


def map_rows(code, map_t):
    lanes = code.shape[1]
    raw = code & 0xFFFF
    spread = one_hot(iota((64, lanes), 0) == (raw >> 7))
    both = dot(map_t, spread)
    wide = both[:128] * 64.0 + both[128:]
    return jnp.sum(
        jnp.where(iota((128, lanes), 0) == (raw & 127), wide, 0.0), axis=0, keepdims=True
    )


def as_column(row):
    return jnp.broadcast_to(row, (128, row.shape[1])).T


def low_one_hot(low):
    lane = iota(low.shape, 1)
    narrow = low.astype(f32).astype(bf16)
    return jnp.concatenate(
        [
            packed_hot(narrow == (lane + 128 * part).astype(f32).astype(bf16))
            for part in range(2)
        ],
        axis=1,
    )


def pick_rows(spread, high, table_pair, pairs):
    found = jnp.zeros((spread.shape[0], 128), f32)
    for pair in range(pairs):
        both = dot(spread, table_pair(pair))
        found = jnp.where(high == 2 * pair, both[:, :128], found)
        found = jnp.where(high == 2 * pair + 1, both[:, 128:], found)
    return found


def gather_kernel(req_ref, map_ref, table_ref, *refs):
    out_ref, spread_ref, high_ref = refs[-3:]
    map_t = map_ref[...]
    chunks = req_ref.shape[0]

    @pl.loop(0, chunks // 4)
    def _(group):
        for part in range(4):
            chunk = group * 4 + part
            code = req_ref[pl.ds(chunk, 1), :]
            row = jnp.where(code >= 65536, map_rows(code, map_t), -1.0)
            column = as_column(row).astype(i32)
            place = pl.ds(pl.multiple_of(chunk * 128, 128), 128)
            spread_ref[place, :] = low_one_hot(column & 255)
            high_ref[place, :] = column >> 8

    block = 512

    @pl.loop(0, out_ref.shape[0] // block)
    def _(step):
        place = pl.ds(pl.multiple_of(step * block, block), block)

        def table_pair(pair):
            return jnp.concatenate(
                [
                    table_ref[pair * 512 : pair * 512 + 256, :],
                    table_ref[pair * 512 + 256 : pair * 512 + 512, :],
                ],
                axis=1,
            )

        out_ref[place, :] = pick_rows(
            spread_ref[place, :], high_ref[place, :], table_pair, 8
        ).astype(bf16)


def gather_call(asked, map_t, table, half, before):
    chunks = asked.shape[0] // 2
    rows = chunks * 128
    operands = [asked, map_t, table]
    specs = [
        pl.BlockSpec((chunks, 128), lambda i: (half, 0)),
        whole_spec(*map_t.shape),
        whole_spec(*table.shape),
    ]
    aliases = {}
    if before is not None:
        operands.append(before)
        specs.append(pl.BlockSpec(memory_space=pl.ANY))
        aliases = {3: 0}
    return pl.pallas_call(
        gather_kernel,
        grid=(1,),
        out_shape=jax.ShapeDtypeStruct((2 * rows, 128), bf16),
        in_specs=specs,
        out_specs=pl.BlockSpec((rows, 128), lambda i: (half, 0)),
        scratch_shapes=[pltpu.VMEM((rows, 256), bf16), pltpu.VMEM((rows, 128), i32)],
        input_output_aliases=aliases,
        cost_estimate=cost(5e9),
        compiler_params=params(16),
    )(*operands)


def map_kernel(hot_ref, asked_ref, low_ref, high_ref, map_ref, after_ref, row_ref, samp_ref, code_ref):
    map_t = map_ref[...]
    blocks = asked_ref.shape[0]
    is_hot = hot_ref[0] == 1
    code_ref[0:blocks, :] = asked_ref[...]

    @pl.when(is_hot)
    def _():
        for chunk in range(3):
            all_ref = low_ref if chunk < 2 else high_ref
            even = all_ref[pl.ds(0, blocks, stride=16), :]
            odd = all_ref[pl.ds(8, blocks, stride=16), :]
            lanes = slice(chunk % 2 * 64, chunk % 2 * 64 + 64)
            code_ref[chunk * blocks : (chunk + 1) * blocks, :] = jnp.concatenate(
                [even[:, lanes], odd[:, lanes]], axis=1
            )

    @pl.loop(0, jnp.where(is_hot, 3 * blocks // 8, blocks // 8))
    def _(group):
        place = pl.ds(pl.multiple_of(group * 8, 8), 8)
        code = code_ref[place, :]
        samp_ref[place, :] = (code >> 16) - 1
        for half in range(2):
            wide = jnp.concatenate(
                [code[half * 4 + part : half * 4 + part + 1, :] for part in range(4)], axis=1
            )
            row = map_rows(wide, map_t).astype(i32)
            for part in range(4):
                row_ref[pl.ds(group * 8 + half * 4 + part, 1), :] = row[
                    :, part * 128 : part * 128 + 128
                ]


def pool_kernel(place_ref, req_ref, hot_ref, rows_ref, own_ref, sib_ref, len_ref, out_ref):
    samples = out_ref.shape[0]
    sample_col = iota((samples, 128), 0)
    summed = jnp.zeros((samples, 128), f32)
    for pair in range(req_ref.shape[0] // 2):
        parts = [
            one_hot(sample_col == (req_ref[2 * pair + half : 2 * pair + half + 1, :] >> 16) - 1)
            for half in range(2)
        ]
        summed = summed + dot(
            jnp.concatenate(parts, axis=1), rows_ref[pair * 256 : pair * 256 + 256, :]
        )
    across, core = place_ref[1], place_ref[2]

    def piece(index, start, size):
        half, slot = index // 4, (across - index % 4) & 3
        own = own_ref[slot, start : start + size, :].astype(f32)
        sib = sib_ref[slot, start : start + size, :].astype(f32)
        return jnp.where(core == half, own, sib)

    planes = [
        jnp.concatenate([piece(4 * plane + part, 512, 16) for part in range(4)], axis=0).T
        for plane in range(2)
    ]
    map_t = jnp.concatenate(planes, axis=0).astype(bf16)
    code = jnp.where(iota((1, HOT_LANES), 1) < HOT_CAP, hot_ref[...], 0)
    row = jnp.where(code >= 65536, map_rows(code, map_t), -1.0)
    column = as_column(row).astype(i32)

    def table_pair(pair):
        return jnp.concatenate(
            [piece(pair, 0, 256), piece(pair, 256, 256)], axis=1
        ).astype(bf16)

    hot_rows = pick_rows(low_one_hot(column & 255), column >> 8, table_pair, 8).astype(bf16)
    spread = one_hot(iota((samples, HOT_LANES), 0) == (code >> 16) - 1)
    summed = summed + dot(spread, hot_rows)
    out_ref[...] = (summed / len_ref[...].astype(f32)).astype(bf16)


def scatter_block(chunks, level, shifts, across, offset, row_ref, samp_ref, own_ref, sib_ref,
                  out_ref, wide_ref, spread_ref):
    lane = iota((128, 128), 1).astype(f32).astype(bf16)
    sub = iota((128, 128), 0).astype(f32).astype(bf16)
    span = 128 * chunks
    for order, shift in enumerate(shifts):
        block = level + ((across - shift) & 3)
        highs, picks = [], []
        for chunk in range(chunks):
            line = pl.ds(chunk * 32 + block, 1)
            row, samp = row_ref[line, :], samp_ref[line, :]
            samp = as_column(jnp.where(samp < 0, -1, samp + offset).astype(f32))
            low = row & (LOW_ROWS - 1)
            start = order * span + chunk * 128
            place = slice(start, start + 128)
            highs.append(as_column((row >> LOW_BITS).astype(f32)).astype(bf16))
            picks.append(
                jnp.concatenate(
                    [packed_hot((samp - 128.0 * part).astype(bf16) == lane) for part in range(4)],
                    axis=1,
                )
            )
            for part in range(LOW_ROWS // 128):
                shifted = (low - 128 * part).astype(f32)
                shifted = jnp.broadcast_to(shifted, (128, 128)).astype(bf16)
                spread_ref[part * 128 : part * 128 + 128, place] = packed_hot(shifted == sub)
        picked = jnp.concatenate(picks, axis=0) if chunks > 1 else picks[0]
        source = jnp.concatenate([own_ref[order], sib_ref[order]], axis=0)
        slots = dot(picked, source).astype(bf16)
        for chunk in range(chunks):
            start = order * span + chunk * 128
            part = slots[chunk * 128 : chunk * 128 + 128, :]
            for high in range(HIGHS):
                wide_ref[start : start + 128, high * 128 : high * 128 + 128] = jnp.where(
                    highs[chunk] == jnp.asarray(high, bf16), part, jnp.zeros((), bf16)
                )
    used = len(shifts) * span
    for pair in range(HIGHS // 2):
        both = dot(spread_ref[:, :used], wide_ref[:used, pair * 256 : pair * 256 + 256])
        start = 2 * pair * LOW_ROWS
        out_ref[start : start + LOW_ROWS, :] += both[:, :128]
        out_ref[start + LOW_ROWS : start + 2 * LOW_ROWS, :] += both[:, 128:]


def scatter_kernel(steps, place_ref, row_ref, samp_ref, *refs):
    count = len(steps)
    grads = refs[: 2 * count]
    if len(refs) == 2 * count + 3:
        out_ref, wide_ref, spread_ref = refs[2 * count :]
        out_ref[...] = jnp.zeros_like(out_ref)
    else:
        seen_ref, out_ref, wide_ref, spread_ref = refs[2 * count :]
        out_ref[...] = seen_ref[...]
    depth, across, core, chunks = place_ref[0], place_ref[1], place_ref[2], place_ref[3]
    offset = jnp.where(iota((1, 128), 1) < 64, core * 256, (1 - core) * 256)

    def every(count_chunks):
        for index, (step, shifts) in enumerate(steps):
            level = ((depth - step) & 7) * 4
            scatter_block(
                count_chunks, level, shifts, across, offset, row_ref, samp_ref,
                grads[2 * index], grads[2 * index + 1], out_ref, wide_ref, spread_ref,
            )

    @pl.when(chunks == 1)
    def _():
        every(1)

    @pl.when(chunks != 1)
    def _():
        every(3)


def scatter_call(steps, place, rows, samps, grads, seen, last=False):
    operands = [place, rows, samps, *grads]
    if seen is not None:
        operands.append(near_core(seen))
    return pl.pallas_call(
        functools.partial(scatter_kernel, steps),
        out_shape=(pltpu.HBM if last else pltpu.VMEM)((4096, 128), f32),
        in_specs=[SMEM] + [VMEM] * (len(operands) - 1),
        out_specs=VMEM,
        scratch_shapes=[
            pltpu.VMEM((1536, HIGHS * 128), bf16),
            pltpu.VMEM((LOW_ROWS, 1536), bf16),
        ],
        cost_estimate=cost(4e9 * len(steps)),
        compiler_params=params(16),
    )(*operands)


def forward_kernel(place_ref, felt_ref, spec_own, spec_sib, shared_own, shared_sib, tower_ref,
                   gate_ref, sent_one, sent_two, sent_three, partial_ref, proj_ref, mix_ref, spec_slope, shared_slope,
                   acc_ref):
    step = pl.program_id(0)
    task, core = place_ref[0], place_ref[1]
    first = (task - 2 * core) & 3
    own = jnp.concatenate([felt_ref[first], felt_ref[(first - 1) & 3]], axis=1)
    sib = jnp.concatenate([felt_ref[(first - 2) & 3], felt_ref[(first - 3) & 3]], axis=1)

    @pl.when(step == 0)
    def _():
        acc_ref[...] = jnp.zeros_like(acc_ref)
        scores = dot(own, gate_ref[pl.ds(pl.multiple_of(core * 256, 256), 256), :]) + dot(
            sib, gate_ref[pl.ds(pl.multiple_of(256 - core * 256, 256), 256), :]
        )
        lane = iota(scores.shape, 1)
        raised = jnp.where(lane % 8 < 5, jnp.exp(scores), 0.0)
        bottom = jnp.ones_like(raised)
        for other in range(4):
            group = lane // 8 == other
            whole = jnp.sum(jnp.where(group, raised, 0.0), axis=1, keepdims=True)
            bottom = jnp.where(group, whole, bottom)
        mix_ref[...] = raised / bottom

    def activate(value, slope_ref):
        sig = sigmoid(value)
        out = value * sig
        slope_ref[...] = (sig + out * (1.0 - sig)).astype(bf16)
        return out.astype(bf16)

    spec_out = activate(dot(own, spec_own[...]) + dot(sib, spec_sib[...]), spec_slope)
    shared_out = activate(dot(own, shared_own[...]) + dot(sib, shared_sib[...]), shared_slope)
    for other in range(4):
        acc_ref[other] += dot(shared_out, tower_ref[other])
    acc_ref[4] += dot(spec_out, tower_ref[task])

    @pl.when(step == pl.num_programs(0) - 1)
    def _():
        mix = mix_ref[...]
        lane = iota(mix.shape, 1)

        def column(index):
            return jnp.sum(jnp.where(lane == index, mix, 0.0), axis=1, keepdims=True)

        proj_ref[...] = acc_ref[...]
        for shift in range(4):
            other = (task + shift) & 3
            part = column(other * 8 + 1 + task) * acc_ref[other]
            if shift == 0:
                partial_ref[...] = part + column(task * 8) * acc_ref[4]
            else:
                (sent_one, sent_two, sent_three)[shift - 1][...] = part.astype(bf16)


def middle_kernel(partial_ref, one_ref, two_ref, three_ref, head_ref, label_ref, logit_ref,
                  pre_ref, balance_ref):
    value = partial_ref[...] + (
        one_ref[...].astype(f32) + two_ref[...].astype(f32) + three_ref[...].astype(f32)
    )
    head = head_ref[...].astype(f32)
    sig = sigmoid(value)
    logit = jnp.sum(value * sig * head, axis=1, keepdims=True)
    logit_ref[...] = logit
    grad = loss_scale * (sigmoid(logit) - label_ref[...].astype(f32))
    pre = (grad * head * (sig * (1.0 + value * (1.0 - sig)))).astype(bf16)
    pre_ref[...] = pre
    balance_ref[...] = jnp.sum(pre.astype(f32) * value, axis=1, keepdims=True)


def backward_kernel(place_ref, pre_own, pre_one, pre_two, pre_three, proj_ref, mix_ref,
                    balance_ref, gate_ref, spec_own, spec_sib, shared_own, shared_sib, tower_ref,
                    spec_slope, shared_slope, sent_one, sent_two, sent_three, field_ref,
                    scaled_ref, score_ref, acc_ref):
    step = pl.program_id(0)
    task, core = place_ref[0], place_ref[1]

    @pl.when(step == 0)
    def _():
        acc_ref[...] = jnp.zeros_like(acc_ref)
        mix = mix_ref[...]
        lane = iota(mix.shape, 1)

        def column(index):
            return jnp.sum(jnp.where(lane == index, mix, 0.0), axis=1, keepdims=True)

        score = jnp.where(lane // 8 == task, -mix * balance_ref[...], 0.0)
        for shift, pre_ref in enumerate((pre_own, pre_one, pre_two, pre_three)):
            other = (task - shift) & 3
            index = other * 8 + 1 + task
            scaled = column(index) * pre_ref[...].astype(f32)
            scaled_ref[shift] = scaled.astype(bf16)
            gained = jnp.sum(scaled * proj_ref[other], axis=1, keepdims=True)
            score = score + jnp.where(lane == index, gained, 0.0)
        scaled = column(task * 8) * pre_own[...].astype(f32)
        scaled_ref[4] = scaled.astype(bf16)
        gained = jnp.sum(scaled * proj_ref[4], axis=1, keepdims=True)
        score_ref[...] = score + jnp.where(lane == task * 8, gained, 0.0)

    shared_back = dot_last(scaled_ref[0], tower_ref[task])
    for shift in (1, 2, 3):
        shared_back = shared_back + dot_last(scaled_ref[shift], tower_ref[(task - shift) & 3])
    spec_back = dot_last(scaled_ref[4], tower_ref[task])
    spec_inner = (spec_back * spec_slope[...].astype(f32)).astype(bf16)
    shared_inner = (shared_back * shared_slope[...].astype(f32)).astype(bf16)
    acc_ref[0] += dot_last(spec_inner, spec_own[...]) + dot_last(shared_inner, shared_own[...])
    acc_ref[1] += dot_last(spec_inner, spec_sib[...]) + dot_last(shared_inner, shared_sib[...])

    @pl.when(step == pl.num_programs(0) - 1)
    def _():
        score = score_ref[...]
        parts = []
        for _ in range(3):
            parts.append(score.astype(bf16))
            score = score - parts[-1].astype(f32)
        for rel in range(2):
            half = core if rel == 0 else 1 - core
            gate = gate_ref[pl.ds(pl.multiple_of(half * 256, 256), 256), :]
            total = acc_ref[rel] + dot_last(parts[2], gate)
            total = total + dot_last(parts[1], gate) + dot_last(parts[0], gate)
            for side in range(2):
                block = total[:, side * 128 : side * 128 + 128]
                slot = (2 * half + side - task) & 3

                @pl.when(slot == 0)
                def _():
                    field_ref[...] = block

                for order, sent_ref in enumerate((sent_one, sent_two, sent_three)):

                    @pl.when(slot == order + 1)
                    def _():
                        sent_ref[...] = block.astype(bf16)


def dense_specs(tile):
    weight = pl.BlockSpec((256, tile), lambda i: (0, i))
    tower = pl.BlockSpec((4, tile, 256), lambda i: (0, i, 0))
    return weight, tower


def whole_spec(*shape):
    return pl.BlockSpec(shape, lambda i: (0,) * len(shape))


def ring(size, shift):
    return [(i, (i + shift) % size) for i in range(size)]


def along_task(value, shift):
    return lax.ppermute(value, "task", ring(4, shift))


def across_core(value):
    return lax.ppermute(value, "fsdp", [(0, 1), (1, 0)])


def along_x(value, shift):
    return lax.ppermute(
        value, "table", [(z * 4 + x, z * 4 + (x + shift) % 4) for z in range(8) for x in range(4)]
    )


def along_z(value, shift):
    return lax.ppermute(
        value,
        "table",
        [(z * 4 + x, (z + shift) % 8 * 4 + x) for z in range(8) for x in range(4)],
    )


def at(stack, index):
    return lax.dynamic_index_in_dim(stack, index, 0, keepdims=False)


def local(
    raw_ids,
    bag_len,
    labels,
    emb_table,
    bucket_map,
    spec_weight,
    shared_weight,
    gate_weight,
    tower_weight,
    head_vector,
):
    task = lax.axis_index("task")
    core = lax.axis_index("fsdp")
    table_index = lax.axis_index("table")
    depth, across = table_index // 4, table_index % 4
    me = table_index * 2 + core
    samples = raw_ids.shape[0]
    lookups = OWNERS * CAP

    tower_all = lax.all_gather(tower_weight[0], ("task", "fsdp"), axis=0, tiled=True)
    tower_all = tower_all.reshape(4, 4096, 256)
    spec_sib = across_core(spec_weight[0])
    shared_sib = across_core(shared_weight[0])

    ids_t = raw_ids[:, 0, :].T
    req, hot_row = pl.pallas_call(
        bucket_kernel,
        out_shape=(
            jax.ShapeDtypeStruct((OWNERS, CAP), i32),
            jax.ShapeDtypeStruct((1, HOT_LANES), i32),
        ),
        in_specs=[VMEM] * 2,
        out_specs=(VMEM, VMEM),
        compiler_params=params(16),
    )(ids_t, bag_len.reshape(1, samples))
    hot_index = hot_row[0, HOT_CAP]
    hot_z, hot_x, hot_c = hot_index // 8, hot_index // 2 % 4, hot_index % 2
    away_z, away_x = (depth - hot_z) % 8, (across - hot_x) % 4

    row_map = bucket_map[0].reshape(64, 128)
    planes = jnp.concatenate([row_map >> 6, row_map & 63], axis=0).astype(bf16)
    map_t = jnp.concatenate([(row_map >> 6).T, (row_map & 63).T], axis=0).astype(bf16)
    shard_rows = emb_table[0]

    pieces = jnp.concatenate(
        [shard_rows.reshape(8, 512, 128), planes.reshape(8, 16, 128)], axis=1
    ).reshape(2, 4, PIECE_ROWS, 128)
    half = jnp.where(hot_c == core, at(pieces, core), across_core(at(pieces, 1 - core)))

    asked = lax.all_to_all(req, ("table", "fsdp"), split_axis=0, concat_axis=0, tiled=True)
    asked = asked.reshape(lookups // 128, 128)

    quarters = [at(half, across)] + [
        along_x(at(half, (across + shift) % 4), shift) for shift in (1, 2, 3)
    ]
    part = lax.select_n(away_x, *quarters)
    part, asked = lax.optimization_barrier((part, asked))
    part = lax.select_n(
        jnp.where(away_z == 1, 1, jnp.where(away_z == 7, 2, 0)),
        part,
        along_z(part, 1),
        along_z(part, 7),
    )

    fetched = gather_call(asked, map_t, shard_rows, 0, None)
    fetched, part = lax.optimization_barrier((fetched, part))
    part = lax.select_n(
        jnp.where((away_z >= 2) & (away_z <= 4), 1, jnp.where((away_z == 5) | (away_z == 6), 2, 0)),
        part,
        along_z(part, 3),
        along_z(part, 5),
    )
    fetched = gather_call(asked, map_t, shard_rows, 1, fetched)
    fetched, part = lax.optimization_barrier((fetched, part))
    hot_own = jnp.stack([part] + [along_x(part, shift) for shift in (1, 2, 3)])
    returned = lax.all_to_all(
        fetched.reshape(OWNERS, CAP, 128),
        ("table", "fsdp"),
        split_axis=0,
        concat_axis=0,
        tiled=True,
    )
    gate_cat = jnp.pad(gate_weight, ((0, 0), (0, 0), (0, 3))).transpose(1, 0, 2)
    gate_cat = jnp.pad(gate_cat.reshape(512, 32), ((0, 0), (0, 96)))
    req_wide = req.reshape(lookups // 128, 128)
    returned, hot_own, gate_cat, req_wide = lax.optimization_barrier(
        (returned, hot_own, gate_cat, req_wide)
    )
    returned = returned.reshape(lookups, 128)
    hot_sib = across_core(hot_own)

    place = jnp.stack([depth, across, core]).astype(i32)
    pooled = pl.pallas_call(
        pool_kernel,
        out_shape=jax.ShapeDtypeStruct((samples, 128), bf16),
        in_specs=[SMEM] + [VMEM] * 6,
        out_specs=VMEM,
        compiler_params=params(16),
    )(place, req_wide, hot_row, returned, hbm(hot_own), hbm(hot_sib), bag_len)

    hot_wide = jnp.pad(hot_row, ((0, 7), (0, 512 - HOT_LANES)))
    hot_all = lax.all_gather(hot_wide, ("table", "fsdp"), axis=0, tiled=True)
    is_hot = hot_index == me
    felt = jnp.stack([pooled] + [along_task(pooled, shift) for shift in (1, 2, 3)])
    dense_place = jnp.stack([task, core]).astype(i32)
    weight, tower = dense_specs(TILE)
    wide = spec_weight.shape[2]
    grid = (wide // TILE,)
    weights = [
        hbm(value)
        for value in (spec_weight[0], spec_sib, shared_weight[0], shared_sib, tower_all)
    ]
    *sent, partial, proj, mix, spec_slope, shared_slope = pl.pallas_call(
        forward_kernel,
        grid=grid,
        out_shape=(
            *[pltpu.HBM((samples, 256), bf16)] * 3,
            pltpu.HBM((samples, 256), f32),
            pltpu.HBM((5, samples, 256), f32),
            pltpu.HBM((samples, 128), f32),
            pltpu.HBM((samples, wide), bf16),
            pltpu.HBM((samples, wide), bf16),
        ),
        in_specs=[SMEM, whole_spec(4, samples, 128)]
        + [weight] * 4
        + [tower, whole_spec(512, 128)],
        out_specs=(
            *[whole_spec(samples, 256)] * 3,
            whole_spec(samples, 256),
            whole_spec(5, samples, 256),
            whole_spec(samples, 128),
            weight,
            weight,
        ),
        scratch_shapes=[pltpu.VMEM((5, samples, 256), f32)],
        compiler_params=params(28),
    )(dense_place, hbm(felt), *weights, hbm(gate_cat))
    received = [along_task(sent[shift - 1], shift) for shift in (1, 2, 3)]
    logit_own, pre_grad, balance = pl.pallas_call(
        middle_kernel,
        out_shape=(
            pltpu.HBM((samples, 1), f32),
            pltpu.HBM((samples, 256), bf16),
            pltpu.HBM((samples, 1), f32),
        ),
        in_specs=[VMEM] * 6,
        out_specs=(VMEM,) * 3,
        compiler_params=params(16),
    )(hbm(partial), *received, head_vector, labels)
    others = [along_task(pre_grad, shift) for shift in (1, 2, 3)]
    *sent_blocks, field_grad = pl.pallas_call(
        backward_kernel,
        grid=grid,
        out_shape=(
            *[pltpu.HBM((samples, 128), bf16)] * 3,
            pltpu.HBM((samples, 128), f32),
        ),
        in_specs=[SMEM]
        + [whole_spec(samples, 256)] * 4
        + [
            whole_spec(5, samples, 256),
            whole_spec(samples, 128),
            whole_spec(samples, 1),
            whole_spec(512, 128),
        ]
        + [weight] * 4
        + [tower, weight, weight],
        out_specs=(whole_spec(samples, 128),) * 4,
        scratch_shapes=[
            pltpu.VMEM((5, samples, 256), bf16),
            pltpu.VMEM((samples, 128), f32),
            pltpu.VMEM((2, samples, 256), f32),
        ],
        compiler_params=params(28),
    )(dense_place, hbm(pre_grad), *others, hbm(proj),
      hbm(mix), hbm(balance), hbm(gate_cat), *weights, hbm(spec_slope),
      hbm(shared_slope))
    rows, samps = pl.pallas_call(
        map_kernel,
        grid=(1,),
        out_shape=(jax.ShapeDtypeStruct((96, 128), i32),) * 2,
        in_specs=[
            SMEM,
            whole_spec(*asked.shape),
            pl.BlockSpec((8 * OWNERS, 128), lambda i: (0, 0)),
            pl.BlockSpec((8 * OWNERS, 128), lambda i: (0, 1)),
            whole_spec(*map_t.shape),
            pl.BlockSpec(memory_space=pl.ANY),
        ],
        out_specs=(whole_spec(96, 128),) * 2,
        scratch_shapes=[pltpu.VMEM((96, 128), i32)],
        cost_estimate=cost(4e9),
        compiler_params=params(16),
    )(is_hot.astype(i32).reshape(1), asked, hbm(hot_all), hbm(hot_all), map_t, hbm(field_grad))
    blocks = [along_task(sent_blocks[shift - 1], shift).astype(f32) for shift in (1, 2, 3)]
    field_grad = field_grad + (blocks[0] + blocks[1] + blocks[2])
    lookup_grad = (field_grad / bag_len.astype(f32)).astype(bf16)
    lookup_grad, rows, samps = lax.optimization_barrier((lookup_grad, rows, samps))

    place4 = jnp.stack([depth, across, core, jnp.where(is_hot, 3, 1)]).astype(i32)
    near = jnp.stack([lookup_grad] + [along_x(lookup_grad, shift) for shift in (1, 2, 3)])
    near_sib = across_core(near)
    table_grad = None
    up, down = near, near
    every = (0, 1, 2, 3)
    steps, ready = ((0, every),), [near, near_sib]
    for step in (1, 2, 3):
        up, down = along_z(up, 1), along_z(down, 7)
        table_grad = scatter_call(steps, place4, rows, samps, ready, table_grad)
        table_grad, up, down = lax.optimization_barrier((table_grad, up, down))
        steps = ((step, every), (-step, every))
        ready = [up, across_core(up), down, across_core(down)]
    far = [along_z(up[:2], 1), along_z(down[2:], 7)]
    table_grad = scatter_call(steps, place4, rows, samps, ready, table_grad)
    table_grad, *far = lax.optimization_barrier((table_grad, *far))
    table_grad = scatter_call(
        ((4, (0, 1)), (4, (2, 3))),
        place4,
        rows,
        samps,
        [far[0], across_core(far[0]), far[1], across_core(far[1])],
        table_grad,
        last=True,
    )
    return (logit_own, table_grad[None])


def solution(mesh):
    return jax.shard_map(
        local,
        mesh=mesh,
        in_specs=(
            P(("table", "fsdp"), "task", None),
            P(("table", "fsdp"), "task"),
            P(("table", "fsdp"), "task"),
            P("task", ("table", "fsdp"), None),
            P("task", ("table", "fsdp")),
            P("task", "fsdp", None),
            P("task", "fsdp", None),
            P(),
            P("task", "fsdp", None),
            P("task", None),
        ),
        out_specs=(P(("table", "fsdp"), "task"), P("task", ("table", "fsdp"), None)),
        check_vma=False,
    )
```

```python
import functools

import jax
import jax.numpy as jnp
from jax import lax
from jax.experimental import pallas as pl
from jax.experimental.pallas import tpu as pltpu
from jax.sharding import PartitionSpec as P

loss_scale = 1024.0
highest = lax.Precision.HIGHEST
contract_last = (((1,), (1,)), ((), ()))
bf16 = jnp.bfloat16
f32 = jnp.float32
i32 = jnp.int32
OWNERS = 64
CAP = 64
HOT_CAP = 192
HOT_LANES = 256
RAW_BITS = 13
PIECE_ROWS = 528
HIGHS = 8
LOW_ROWS = 512
LOW_BITS = 9
TILE = 1024
VMEM = pl.BlockSpec(memory_space=pltpu.VMEM)
SMEM = pl.BlockSpec(memory_space=pltpu.SMEM)


def params(mib):
    return pltpu.CompilerParams(vmem_limit_bytes=mib * 1024 * 1024)


def sigmoid(value):
    return 0.5 * jnp.tanh(0.5 * value) + 0.5


def hbm(value):
    return pltpu.with_memory_space_constraint(value, pltpu.HBM)


def near_core(value):
    return pltpu.with_memory_space_constraint(value, pltpu.VMEM)


def cost(flops):
    return pl.CostEstimate(flops=int(flops), bytes_accessed=4194304, transcendentals=0)


def iota(shape, dim):
    return lax.broadcasted_iota(i32, shape, dim)


def dot(left, right):
    return jnp.dot(left, right, preferred_element_type=f32)


def dot_last(left, right):
    return lax.dot_general(left, right, contract_last, preferred_element_type=f32)


def one_hot(mask):
    return jnp.where(mask, 1.0, 0.0).astype(bf16)


def packed_hot(mask):
    return jnp.where(mask, jnp.ones((), bf16), jnp.zeros((), bf16))


def bucket_kernel(ids_ref, len_ref, req_ref, hot_ref):
    slots, samples = ids_ref.shape
    owner_row = iota((OWNERS, samples), 0)
    sample1 = (iota((1, samples), 1) + 1).astype(f32)
    before = one_hot(iota((samples, samples), 0) < iota((samples, samples), 1))
    rank_row = iota((HOT_CAP, samples), 0)
    lens = len_ref[...]
    base = jnp.zeros((OWNERS, 1), f32)
    total = jnp.zeros((3 * OWNERS, HOT_CAP), f32)
    for slot in range(slots):
        ids = ids_ref[slot : slot + 1, :]
        owner = jnp.where(lens > slot, ids >> RAW_BITS, -1)
        hit = owner_row == owner
        hit_f = jnp.where(hit, 1.0, 0.0)
        seen = dot(hit_f.astype(bf16), before) + base
        base = base + jnp.sum(hit_f, axis=1, keepdims=True)
        rank = jnp.sum(hit_f * seen, axis=0, keepdims=True).astype(i32)
        raw = ids & ((1 << RAW_BITS) - 1)
        planes = jnp.concatenate(
            [
                hit_f * (raw >> 7).astype(f32),
                hit_f * (raw & 127).astype(f32),
                hit_f * sample1,
            ],
            axis=0,
        ).astype(bf16)
        total = total + dot_last(planes, one_hot(rank_row == rank))
    hot = base > float(CAP)
    high, low, samp = total[:OWNERS], total[OWNERS : 2 * OWNERS], total[2 * OWNERS :]
    cold = jnp.where(hot, 0.0, 1.0)
    warm = 1.0 - cold
    raw_all = high * 128.0 + low
    req_ref[...] = ((samp * cold)[:, :CAP].astype(i32) << 16) + (raw_all * cold)[:, :CAP].astype(
        i32
    )
    hot_samp = jnp.sum(samp * warm, axis=0, keepdims=True).astype(i32)
    hot_raw = jnp.sum(raw_all * warm, axis=0, keepdims=True).astype(i32)
    index = jnp.sum(warm * iota((OWNERS, 1), 0).astype(f32), axis=0, keepdims=True)
    pad = jnp.broadcast_to(index.astype(i32), (1, HOT_LANES - HOT_CAP))
    hot_ref[...] = jnp.concatenate([(hot_samp << 16) + hot_raw, pad], axis=1)


def map_rows(code, map_t):
    lanes = code.shape[1]
    raw = code & 0xFFFF
    spread = one_hot(iota((64, lanes), 0) == (raw >> 7))
    both = dot(map_t, spread)
    wide = both[:128] * 64.0 + both[128:]
    return jnp.sum(
        jnp.where(iota((128, lanes), 0) == (raw & 127), wide, 0.0), axis=0, keepdims=True
    )


def as_column(row):
    return jnp.broadcast_to(row, (128, row.shape[1])).T


def low_one_hot(low):
    lane = iota(low.shape, 1)
    narrow = low.astype(f32).astype(bf16)
    return jnp.concatenate(
        [
            packed_hot(narrow == (lane + 128 * part).astype(f32).astype(bf16))
            for part in range(2)
        ],
        axis=1,
    )


def pick_rows(spread, high, table_pair, pairs):
    found = jnp.zeros((spread.shape[0], 128), f32)
    for pair in range(pairs):
        both = dot(spread, table_pair(pair))
        found = jnp.where(high == 2 * pair, both[:, :128], found)
        found = jnp.where(high == 2 * pair + 1, both[:, 128:], found)
    return found


def gather_kernel(req_ref, map_ref, table_ref, *refs):
    out_ref, spread_ref, high_ref = refs[-3:]
    map_t = map_ref[...]
    chunks = req_ref.shape[0]

    @pl.loop(0, chunks // 4)
    def _(group):
        for part in range(4):
            chunk = group * 4 + part
            code = req_ref[pl.ds(chunk, 1), :]
            row = jnp.where(code >= 65536, map_rows(code, map_t), -1.0)
            column = as_column(row).astype(i32)
            place = pl.ds(pl.multiple_of(chunk * 128, 128), 128)
            spread_ref[place, :] = low_one_hot(column & 255)
            high_ref[place, :] = column >> 8

    block = 512

    @pl.loop(0, out_ref.shape[0] // block)
    def _(step):
        place = pl.ds(pl.multiple_of(step * block, block), block)

        def table_pair(pair):
            return jnp.concatenate(
                [
                    table_ref[pair * 512 : pair * 512 + 256, :],
                    table_ref[pair * 512 + 256 : pair * 512 + 512, :],
                ],
                axis=1,
            )

        out_ref[place, :] = pick_rows(
            spread_ref[place, :], high_ref[place, :], table_pair, 8
        ).astype(bf16)


def gather_call(asked, map_t, table, half, before):
    chunks = asked.shape[0] // 2
    rows = chunks * 128
    operands = [asked, map_t, table]
    specs = [
        pl.BlockSpec((chunks, 128), lambda i: (half, 0)),
        whole_spec(*map_t.shape),
        whole_spec(*table.shape),
    ]
    aliases = {}
    if before is not None:
        operands.append(before)
        specs.append(pl.BlockSpec(memory_space=pl.ANY))
        aliases = {3: 0}
    return pl.pallas_call(
        gather_kernel,
        grid=(1,),
        out_shape=jax.ShapeDtypeStruct((2 * rows, 128), bf16),
        in_specs=specs,
        out_specs=pl.BlockSpec((rows, 128), lambda i: (half, 0)),
        scratch_shapes=[pltpu.VMEM((rows, 256), bf16), pltpu.VMEM((rows, 128), i32)],
        input_output_aliases=aliases,
        cost_estimate=cost(5e9),
        compiler_params=params(16),
    )(*operands)


def map_kernel(hot_ref, asked_ref, low_ref, high_ref, map_ref, after_ref, row_ref, samp_ref, code_ref):
    map_t = map_ref[...]
    blocks = asked_ref.shape[0]
    is_hot = hot_ref[0] == 1
    code_ref[0:blocks, :] = asked_ref[...]

    @pl.when(is_hot)
    def _():
        for chunk in range(3):
            all_ref = low_ref if chunk < 2 else high_ref
            even = all_ref[pl.ds(0, blocks, stride=16), :]
            odd = all_ref[pl.ds(8, blocks, stride=16), :]
            lanes = slice(chunk % 2 * 64, chunk % 2 * 64 + 64)
            code_ref[chunk * blocks : (chunk + 1) * blocks, :] = jnp.concatenate(
                [even[:, lanes], odd[:, lanes]], axis=1
            )

    @pl.loop(0, jnp.where(is_hot, 3 * blocks // 8, blocks // 8))
    def _(group):
        place = pl.ds(pl.multiple_of(group * 8, 8), 8)
        code = code_ref[place, :]
        samp_ref[place, :] = (code >> 16) - 1
        for half in range(2):
            wide = jnp.concatenate(
                [code[half * 4 + part : half * 4 + part + 1, :] for part in range(4)], axis=1
            )
            row = map_rows(wide, map_t).astype(i32)
            for part in range(4):
                row_ref[pl.ds(group * 8 + half * 4 + part, 1), :] = row[
                    :, part * 128 : part * 128 + 128
                ]


def pool_kernel(place_ref, req_ref, hot_ref, rows_ref, own_ref, sib_ref, len_ref, out_ref):
    samples = out_ref.shape[0]
    sample_col = iota((samples, 128), 0)
    summed = jnp.zeros((samples, 128), f32)
    for pair in range(req_ref.shape[0] // 2):
        parts = [
            one_hot(sample_col == (req_ref[2 * pair + half : 2 * pair + half + 1, :] >> 16) - 1)
            for half in range(2)
        ]
        summed = summed + dot(
            jnp.concatenate(parts, axis=1), rows_ref[pair * 256 : pair * 256 + 256, :]
        )
    across, core = place_ref[1], place_ref[2]

    def piece(index, start, size):
        half, slot = index // 4, (across - index % 4) & 3
        own = own_ref[slot, start : start + size, :].astype(f32)
        sib = sib_ref[slot, start : start + size, :].astype(f32)
        return jnp.where(core == half, own, sib)

    planes = [
        jnp.concatenate([piece(4 * plane + part, 512, 16) for part in range(4)], axis=0).T
        for plane in range(2)
    ]
    map_t = jnp.concatenate(planes, axis=0).astype(bf16)
    code = jnp.where(iota((1, HOT_LANES), 1) < HOT_CAP, hot_ref[...], 0)
    row = jnp.where(code >= 65536, map_rows(code, map_t), -1.0)
    column = as_column(row).astype(i32)

    def table_pair(pair):
        return jnp.concatenate(
            [piece(pair, 0, 256), piece(pair, 256, 256)], axis=1
        ).astype(bf16)

    hot_rows = pick_rows(low_one_hot(column & 255), column >> 8, table_pair, 8).astype(bf16)
    spread = one_hot(iota((samples, HOT_LANES), 0) == (code >> 16) - 1)
    summed = summed + dot(spread, hot_rows)
    out_ref[...] = (summed / len_ref[...].astype(f32)).astype(bf16)


def scatter_block(chunks, level, shifts, across, offset, row_ref, samp_ref, own_ref, sib_ref,
                  out_ref, wide_ref, spread_ref):
    lane = iota((128, 128), 1).astype(f32).astype(bf16)
    sub = iota((128, 128), 0).astype(f32).astype(bf16)
    span = 128 * chunks
    for order, shift in enumerate(shifts):
        block = level + ((across - shift) & 3)
        highs, picks = [], []
        for chunk in range(chunks):
            line = pl.ds(chunk * 32 + block, 1)
            row, samp = row_ref[line, :], samp_ref[line, :]
            samp = as_column(jnp.where(samp < 0, -1, samp + offset).astype(f32))
            low = row & (LOW_ROWS - 1)
            start = order * span + chunk * 128
            place = slice(start, start + 128)
            highs.append(as_column((row >> LOW_BITS).astype(f32)).astype(bf16))
            picks.append(
                jnp.concatenate(
                    [packed_hot((samp - 128.0 * part).astype(bf16) == lane) for part in range(4)],
                    axis=1,
                )
            )
            for part in range(LOW_ROWS // 128):
                shifted = (low - 128 * part).astype(f32)
                shifted = jnp.broadcast_to(shifted, (128, 128)).astype(bf16)
                spread_ref[part * 128 : part * 128 + 128, place] = packed_hot(shifted == sub)
        picked = jnp.concatenate(picks, axis=0) if chunks > 1 else picks[0]
        source = jnp.concatenate([own_ref[order], sib_ref[order]], axis=0)
        slots = dot(picked, source).astype(bf16)
        for chunk in range(chunks):
            start = order * span + chunk * 128
            part = slots[chunk * 128 : chunk * 128 + 128, :]
            for high in range(HIGHS):
                wide_ref[start : start + 128, high * 128 : high * 128 + 128] = jnp.where(
                    highs[chunk] == jnp.asarray(high, bf16), part, jnp.zeros((), bf16)
                )
    used = len(shifts) * span
    for pair in range(HIGHS // 2):
        both = dot(spread_ref[:, :used], wide_ref[:used, pair * 256 : pair * 256 + 256])
        start = 2 * pair * LOW_ROWS
        out_ref[start : start + LOW_ROWS, :] += both[:, :128]
        out_ref[start + LOW_ROWS : start + 2 * LOW_ROWS, :] += both[:, 128:]


def scatter_kernel(steps, place_ref, row_ref, samp_ref, *refs):
    count = len(steps)
    grads = refs[: 2 * count]
    if len(refs) == 2 * count + 3:
        out_ref, wide_ref, spread_ref = refs[2 * count :]
        out_ref[...] = jnp.zeros_like(out_ref)
    else:
        seen_ref, out_ref, wide_ref, spread_ref = refs[2 * count :]
        out_ref[...] = seen_ref[...]
    depth, across, core, chunks = place_ref[0], place_ref[1], place_ref[2], place_ref[3]
    offset = jnp.where(iota((1, 128), 1) < 64, core * 256, (1 - core) * 256)

    def every(count_chunks):
        for index, (step, shifts) in enumerate(steps):
            level = ((depth - step) & 7) * 4
            scatter_block(
                count_chunks, level, shifts, across, offset, row_ref, samp_ref,
                grads[2 * index], grads[2 * index + 1], out_ref, wide_ref, spread_ref,
            )

    @pl.when(chunks == 1)
    def _():
        every(1)

    @pl.when(chunks != 1)
    def _():
        every(3)


def scatter_call(steps, place, rows, samps, grads, seen, last=False):
    operands = [place, rows, samps, *grads]
    if seen is not None:
        operands.append(near_core(seen))
    return pl.pallas_call(
        functools.partial(scatter_kernel, steps),
        out_shape=(pltpu.HBM if last else pltpu.VMEM)((4096, 128), f32),
        in_specs=[SMEM] + [VMEM] * (len(operands) - 1),
        out_specs=VMEM,
        scratch_shapes=[
            pltpu.VMEM((1536, HIGHS * 128), bf16),
            pltpu.VMEM((LOW_ROWS, 1536), bf16),
        ],
        cost_estimate=cost(4e9 * len(steps)),
        compiler_params=params(16),
    )(*operands)


def feature_halves(task, core, felt_ref):
    first = (task - 2 * core) & 3
    own = jnp.concatenate([felt_ref[first], felt_ref[(first - 1) & 3]], axis=1)
    sib = jnp.concatenate([felt_ref[(first - 2) & 3], felt_ref[(first - 3) & 3]], axis=1)
    return own, sib


def activate(value, slope_ref):
    sig = sigmoid(value)
    out = value * sig
    slope_ref[...] = (sig + out * (1.0 - sig)).astype(bf16)
    return out.astype(bf16)


def mix_column(mix, index):
    return jnp.sum(jnp.where(iota(mix.shape, 1) == index, mix, 0.0), axis=1, keepdims=True)


def forward_kernel(place_ref, felt_ref, shared_own, shared_sib, tower_ref, gate_ref, sent_one,
                   sent_two, sent_three, partial_ref, proj_ref, mix_ref, shared_slope, acc_ref):
    step = pl.program_id(0)
    task, core = place_ref[0], place_ref[1]
    own, sib = feature_halves(task, core, felt_ref)

    @pl.when(step == 0)
    def _():
        acc_ref[...] = jnp.zeros_like(acc_ref)
        scores = dot(own, gate_ref[pl.ds(pl.multiple_of(core * 256, 256), 256), :]) + dot(
            sib, gate_ref[pl.ds(pl.multiple_of(256 - core * 256, 256), 256), :]
        )
        lane = iota(scores.shape, 1)
        raised = jnp.where(lane % 8 < 5, jnp.exp(scores), 0.0)
        bottom = jnp.ones_like(raised)
        for other in range(4):
            group = lane // 8 == other
            whole = jnp.sum(jnp.where(group, raised, 0.0), axis=1, keepdims=True)
            bottom = jnp.where(group, whole, bottom)
        mix_ref[...] = raised / bottom

    shared_out = activate(dot(own, shared_own[...]) + dot(sib, shared_sib[...]), shared_slope)
    for other in range(4):
        acc_ref[other] += dot(shared_out, tower_ref[other])

    @pl.when(step == pl.num_programs(0) - 1)
    def _():
        mix = mix_ref[...]
        proj_ref[...] = acc_ref[...]
        for shift in range(4):
            other = (task + shift) & 3
            part = mix_column(mix, other * 8 + 1 + task) * acc_ref[other]
            if shift == 0:
                partial_ref[...] = part
            else:
                (sent_one, sent_two, sent_three)[shift - 1][...] = part.astype(bf16)


def forward_spec_kernel(place_ref, felt_ref, spec_own, spec_sib, tower_ref, mix_ref, part_ref,
                        proj_ref, spec_slope, acc_ref):
    step = pl.program_id(0)
    task, core = place_ref[0], place_ref[1]
    own, sib = feature_halves(task, core, felt_ref)

    @pl.when(step == 0)
    def _():
        acc_ref[...] = jnp.zeros_like(acc_ref)

    spec_out = activate(dot(own, spec_own[...]) + dot(sib, spec_sib[...]), spec_slope)
    acc_ref[...] += dot(spec_out, tower_ref[0])

    @pl.when(step == pl.num_programs(0) - 1)
    def _():
        proj_ref[...] = acc_ref[...]
        part_ref[...] = mix_column(mix_ref[...], task * 8) * acc_ref[...]


def middle_kernel(partial_ref, spec_ref, one_ref, two_ref, three_ref, head_ref, label_ref, logit_ref,
                  pre_ref, balance_ref):
    value = (partial_ref[...] + spec_ref[...]) + (
        one_ref[...].astype(f32) + two_ref[...].astype(f32) + three_ref[...].astype(f32)
    )
    head = head_ref[...].astype(f32)
    sig = sigmoid(value)
    logit = jnp.sum(value * sig * head, axis=1, keepdims=True)
    logit_ref[...] = logit
    grad = loss_scale * (sigmoid(logit) - label_ref[...].astype(f32))
    pre = (grad * head * (sig * (1.0 + value * (1.0 - sig)))).astype(bf16)
    pre_ref[...] = pre
    balance_ref[...] = jnp.sum(pre.astype(f32) * value, axis=1, keepdims=True)


def backward_spec_kernel(place_ref, pre_ref, proj_ref, mix_ref, balance_ref, spec_own, spec_sib,
                         tower_ref, spec_slope, field_ref, score_ref, scaled_ref):
    step = pl.program_id(0)
    task = place_ref[0]

    @pl.when(step == 0)
    def _():
        field_ref[...] = jnp.zeros_like(field_ref)
        mix = mix_ref[...]
        lane = iota(mix.shape, 1)
        scaled = mix_column(mix, task * 8) * pre_ref[...].astype(f32)
        scaled_ref[...] = scaled.astype(bf16)
        gained = jnp.sum(scaled * proj_ref[...], axis=1, keepdims=True)
        score = jnp.where(lane // 8 == task, -mix * balance_ref[...], 0.0)
        score_ref[...] = score + jnp.where(lane == task * 8, gained, 0.0)

    back = dot_last(scaled_ref[...], tower_ref[0])
    inner = (back * spec_slope[...].astype(f32)).astype(bf16)
    field_ref[0] += dot_last(inner, spec_own[...])
    field_ref[1] += dot_last(inner, spec_sib[...])


def backward_kernel(place_ref, pre_own, pre_one, pre_two, pre_three, proj_ref, mix_ref,
                    gate_ref, start_ref, before_ref, shared_own, shared_sib, tower_ref,
                    shared_slope, sent_one, sent_two, sent_three, field_ref, scaled_ref, score_ref,
                    acc_ref):
    step = pl.program_id(0)
    task, core = place_ref[0], place_ref[1]

    @pl.when(step == 0)
    def _():
        acc_ref[...] = start_ref[...]
        mix = mix_ref[...]
        lane = iota(mix.shape, 1)
        score = before_ref[...]
        for shift, pre_ref in enumerate((pre_own, pre_one, pre_two, pre_three)):
            other = (task - shift) & 3
            index = other * 8 + 1 + task
            scaled = mix_column(mix, index) * pre_ref[...].astype(f32)
            scaled_ref[shift] = scaled.astype(bf16)
            gained = jnp.sum(scaled * proj_ref[other], axis=1, keepdims=True)
            score = score + jnp.where(lane == index, gained, 0.0)
        score_ref[...] = score

    shared_back = dot_last(scaled_ref[0], tower_ref[task])
    for shift in (1, 2, 3):
        shared_back = shared_back + dot_last(scaled_ref[shift], tower_ref[(task - shift) & 3])
    shared_inner = (shared_back * shared_slope[...].astype(f32)).astype(bf16)
    acc_ref[0] += dot_last(shared_inner, shared_own[...])
    acc_ref[1] += dot_last(shared_inner, shared_sib[...])

    @pl.when(step == pl.num_programs(0) - 1)
    def _():
        score = score_ref[...]
        parts = []
        for _ in range(3):
            parts.append(score.astype(bf16))
            score = score - parts[-1].astype(f32)
        for rel in range(2):
            half = core if rel == 0 else 1 - core
            gate = gate_ref[pl.ds(pl.multiple_of(half * 256, 256), 256), :]
            total = acc_ref[rel] + dot_last(parts[2], gate)
            total = total + dot_last(parts[1], gate) + dot_last(parts[0], gate)
            for side in range(2):
                block = total[:, side * 128 : side * 128 + 128]
                slot = (2 * half + side - task) & 3

                @pl.when(slot == 0)
                def _():
                    field_ref[...] = block

                for order, sent_ref in enumerate((sent_one, sent_two, sent_three)):

                    @pl.when(slot == order + 1)
                    def _():
                        sent_ref[...] = block.astype(bf16)


def tower_spec(tile):
    return pl.BlockSpec((1, tile, 256), lambda i, place: (place[0], i, 0))


def prefetched(spec):
    index = spec.index_map
    return pl.BlockSpec(spec.block_shape, lambda i, place: index(i))


def dense_specs(tile):
    weight = pl.BlockSpec((256, tile), lambda i: (0, i))
    tower = pl.BlockSpec((4, tile, 256), lambda i: (0, i, 0))
    return weight, tower


def whole_spec(*shape):
    return pl.BlockSpec(shape, lambda i: (0,) * len(shape))


def ring(size, shift):
    return [(i, (i + shift) % size) for i in range(size)]


def along_task(value, shift):
    return lax.ppermute(value, "task", ring(4, shift))


def across_core(value):
    return lax.ppermute(value, "fsdp", [(0, 1), (1, 0)])


def along_x(value, shift):
    return lax.ppermute(
        value, "table", [(z * 4 + x, z * 4 + (x + shift) % 4) for z in range(8) for x in range(4)]
    )


def along_z(value, shift):
    return lax.ppermute(
        value,
        "table",
        [(z * 4 + x, (z + shift) % 8 * 4 + x) for z in range(8) for x in range(4)],
    )


def at(stack, index):
    return lax.dynamic_index_in_dim(stack, index, 0, keepdims=False)


def local(
    raw_ids,
    bag_len,
    labels,
    emb_table,
    bucket_map,
    spec_weight,
    shared_weight,
    gate_weight,
    tower_weight,
    head_vector,
):
    task = lax.axis_index("task")
    core = lax.axis_index("fsdp")
    table_index = lax.axis_index("table")
    depth, across = table_index // 4, table_index % 4
    me = table_index * 2 + core
    samples = raw_ids.shape[0]
    lookups = OWNERS * CAP

    tower_all = lax.all_gather(tower_weight[0], ("task", "fsdp"), axis=0, tiled=True)
    tower_all = tower_all.reshape(4, 4096, 256)
    spec_sib = across_core(spec_weight[0])
    shared_sib = across_core(shared_weight[0])

    ids_t = raw_ids[:, 0, :].T
    req, hot_row = pl.pallas_call(
        bucket_kernel,
        out_shape=(
            jax.ShapeDtypeStruct((OWNERS, CAP), i32),
            jax.ShapeDtypeStruct((1, HOT_LANES), i32),
        ),
        in_specs=[VMEM] * 2,
        out_specs=(VMEM, VMEM),
        compiler_params=params(16),
    )(ids_t, bag_len.reshape(1, samples))
    hot_index = hot_row[0, HOT_CAP]
    hot_z, hot_x, hot_c = hot_index // 8, hot_index // 2 % 4, hot_index % 2
    away_z, away_x = (depth - hot_z) % 8, (across - hot_x) % 4

    row_map = bucket_map[0].reshape(64, 128)
    planes = jnp.concatenate([row_map >> 6, row_map & 63], axis=0).astype(bf16)
    map_t = jnp.concatenate([(row_map >> 6).T, (row_map & 63).T], axis=0).astype(bf16)
    shard_rows = emb_table[0]

    pieces = jnp.concatenate(
        [shard_rows.reshape(8, 512, 128), planes.reshape(8, 16, 128)], axis=1
    ).reshape(2, 4, PIECE_ROWS, 128)
    half = jnp.where(hot_c == core, at(pieces, core), across_core(at(pieces, 1 - core)))

    asked = lax.all_to_all(req, ("table", "fsdp"), split_axis=0, concat_axis=0, tiled=True)
    asked = asked.reshape(lookups // 128, 128)

    quarters = [at(half, across)] + [
        along_x(at(half, (across + shift) % 4), shift) for shift in (1, 2, 3)
    ]
    part = lax.select_n(away_x, *quarters)
    part, asked = lax.optimization_barrier((part, asked))
    part = lax.select_n(
        jnp.where(away_z == 1, 1, jnp.where(away_z == 7, 2, 0)),
        part,
        along_z(part, 1),
        along_z(part, 7),
    )

    fetched = gather_call(asked, map_t, shard_rows, 0, None)
    fetched, part = lax.optimization_barrier((fetched, part))
    part = lax.select_n(
        jnp.where((away_z >= 2) & (away_z <= 4), 1, jnp.where((away_z == 5) | (away_z == 6), 2, 0)),
        part,
        along_z(part, 3),
        along_z(part, 5),
    )
    fetched = gather_call(asked, map_t, shard_rows, 1, fetched)
    fetched, part = lax.optimization_barrier((fetched, part))
    hot_own = jnp.stack([part] + [along_x(part, shift) for shift in (1, 2, 3)])
    returned = lax.all_to_all(
        fetched.reshape(OWNERS, CAP, 128),
        ("table", "fsdp"),
        split_axis=0,
        concat_axis=0,
        tiled=True,
    )
    gate_cat = jnp.pad(gate_weight, ((0, 0), (0, 0), (0, 3))).transpose(1, 0, 2)
    gate_cat = jnp.pad(gate_cat.reshape(512, 32), ((0, 0), (0, 96)))
    req_wide = req.reshape(lookups // 128, 128)
    returned, hot_own, gate_cat, req_wide = lax.optimization_barrier(
        (returned, hot_own, gate_cat, req_wide)
    )
    returned = returned.reshape(lookups, 128)
    hot_sib = across_core(hot_own)

    place = jnp.stack([depth, across, core]).astype(i32)
    pooled = pl.pallas_call(
        pool_kernel,
        out_shape=jax.ShapeDtypeStruct((samples, 128), bf16),
        in_specs=[SMEM] + [VMEM] * 6,
        out_specs=VMEM,
        compiler_params=params(16),
    )(place, req_wide, hot_row, returned, hot_own, hot_sib, bag_len)

    hot_wide = jnp.pad(hot_row, ((0, 7), (0, 512 - HOT_LANES)))
    hot_near = jnp.pad(across_core(hot_row), ((0, 7), (0, 512 - HOT_LANES)))
    hot_wide = jnp.concatenate(
        [jnp.where(core == 0, hot_wide, hot_near), jnp.where(core == 0, hot_near, hot_wide)], axis=0
    )
    hot_all = lax.all_gather(hot_wide, "table", axis=0, tiled=True)
    is_hot = hot_index == me
    felt = jnp.stack([pooled] + [along_task(pooled, shift) for shift in (1, 2, 3)])
    dense_place = jnp.stack([task, core]).astype(i32)
    weight, tower = dense_specs(TILE)
    wide = spec_weight.shape[2]
    grid = (wide // TILE,)
    spec_pair = [hbm(spec_weight[0]), hbm(spec_sib)]
    shared_pair = [hbm(shared_weight[0]), hbm(shared_sib)]
    towers, felt, gate_cat = hbm(tower_all), hbm(felt), hbm(gate_cat)
    flat = pltpu.HBM((samples, 256), f32)
    flat_spec = whole_spec(samples, 256)
    mix_spec = whole_spec(samples, 128)
    *sent, partial, proj, mix, shared_slope = pl.pallas_call(
        forward_kernel,
        grid=grid,
        out_shape=(
            *[pltpu.HBM((samples, 256), bf16)] * 3,
            flat,
            pltpu.HBM((4, samples, 256), f32),
            pltpu.HBM((samples, 128), f32),
            pltpu.HBM((samples, wide), bf16),
        ),
        in_specs=[SMEM, whole_spec(4, samples, 128), weight, weight, tower, whole_spec(512, 128)],
        out_specs=(
            *[flat_spec] * 4,
            whole_spec(4, samples, 256),
            mix_spec,
            weight,
        ),
        scratch_shapes=[pltpu.VMEM((4, samples, 256), f32)],
        cost_estimate=cost(9e9),
        compiler_params=params(28),
    )(dense_place, felt, *shared_pair, towers, gate_cat)
    received = [along_task(sent[shift - 1], shift) for shift in (1, 2, 3)]
    spec_part, spec_proj, spec_slope = pl.pallas_call(
        forward_spec_kernel,
        grid_spec=pltpu.PrefetchScalarGridSpec(
            num_scalar_prefetch=1,
            grid=grid,
            in_specs=[
                prefetched(spec)
                for spec in (whole_spec(4, samples, 128), weight, weight)
            ]
            + [tower_spec(TILE), prefetched(mix_spec)],
            out_specs=[prefetched(spec) for spec in (flat_spec, flat_spec, weight)],
            scratch_shapes=[pltpu.VMEM((samples, 256), f32)],
        ),
        out_shape=(flat, flat, pltpu.HBM((samples, wide), bf16)),
        cost_estimate=cost(5e9),
        compiler_params=params(28),
    )(dense_place, felt, *spec_pair, towers, hbm(mix))
    logit_own, pre_grad, balance = pl.pallas_call(
        middle_kernel,
        out_shape=(
            pltpu.HBM((samples, 1), f32),
            pltpu.HBM((samples, 256), bf16),
            pltpu.HBM((samples, 1), f32),
        ),
        in_specs=[VMEM] * 7,
        out_specs=(VMEM,) * 3,
        compiler_params=params(16),
    )(hbm(partial), hbm(spec_part), *received, head_vector, labels)
    others = [along_task(pre_grad, shift) for shift in (1, 2, 3)]
    start, score = pl.pallas_call(
        backward_spec_kernel,
        grid_spec=pltpu.PrefetchScalarGridSpec(
            num_scalar_prefetch=1,
            grid=grid,
            in_specs=[
                prefetched(spec)
                for spec in (
                    flat_spec, flat_spec, mix_spec, whole_spec(samples, 1), weight, weight,
                )
            ]
            + [tower_spec(TILE), prefetched(weight)],
            out_specs=[prefetched(spec) for spec in (whole_spec(2, samples, 256), mix_spec)],
            scratch_shapes=[pltpu.VMEM((samples, 256), bf16)],
        ),
        out_shape=(pltpu.HBM((2, samples, 256), f32), pltpu.HBM((samples, 128), f32)),
        cost_estimate=cost(5e9),
        compiler_params=params(28),
    )(dense_place, hbm(pre_grad), hbm(spec_proj), hbm(mix), hbm(balance), *spec_pair, towers,
      hbm(spec_slope))
    *sent_blocks, field_grad = pl.pallas_call(
        backward_kernel,
        grid=grid,
        out_shape=(
            *[pltpu.HBM((samples, 128), bf16)] * 3,
            pltpu.HBM((samples, 128), f32),
        ),
        in_specs=[SMEM]
        + [flat_spec] * 4
        + [
            whole_spec(4, samples, 256),
            mix_spec,
            whole_spec(512, 128),
            whole_spec(2, samples, 256),
            mix_spec,
        ]
        + [weight, weight, tower, weight],
        out_specs=(mix_spec,) * 4,
        scratch_shapes=[
            pltpu.VMEM((4, samples, 256), bf16),
            pltpu.VMEM((samples, 128), f32),
            pltpu.VMEM((2, samples, 256), f32),
        ],
        cost_estimate=cost(9e9),
        compiler_params=params(28),
    )(dense_place, hbm(pre_grad), *others, hbm(proj), hbm(mix), gate_cat, hbm(start), hbm(score),
      *shared_pair, towers, hbm(shared_slope))
    rows, samps = pl.pallas_call(
        map_kernel,
        grid=(1,),
        out_shape=(jax.ShapeDtypeStruct((96, 128), i32),) * 2,
        in_specs=[
            SMEM,
            whole_spec(*asked.shape),
            pl.BlockSpec((8 * OWNERS, 128), lambda i: (0, 0)),
            pl.BlockSpec((8 * OWNERS, 128), lambda i: (0, 1)),
            whole_spec(*map_t.shape),
            pl.BlockSpec(memory_space=pl.ANY),
        ],
        out_specs=(whole_spec(96, 128),) * 2,
        scratch_shapes=[pltpu.VMEM((96, 128), i32)],
        cost_estimate=cost(4e9),
        compiler_params=params(16),
    )(is_hot.astype(i32).reshape(1), asked, hbm(hot_all), hbm(hot_all), map_t, hbm(field_grad))
    blocks = [along_task(sent_blocks[shift - 1], shift).astype(f32) for shift in (1, 2, 3)]
    field_grad = field_grad + (blocks[0] + blocks[1] + blocks[2])
    lookup_grad = (field_grad / bag_len.astype(f32)).astype(bf16)
    lookup_grad, rows, samps = lax.optimization_barrier((lookup_grad, rows, samps))

    place4 = jnp.stack([depth, across, core, jnp.where(is_hot, 3, 1)]).astype(i32)
    near = jnp.stack([lookup_grad] + [along_x(lookup_grad, shift) for shift in (1, 2, 3)])
    near_sib = across_core(near)
    table_grad = None
    up, down = near, near
    every = (0, 1, 2, 3)
    steps, ready = ((0, every),), [near, near_sib]
    for step in (1, 2, 3):
        up, down = along_z(up, 1), along_z(down, 7)
        table_grad = scatter_call(steps, place4, rows, samps, ready, table_grad)
        table_grad, up, down = lax.optimization_barrier((table_grad, up, down))
        steps = ((step, every), (-step, every))
        ready = [up, across_core(up), down, across_core(down)]
    far = [along_z(up[:2], 1), along_z(down[2:], 7)]
    table_grad = scatter_call(steps, place4, rows, samps, ready, table_grad)
    table_grad, *far = lax.optimization_barrier((table_grad, *far))
    table_grad = scatter_call(
        ((4, (0, 1)), (4, (2, 3))),
        place4,
        rows,
        samps,
        [far[0], across_core(far[0]), far[1], across_core(far[1])],
        table_grad,
        last=True,
    )
    return (logit_own, table_grad[None])


def solution(mesh):
    return jax.shard_map(
        local,
        mesh=mesh,
        in_specs=(
            P(("table", "fsdp"), "task", None),
            P(("table", "fsdp"), "task"),
            P(("table", "fsdp"), "task"),
            P("task", ("table", "fsdp"), None),
            P("task", ("table", "fsdp")),
            P("task", "fsdp", None),
            P("task", "fsdp", None),
            P(),
            P("task", "fsdp", None),
            P("task", None),
        ),
        out_specs=(P(("table", "fsdp"), "task"), P("task", ("table", "fsdp"), None)),
        check_vma=False,
    )
```

```python
import functools

import jax
import jax.numpy as jnp
from jax import lax
from jax.experimental import pallas as pl
from jax.experimental.pallas import tpu as pltpu
from jax.sharding import PartitionSpec as P

loss_scale = 1024.0
highest = lax.Precision.HIGHEST
contract_last = (((1,), (1,)), ((), ()))
bf16 = jnp.bfloat16
f32 = jnp.float32
i32 = jnp.int32
OWNERS = 64
CAP = 64
HOT_CAP = 192
HOT_LANES = 256
RAW_BITS = 13
PIECE_ROWS = 528
HIGHS = 8
LOW_ROWS = 512
LOW_BITS = 9
TILE = 1024
VMEM = pl.BlockSpec(memory_space=pltpu.VMEM)
SMEM = pl.BlockSpec(memory_space=pltpu.SMEM)


def params(mib):
    return pltpu.CompilerParams(vmem_limit_bytes=mib * 1024 * 1024)


def sigmoid(value):
    return 0.5 * jnp.tanh(0.5 * value) + 0.5


def hbm(value):
    return pltpu.with_memory_space_constraint(value, pltpu.HBM)


def near_core(value):
    return pltpu.with_memory_space_constraint(value, pltpu.VMEM)


def cost(flops):
    return pl.CostEstimate(flops=int(flops), bytes_accessed=4194304, transcendentals=0)


def iota(shape, dim):
    return lax.broadcasted_iota(i32, shape, dim)


def dot(left, right):
    return jnp.dot(left, right, preferred_element_type=f32)


def dot_last(left, right):
    return lax.dot_general(left, right, contract_last, preferred_element_type=f32)


def one_hot(mask):
    return jnp.where(mask, 1.0, 0.0).astype(bf16)


def packed_hot(mask):
    return jnp.where(mask, jnp.ones((), bf16), jnp.zeros((), bf16))


def bucket_kernel(ids_ref, len_ref, req_ref, hot_ref):
    slots, samples = ids_ref.shape
    owner_row = iota((OWNERS, samples), 0)
    sample1 = (iota((1, samples), 1) + 1).astype(f32)
    before = one_hot(iota((samples, samples), 0) < iota((samples, samples), 1))
    rank_row = iota((HOT_CAP, samples), 0)
    lens = len_ref[...]
    base = jnp.zeros((OWNERS, 1), f32)
    total = jnp.zeros((3 * OWNERS, HOT_CAP), f32)
    for slot in range(slots):
        ids = ids_ref[slot : slot + 1, :]
        owner = jnp.where(lens > slot, ids >> RAW_BITS, -1)
        hit = owner_row == owner
        hit_f = jnp.where(hit, 1.0, 0.0)
        seen = dot(hit_f.astype(bf16), before) + base
        base = base + jnp.sum(hit_f, axis=1, keepdims=True)
        rank = jnp.sum(hit_f * seen, axis=0, keepdims=True).astype(i32)
        raw = ids & ((1 << RAW_BITS) - 1)
        planes = jnp.concatenate(
            [
                hit_f * (raw >> 7).astype(f32),
                hit_f * (raw & 127).astype(f32),
                hit_f * sample1,
            ],
            axis=0,
        ).astype(bf16)
        total = total + dot_last(planes, one_hot(rank_row == rank))
    hot = base > float(CAP)
    high, low, samp = total[:OWNERS], total[OWNERS : 2 * OWNERS], total[2 * OWNERS :]
    cold = jnp.where(hot, 0.0, 1.0)
    warm = 1.0 - cold
    raw_all = high * 128.0 + low
    req_ref[...] = ((samp * cold)[:, :CAP].astype(i32) << 16) + (raw_all * cold)[:, :CAP].astype(
        i32
    )
    hot_samp = jnp.sum(samp * warm, axis=0, keepdims=True).astype(i32)
    hot_raw = jnp.sum(raw_all * warm, axis=0, keepdims=True).astype(i32)
    index = jnp.sum(warm * iota((OWNERS, 1), 0).astype(f32), axis=0, keepdims=True)
    pad = jnp.broadcast_to(index.astype(i32), (1, HOT_LANES - HOT_CAP))
    hot_ref[...] = jnp.concatenate([(hot_samp << 16) + hot_raw, pad], axis=1)


def map_rows(code, map_t):
    lanes = code.shape[1]
    raw = code & 0xFFFF
    spread = one_hot(iota((64, lanes), 0) == (raw >> 7))
    both = dot(map_t, spread)
    wide = both[:128] * 64.0 + both[128:]
    return jnp.sum(
        jnp.where(iota((128, lanes), 0) == (raw & 127), wide, 0.0), axis=0, keepdims=True
    )


def as_column(row):
    return jnp.broadcast_to(row, (128, row.shape[1])).T


def low_one_hot(low):
    lane = iota(low.shape, 1)
    narrow = low.astype(f32).astype(bf16)
    return jnp.concatenate(
        [
            packed_hot(narrow == (lane + 128 * part).astype(f32).astype(bf16))
            for part in range(2)
        ],
        axis=1,
    )


def pick_rows(spread, high, table_pair, pairs):
    found = jnp.zeros((spread.shape[0], 128), f32)
    for pair in range(pairs):
        both = dot(spread, table_pair(pair))
        found = jnp.where(high == 2 * pair, both[:, :128], found)
        found = jnp.where(high == 2 * pair + 1, both[:, 128:], found)
    return found


def gather_kernel(req_ref, map_ref, table_ref, *refs):
    out_ref, spread_ref, high_ref = refs[-3:]
    map_t = map_ref[...]
    chunks = req_ref.shape[0]

    @pl.loop(0, chunks // 4)
    def _(group):
        for part in range(4):
            chunk = group * 4 + part
            code = req_ref[pl.ds(chunk, 1), :]
            row = jnp.where(code >= 65536, map_rows(code, map_t), -1.0)
            column = as_column(row).astype(i32)
            place = pl.ds(pl.multiple_of(chunk * 128, 128), 128)
            spread_ref[place, :] = low_one_hot(column & 255)
            high_ref[place, :] = column >> 8

    block = 512

    @pl.loop(0, out_ref.shape[0] // block)
    def _(step):
        place = pl.ds(pl.multiple_of(step * block, block), block)

        def table_pair(pair):
            return jnp.concatenate(
                [
                    table_ref[pair * 512 : pair * 512 + 256, :],
                    table_ref[pair * 512 + 256 : pair * 512 + 512, :],
                ],
                axis=1,
            )

        out_ref[place, :] = pick_rows(
            spread_ref[place, :], high_ref[place, :], table_pair, 8
        ).astype(bf16)


def gather_call(asked, map_t, table, half, before):
    chunks = asked.shape[0] // 2
    rows = chunks * 128
    operands = [asked, map_t, table]
    specs = [
        pl.BlockSpec((chunks, 128), lambda i: (half, 0)),
        whole_spec(*map_t.shape),
        whole_spec(*table.shape),
    ]
    aliases = {}
    if before is not None:
        operands.append(before)
        specs.append(pl.BlockSpec(memory_space=pl.ANY))
        aliases = {3: 0}
    return pl.pallas_call(
        gather_kernel,
        grid=(1,),
        out_shape=jax.ShapeDtypeStruct((2 * rows, 128), bf16),
        in_specs=specs,
        out_specs=pl.BlockSpec((rows, 128), lambda i: (half, 0)),
        scratch_shapes=[pltpu.VMEM((rows, 256), bf16), pltpu.VMEM((rows, 128), i32)],
        input_output_aliases=aliases,
        cost_estimate=cost(5e9),
        compiler_params=params(16),
    )(*operands)


def map_kernel(hot_ref, asked_ref, low_ref, high_ref, map_ref, after_ref, row_ref, samp_ref, code_ref):
    map_t = map_ref[...]
    blocks = asked_ref.shape[0]
    is_hot = hot_ref[0] == 1
    code_ref[0:blocks, :] = asked_ref[...]

    @pl.when(is_hot)
    def _():
        for chunk in range(3):
            all_ref = low_ref if chunk < 2 else high_ref
            even = all_ref[pl.ds(0, blocks, stride=16), :]
            odd = all_ref[pl.ds(8, blocks, stride=16), :]
            lanes = slice(chunk % 2 * 64, chunk % 2 * 64 + 64)
            code_ref[chunk * blocks : (chunk + 1) * blocks, :] = jnp.concatenate(
                [even[:, lanes], odd[:, lanes]], axis=1
            )

    @pl.loop(0, jnp.where(is_hot, 3 * blocks // 8, blocks // 8))
    def _(group):
        place = pl.ds(pl.multiple_of(group * 8, 8), 8)
        code = code_ref[place, :]
        samp_ref[place, :] = (code >> 16) - 1
        for half in range(2):
            wide = jnp.concatenate(
                [code[half * 4 + part : half * 4 + part + 1, :] for part in range(4)], axis=1
            )
            row = map_rows(wide, map_t).astype(i32)
            for part in range(4):
                row_ref[pl.ds(group * 8 + half * 4 + part, 1), :] = row[
                    :, part * 128 : part * 128 + 128
                ]


def pool_kernel(place_ref, req_ref, hot_ref, rows_ref, own_ref, sib_ref, len_ref, out_ref):
    samples = out_ref.shape[0]
    sample_col = iota((samples, 128), 0)
    summed = jnp.zeros((samples, 128), f32)
    for pair in range(req_ref.shape[0] // 2):
        parts = [
            one_hot(sample_col == (req_ref[2 * pair + half : 2 * pair + half + 1, :] >> 16) - 1)
            for half in range(2)
        ]
        summed = summed + dot(
            jnp.concatenate(parts, axis=1), rows_ref[pair * 256 : pair * 256 + 256, :]
        )
    across, core = place_ref[1], place_ref[2]

    def piece(index, start, size):
        half, slot = index // 4, (across - index % 4) & 3
        own = own_ref[slot, start : start + size, :].astype(f32)
        sib = sib_ref[slot, start : start + size, :].astype(f32)
        return jnp.where(core == half, own, sib)

    planes = [
        jnp.concatenate([piece(4 * plane + part, 512, 16) for part in range(4)], axis=0).T
        for plane in range(2)
    ]
    map_t = jnp.concatenate(planes, axis=0).astype(bf16)
    code = jnp.where(iota((1, HOT_LANES), 1) < HOT_CAP, hot_ref[...], 0)
    row = jnp.where(code >= 65536, map_rows(code, map_t), -1.0)
    column = as_column(row).astype(i32)

    def table_pair(pair):
        return jnp.concatenate(
            [piece(pair, 0, 256), piece(pair, 256, 256)], axis=1
        ).astype(bf16)

    hot_rows = pick_rows(low_one_hot(column & 255), column >> 8, table_pair, 8).astype(bf16)
    spread = one_hot(iota((samples, HOT_LANES), 0) == (code >> 16) - 1)
    summed = summed + dot(spread, hot_rows)
    out_ref[...] = (summed / len_ref[...].astype(f32)).astype(bf16)


def scatter_block(chunks, level, shifts, across, offset, row_ref, samp_ref, own_ref, sib_ref,
                  out_ref, wide_ref, spread_ref):
    lane = iota((128, 128), 1).astype(f32).astype(bf16)
    sub = iota((128, 128), 0).astype(f32).astype(bf16)
    span = 128 * chunks
    for order, shift in enumerate(shifts):
        block = level + ((across - shift) & 3)
        highs, picks = [], []
        for chunk in range(chunks):
            line = pl.ds(chunk * 32 + block, 1)
            row, samp = row_ref[line, :], samp_ref[line, :]
            samp = as_column(jnp.where(samp < 0, -1, samp + offset).astype(f32))
            low = row & (LOW_ROWS - 1)
            start = order * span + chunk * 128
            place = slice(start, start + 128)
            highs.append(as_column((row >> LOW_BITS).astype(f32)).astype(bf16))
            picks.append(
                jnp.concatenate(
                    [packed_hot((samp - 128.0 * part).astype(bf16) == lane) for part in range(4)],
                    axis=1,
                )
            )
            for part in range(LOW_ROWS // 128):
                shifted = (low - 128 * part).astype(f32)
                shifted = jnp.broadcast_to(shifted, (128, 128)).astype(bf16)
                spread_ref[part * 128 : part * 128 + 128, place] = packed_hot(shifted == sub)
        picked = jnp.concatenate(picks, axis=0) if chunks > 1 else picks[0]
        source = jnp.concatenate([own_ref[order], sib_ref[order]], axis=0)
        slots = dot(picked, source).astype(bf16)
        for chunk in range(chunks):
            start = order * span + chunk * 128
            part = slots[chunk * 128 : chunk * 128 + 128, :]
            for high in range(HIGHS):
                wide_ref[start : start + 128, high * 128 : high * 128 + 128] = jnp.where(
                    highs[chunk] == jnp.asarray(high, bf16), part, jnp.zeros((), bf16)
                )
    used = len(shifts) * span
    for pair in range(HIGHS // 2):
        both = dot(spread_ref[:, :used], wide_ref[:used, pair * 256 : pair * 256 + 256])
        start = 2 * pair * LOW_ROWS
        out_ref[start : start + LOW_ROWS, :] += both[:, :128]
        out_ref[start + LOW_ROWS : start + 2 * LOW_ROWS, :] += both[:, 128:]


def scatter_kernel(steps, place_ref, row_ref, samp_ref, *refs):
    count = len(steps)
    grads = refs[: 2 * count]
    if len(refs) == 2 * count + 3:
        out_ref, wide_ref, spread_ref = refs[2 * count :]
        out_ref[...] = jnp.zeros_like(out_ref)
    else:
        seen_ref, out_ref, wide_ref, spread_ref = refs[2 * count :]
        out_ref[...] = seen_ref[...]
    depth, across, core, chunks = place_ref[0], place_ref[1], place_ref[2], place_ref[3]
    offset = jnp.where(iota((1, 128), 1) < 64, core * 256, (1 - core) * 256)

    def every(count_chunks):
        for index, (step, shifts) in enumerate(steps):
            level = ((depth - step) & 7) * 4
            scatter_block(
                count_chunks, level, shifts, across, offset, row_ref, samp_ref,
                grads[2 * index], grads[2 * index + 1], out_ref, wide_ref, spread_ref,
            )

    @pl.when(chunks == 1)
    def _():
        every(1)

    @pl.when(chunks != 1)
    def _():
        every(3)


def scatter_call(steps, place, rows, samps, grads, seen, last=False):
    operands = [place, rows, samps, *grads]
    if seen is not None:
        operands.append(near_core(seen))
    return pl.pallas_call(
        functools.partial(scatter_kernel, steps),
        out_shape=(pltpu.HBM if last else pltpu.VMEM)((4096, 128), f32),
        in_specs=[SMEM] + [VMEM] * (len(operands) - 1),
        out_specs=VMEM,
        scratch_shapes=[
            pltpu.VMEM((1536, HIGHS * 128), bf16),
            pltpu.VMEM((LOW_ROWS, 1536), bf16),
        ],
        cost_estimate=cost(4e9 * len(steps)),
        compiler_params=params(16),
    )(*operands)


def feature_halves(task, core, felt_ref):
    first = (task - 2 * core) & 3
    own = jnp.concatenate([felt_ref[first], felt_ref[(first - 1) & 3]], axis=1)
    sib = jnp.concatenate([felt_ref[(first - 2) & 3], felt_ref[(first - 3) & 3]], axis=1)
    return own, sib


def activate(value, slope_ref):
    sig = sigmoid(value)
    out = value * sig
    slope_ref[...] = (sig + out * (1.0 - sig)).astype(bf16)
    return out.astype(bf16)


def mix_column(mix, index):
    return jnp.sum(jnp.where(iota(mix.shape, 1) == index, mix, 0.0), axis=1, keepdims=True)


def forward_kernel(place_ref, felt_ref, shared_own, shared_sib, tower_ref, gate_ref, sent_one,
                   sent_two, sent_three, partial_ref, proj_ref, mix_ref, shared_slope, acc_ref):
    step = pl.program_id(0)
    task, core = place_ref[0], place_ref[1]
    own, sib = feature_halves(task, core, felt_ref)

    @pl.when(step == 0)
    def _():
        acc_ref[...] = jnp.zeros_like(acc_ref)
        scores = dot(own, gate_ref[pl.ds(pl.multiple_of(core * 256, 256), 256), :]) + dot(
            sib, gate_ref[pl.ds(pl.multiple_of(256 - core * 256, 256), 256), :]
        )
        lane = iota(scores.shape, 1)
        raised = jnp.where(lane % 8 < 5, jnp.exp(scores), 0.0)
        bottom = jnp.ones_like(raised)
        for other in range(4):
            group = lane // 8 == other
            whole = jnp.sum(jnp.where(group, raised, 0.0), axis=1, keepdims=True)
            bottom = jnp.where(group, whole, bottom)
        mix_ref[...] = raised / bottom

    shared_out = activate(dot(own, shared_own[...]) + dot(sib, shared_sib[...]), shared_slope)
    for other in range(4):
        acc_ref[other] += dot(shared_out, tower_ref[other])

    @pl.when(step == pl.num_programs(0) - 1)
    def _():
        mix = mix_ref[...]
        proj_ref[...] = acc_ref[...]
        for shift in range(4):
            other = (task + shift) & 3
            part = mix_column(mix, other * 8 + 1 + task) * acc_ref[other]
            if shift == 0:
                partial_ref[...] = part
            else:
                (sent_one, sent_two, sent_three)[shift - 1][...] = part.astype(bf16)


def forward_spec_kernel(place_ref, felt_ref, spec_own, spec_sib, tower_ref, mix_ref, part_ref,
                        proj_ref, spec_slope, acc_ref):
    step = pl.program_id(0)
    task, core = place_ref[0], place_ref[1]
    own, sib = feature_halves(task, core, felt_ref)

    @pl.when(step == 0)
    def _():
        acc_ref[...] = jnp.zeros_like(acc_ref)

    spec_out = activate(dot(own, spec_own[...]) + dot(sib, spec_sib[...]), spec_slope)
    acc_ref[...] += dot(spec_out, tower_ref[0])

    @pl.when(step == pl.num_programs(0) - 1)
    def _():
        proj_ref[...] = acc_ref[...]
        part_ref[...] = mix_column(mix_ref[...], task * 8) * acc_ref[...]


def middle_kernel(partial_ref, spec_ref, one_ref, two_ref, three_ref, head_ref, label_ref, logit_ref,
                  pre_ref, balance_ref):
    value = (partial_ref[...] + spec_ref[...]) + (
        one_ref[...].astype(f32) + two_ref[...].astype(f32) + three_ref[...].astype(f32)
    )
    head = head_ref[...].astype(f32)
    sig = sigmoid(value)
    logit = jnp.sum(value * sig * head, axis=1, keepdims=True)
    logit_ref[...] = logit
    grad = loss_scale * (sigmoid(logit) - label_ref[...].astype(f32))
    pre = (grad * head * (sig * (1.0 + value * (1.0 - sig)))).astype(bf16)
    pre_ref[...] = pre
    balance_ref[...] = jnp.sum(pre.astype(f32) * value, axis=1, keepdims=True)


def backward_spec_kernel(place_ref, pre_ref, proj_ref, mix_ref, balance_ref, spec_own, spec_sib,
                         tower_ref, spec_slope, field_ref, score_ref, scaled_ref):
    step = pl.program_id(0)
    task = place_ref[0]

    @pl.when(step == 0)
    def _():
        field_ref[...] = jnp.zeros_like(field_ref)
        mix = mix_ref[...]
        lane = iota(mix.shape, 1)
        scaled = mix_column(mix, task * 8) * pre_ref[...].astype(f32)
        scaled_ref[...] = scaled.astype(bf16)
        gained = jnp.sum(scaled * proj_ref[...], axis=1, keepdims=True)
        score = jnp.where(lane // 8 == task, -mix * balance_ref[...], 0.0)
        score_ref[...] = score + jnp.where(lane == task * 8, gained, 0.0)

    back = dot_last(scaled_ref[...], tower_ref[0])
    inner = (back * spec_slope[...].astype(f32)).astype(bf16)
    field_ref[0] += dot_last(inner, spec_own[...])
    field_ref[1] += dot_last(inner, spec_sib[...])


def backward_kernel(place_ref, pre_own, pre_one, pre_two, pre_three, proj_ref, mix_ref,
                    gate_ref, start_ref, before_ref, shared_own, shared_sib, tower_ref,
                    shared_slope, sent_one, sent_two, sent_three, field_ref, scaled_ref, score_ref,
                    acc_ref):
    step = pl.program_id(0)
    task, core = place_ref[0], place_ref[1]

    @pl.when(step == 0)
    def _():
        acc_ref[...] = start_ref[...]
        mix = mix_ref[...]
        lane = iota(mix.shape, 1)
        score = before_ref[...]
        for shift, pre_ref in enumerate((pre_own, pre_one, pre_two, pre_three)):
            other = (task - shift) & 3
            index = other * 8 + 1 + task
            scaled = mix_column(mix, index) * pre_ref[...].astype(f32)
            scaled_ref[shift] = scaled.astype(bf16)
            gained = jnp.sum(scaled * proj_ref[other], axis=1, keepdims=True)
            score = score + jnp.where(lane == index, gained, 0.0)
        score_ref[...] = score

    shared_back = dot_last(scaled_ref[0], tower_ref[task])
    for shift in (1, 2, 3):
        shared_back = shared_back + dot_last(scaled_ref[shift], tower_ref[(task - shift) & 3])
    shared_inner = (shared_back * shared_slope[...].astype(f32)).astype(bf16)
    acc_ref[0] += dot_last(shared_inner, shared_own[...])
    acc_ref[1] += dot_last(shared_inner, shared_sib[...])

    @pl.when(step == pl.num_programs(0) - 1)
    def _():
        score = score_ref[...]
        parts = []
        for _ in range(3):
            parts.append(score.astype(bf16))
            score = score - parts[-1].astype(f32)
        for rel in range(2):
            half = core if rel == 0 else 1 - core
            gate = gate_ref[pl.ds(pl.multiple_of(half * 256, 256), 256), :]
            total = acc_ref[rel] + dot_last(parts[2], gate)
            total = total + dot_last(parts[1], gate) + dot_last(parts[0], gate)
            for side in range(2):
                block = total[:, side * 128 : side * 128 + 128]
                slot = (2 * half + side - task) & 3

                @pl.when(slot == 0)
                def _():
                    field_ref[...] = block

                for order, sent_ref in enumerate((sent_one, sent_two, sent_three)):

                    @pl.when(slot == order + 1)
                    def _():
                        sent_ref[...] = block.astype(bf16)


def tower_spec(tile):
    return pl.BlockSpec((1, tile, 256), lambda i, place: (place[0], i, 0))


def prefetched(spec):
    index = spec.index_map
    return pl.BlockSpec(spec.block_shape, lambda i, place: index(i))


def dense_specs(tile):
    weight = pl.BlockSpec((256, tile), lambda i: (0, i))
    tower = pl.BlockSpec((4, tile, 256), lambda i: (0, i, 0))
    return weight, tower


def whole_spec(*shape):
    return pl.BlockSpec(shape, lambda i: (0,) * len(shape))


def ring(size, shift):
    return [(i, (i + shift) % size) for i in range(size)]


def along_task(value, shift):
    return lax.ppermute(value, "task", ring(4, shift))


def across_core(value):
    return lax.ppermute(value, "fsdp", [(0, 1), (1, 0)])


def along_x(value, shift):
    return lax.ppermute(
        value, "table", [(z * 4 + x, z * 4 + (x + shift) % 4) for z in range(8) for x in range(4)]
    )


def along_z(value, shift):
    return lax.ppermute(
        value,
        "table",
        [(z * 4 + x, (z + shift) % 8 * 4 + x) for z in range(8) for x in range(4)],
    )


def at(stack, index):
    return lax.dynamic_index_in_dim(stack, index, 0, keepdims=False)


def local(
    raw_ids,
    bag_len,
    labels,
    emb_table,
    bucket_map,
    spec_weight,
    shared_weight,
    gate_weight,
    tower_weight,
    head_vector,
):
    task = lax.axis_index("task")
    core = lax.axis_index("fsdp")
    table_index = lax.axis_index("table")
    depth, across = table_index // 4, table_index % 4
    me = table_index * 2 + core
    samples = raw_ids.shape[0]
    lookups = OWNERS * CAP

    tower_all = lax.all_gather(tower_weight[0], ("task", "fsdp"), axis=0, tiled=True)
    tower_all = tower_all.reshape(4, 4096, 256)
    spec_sib = across_core(spec_weight[0])
    shared_sib = across_core(shared_weight[0])

    ids_t = raw_ids[:, 0, :].T
    req, hot_row = pl.pallas_call(
        bucket_kernel,
        out_shape=(
            jax.ShapeDtypeStruct((OWNERS, CAP), i32),
            jax.ShapeDtypeStruct((1, HOT_LANES), i32),
        ),
        in_specs=[VMEM] * 2,
        out_specs=(VMEM, VMEM),
        compiler_params=params(16),
    )(ids_t, bag_len.reshape(1, samples))
    hot_index = hot_row[0, HOT_CAP]
    hot_z, hot_x, hot_c = hot_index // 8, hot_index // 2 % 4, hot_index % 2
    away_z, away_x = (depth - hot_z) % 8, (across - hot_x) % 4

    row_map = bucket_map[0].reshape(64, 128)
    planes = jnp.concatenate([row_map >> 6, row_map & 63], axis=0).astype(bf16)
    map_t = jnp.concatenate([(row_map >> 6).T, (row_map & 63).T], axis=0).astype(bf16)
    shard_rows = emb_table[0]

    pieces = jnp.concatenate(
        [shard_rows.reshape(8, 512, 128), planes.reshape(8, 16, 128)], axis=1
    ).reshape(2, 4, PIECE_ROWS, 128)
    half = jnp.where(hot_c == core, at(pieces, core), across_core(at(pieces, 1 - core)))

    asked = lax.all_to_all(req, ("table", "fsdp"), split_axis=0, concat_axis=0, tiled=True)
    asked = asked.reshape(lookups // 128, 128)

    quarters = [at(half, across)] + [
        along_x(at(half, (across + shift) % 4), shift) for shift in (1, 2, 3)
    ]
    part = lax.select_n(away_x, *quarters)
    part, asked = lax.optimization_barrier((part, asked))
    part = lax.select_n(
        jnp.where(away_z == 1, 1, jnp.where(away_z == 7, 2, 0)),
        part,
        along_z(part, 1),
        along_z(part, 7),
    )

    fetched = gather_call(asked, map_t, shard_rows, 0, None)
    fetched, part = lax.optimization_barrier((fetched, part))
    part = lax.select_n(
        jnp.where((away_z >= 2) & (away_z <= 4), 1, jnp.where((away_z == 5) | (away_z == 6), 2, 0)),
        part,
        along_z(part, 3),
        along_z(part, 5),
    )
    fetched = gather_call(asked, map_t, shard_rows, 1, fetched)
    fetched, part = lax.optimization_barrier((fetched, part))
    hot_own = jnp.stack([part] + [along_x(part, shift) for shift in (1, 2, 3)])
    returned = lax.all_to_all(
        fetched.reshape(OWNERS, CAP, 128),
        ("table", "fsdp"),
        split_axis=0,
        concat_axis=0,
        tiled=True,
    )
    gate_cat = jnp.pad(gate_weight, ((0, 0), (0, 0), (0, 3))).transpose(1, 0, 2)
    gate_cat = jnp.pad(gate_cat.reshape(512, 32), ((0, 0), (0, 96)))
    req_wide = req.reshape(lookups // 128, 128)
    returned, hot_own, gate_cat, req_wide = lax.optimization_barrier(
        (returned, hot_own, gate_cat, req_wide)
    )
    returned = returned.reshape(lookups, 128)
    hot_sib = across_core(hot_own)

    place = jnp.stack([depth, across, core]).astype(i32)
    pooled = pl.pallas_call(
        pool_kernel,
        out_shape=jax.ShapeDtypeStruct((samples, 128), bf16),
        in_specs=[SMEM] + [VMEM] * 6,
        out_specs=VMEM,
        compiler_params=params(16),
    )(place, req_wide, hot_row, returned, hot_own, hot_sib, bag_len)

    hot_wide = jnp.pad(hot_row, ((0, 7), (0, 512 - HOT_LANES)))
    hot_all = lax.all_gather(hot_wide, ("table", "fsdp"), axis=0, tiled=True)
    is_hot = hot_index == me
    felt = jnp.stack([pooled] + [along_task(pooled, shift) for shift in (1, 2, 3)])
    dense_place = jnp.stack([task, core]).astype(i32)
    weight, tower = dense_specs(TILE)
    wide = spec_weight.shape[2]
    grid = (wide // TILE,)
    spec_pair = [hbm(spec_weight[0]), hbm(spec_sib)]
    shared_pair = [hbm(shared_weight[0]), hbm(shared_sib)]
    towers, felt, gate_cat = hbm(tower_all), hbm(felt), hbm(gate_cat)
    flat = pltpu.HBM((samples, 256), f32)
    flat_spec = whole_spec(samples, 256)
    mix_spec = whole_spec(samples, 128)
    *sent, partial, proj, mix, shared_slope = pl.pallas_call(
        forward_kernel,
        grid=grid,
        out_shape=(
            *[pltpu.HBM((samples, 256), bf16)] * 3,
            flat,
            pltpu.HBM((4, samples, 256), f32),
            pltpu.HBM((samples, 128), f32),
            pltpu.HBM((samples, wide), bf16),
        ),
        in_specs=[SMEM, whole_spec(4, samples, 128), weight, weight, tower, whole_spec(512, 128)],
        out_specs=(
            *[flat_spec] * 4,
            whole_spec(4, samples, 256),
            mix_spec,
            weight,
        ),
        scratch_shapes=[pltpu.VMEM((4, samples, 256), f32)],
        compiler_params=params(28),
    )(dense_place, felt, *shared_pair, towers, gate_cat)
    received = [along_task(sent[shift - 1], shift) for shift in (1, 2, 3)]
    spec_part, spec_proj, spec_slope = pl.pallas_call(
        forward_spec_kernel,
        grid_spec=pltpu.PrefetchScalarGridSpec(
            num_scalar_prefetch=1,
            grid=grid,
            in_specs=[
                prefetched(spec)
                for spec in (whole_spec(4, samples, 128), weight, weight)
            ]
            + [tower_spec(TILE), prefetched(mix_spec)],
            out_specs=[prefetched(spec) for spec in (flat_spec, flat_spec, weight)],
            scratch_shapes=[pltpu.VMEM((samples, 256), f32)],
        ),
        out_shape=(flat, flat, pltpu.HBM((samples, wide), bf16)),
        cost_estimate=cost(2e9),
        compiler_params=params(28),
    )(dense_place, felt, *spec_pair, towers, hbm(mix))
    logit_own, pre_grad, balance = pl.pallas_call(
        middle_kernel,
        out_shape=(
            pltpu.HBM((samples, 1), f32),
            pltpu.HBM((samples, 256), bf16),
            pltpu.HBM((samples, 1), f32),
        ),
        in_specs=[VMEM] * 7,
        out_specs=(VMEM,) * 3,
        compiler_params=params(16),
    )(hbm(partial), hbm(spec_part), *received, head_vector, labels)
    others = [along_task(pre_grad, shift) for shift in (1, 2, 3)]
    start, score = pl.pallas_call(
        backward_spec_kernel,
        grid_spec=pltpu.PrefetchScalarGridSpec(
            num_scalar_prefetch=1,
            grid=grid,
            in_specs=[
                prefetched(spec)
                for spec in (
                    flat_spec, flat_spec, mix_spec, whole_spec(samples, 1), weight, weight,
                )
            ]
            + [tower_spec(TILE), prefetched(weight)],
            out_specs=[prefetched(spec) for spec in (whole_spec(2, samples, 256), mix_spec)],
            scratch_shapes=[pltpu.VMEM((samples, 256), bf16)],
        ),
        out_shape=(pltpu.HBM((2, samples, 256), f32), pltpu.HBM((samples, 128), f32)),
        cost_estimate=cost(2e9),
        compiler_params=params(28),
    )(dense_place, hbm(pre_grad), hbm(spec_proj), hbm(mix), hbm(balance), *spec_pair, towers,
      hbm(spec_slope))
    *sent_blocks, field_grad = pl.pallas_call(
        backward_kernel,
        grid=grid,
        out_shape=(
            *[pltpu.HBM((samples, 128), bf16)] * 3,
            pltpu.HBM((samples, 128), f32),
        ),
        in_specs=[SMEM]
        + [flat_spec] * 4
        + [
            whole_spec(4, samples, 256),
            mix_spec,
            whole_spec(512, 128),
            whole_spec(2, samples, 256),
            mix_spec,
        ]
        + [weight, weight, tower, weight],
        out_specs=(mix_spec,) * 4,
        scratch_shapes=[
            pltpu.VMEM((4, samples, 256), bf16),
            pltpu.VMEM((samples, 128), f32),
            pltpu.VMEM((2, samples, 256), f32),
        ],
        compiler_params=params(28),
    )(dense_place, hbm(pre_grad), *others, hbm(proj), hbm(mix), gate_cat, hbm(start), hbm(score),
      *shared_pair, towers, hbm(shared_slope))
    rows, samps = pl.pallas_call(
        map_kernel,
        grid=(1,),
        out_shape=(jax.ShapeDtypeStruct((96, 128), i32),) * 2,
        in_specs=[
            SMEM,
            whole_spec(*asked.shape),
            pl.BlockSpec((8 * OWNERS, 128), lambda i: (0, 0)),
            pl.BlockSpec((8 * OWNERS, 128), lambda i: (0, 1)),
            whole_spec(*map_t.shape),
            pl.BlockSpec(memory_space=pl.ANY),
        ],
        out_specs=(whole_spec(96, 128),) * 2,
        scratch_shapes=[pltpu.VMEM((96, 128), i32)],
        cost_estimate=cost(4e9),
        compiler_params=params(16),
    )(is_hot.astype(i32).reshape(1), asked, hbm(hot_all), hbm(hot_all), map_t, hbm(field_grad))
    blocks = [along_task(sent_blocks[shift - 1], shift).astype(f32) for shift in (1, 2, 3)]
    field_grad = field_grad + (blocks[0] + blocks[1] + blocks[2])
    lookup_grad = (field_grad / bag_len.astype(f32)).astype(bf16)
    lookup_grad, rows, samps = lax.optimization_barrier((lookup_grad, rows, samps))

    place4 = jnp.stack([depth, across, core, jnp.where(is_hot, 3, 1)]).astype(i32)
    near = jnp.stack([lookup_grad] + [along_x(lookup_grad, shift) for shift in (1, 2, 3)])
    near_sib = across_core(near)
    table_grad = None
    up, down = near, near
    every = (0, 1, 2, 3)
    steps, ready = ((0, every),), [near, near_sib]
    for step in (1, 2, 3):
        up, down = along_z(up, 1), along_z(down, 7)
        table_grad = scatter_call(steps, place4, rows, samps, ready, table_grad)
        table_grad, up, down = lax.optimization_barrier((table_grad, up, down))
        steps = ((step, every), (-step, every))
        ready = [up, across_core(up), down, across_core(down)]
    far = [along_z(up[:2], 1), along_z(down[2:], 7)]
    table_grad = scatter_call(steps, place4, rows, samps, ready, table_grad)
    table_grad, *far = lax.optimization_barrier((table_grad, *far))
    table_grad = scatter_call(
        ((4, (0, 1)), (4, (2, 3))),
        place4,
        rows,
        samps,
        [far[0], across_core(far[0]), far[1], across_core(far[1])],
        table_grad,
        last=True,
    )
    return (logit_own, table_grad[None])


def solution(mesh):
    return jax.shard_map(
        local,
        mesh=mesh,
        in_specs=(
            P(("table", "fsdp"), "task", None),
            P(("table", "fsdp"), "task"),
            P(("table", "fsdp"), "task"),
            P("task", ("table", "fsdp"), None),
            P("task", ("table", "fsdp")),
            P("task", "fsdp", None),
            P("task", "fsdp", None),
            P(),
            P("task", "fsdp", None),
            P("task", None),
        ),
        out_specs=(P(("table", "fsdp"), "task"), P("task", ("table", "fsdp"), None)),
        check_vma=False,
    )
```

```python
import functools

import jax
import jax.numpy as jnp
from jax import lax
from jax.experimental import pallas as pl
from jax.experimental.pallas import tpu as pltpu
from jax.sharding import PartitionSpec as P

loss_scale = 1024.0
highest = lax.Precision.HIGHEST
contract_last = (((1,), (1,)), ((), ()))
bf16 = jnp.bfloat16
f32 = jnp.float32
i32 = jnp.int32
OWNERS = 64
CAP = 64
HOT_CAP = 192
HOT_LANES = 256
RAW_BITS = 13
PIECE_ROWS = 528
HIGHS = 8
LOW_ROWS = 512
LOW_BITS = 9
TILE = 1024
VMEM = pl.BlockSpec(memory_space=pltpu.VMEM)
SMEM = pl.BlockSpec(memory_space=pltpu.SMEM)


def params(mib):
    return pltpu.CompilerParams(vmem_limit_bytes=mib * 1024 * 1024)


def sigmoid(value):
    return 0.5 * jnp.tanh(0.5 * value) + 0.5


def hbm(value):
    return pltpu.with_memory_space_constraint(value, pltpu.HBM)


def near_core(value):
    return pltpu.with_memory_space_constraint(value, pltpu.VMEM)


def cost(flops):
    return pl.CostEstimate(flops=int(flops), bytes_accessed=4194304, transcendentals=0)


def iota(shape, dim):
    return lax.broadcasted_iota(i32, shape, dim)


def dot(left, right):
    return jnp.dot(left, right, preferred_element_type=f32)


def dot_last(left, right):
    return lax.dot_general(left, right, contract_last, preferred_element_type=f32)


def one_hot(mask):
    return jnp.where(mask, 1.0, 0.0).astype(bf16)


def packed_hot(mask):
    return jnp.where(mask, jnp.ones((), bf16), jnp.zeros((), bf16))


def bucket_kernel(ids_ref, len_ref, req_ref, hot_ref):
    slots, samples = ids_ref.shape
    owner_row = iota((OWNERS, samples), 0)
    sample1 = (iota((1, samples), 1) + 1).astype(f32)
    before = one_hot(iota((samples, samples), 0) < iota((samples, samples), 1))
    rank_row = iota((HOT_CAP, samples), 0)
    lens = len_ref[...]
    base = jnp.zeros((OWNERS, 1), f32)
    total = jnp.zeros((3 * OWNERS, HOT_CAP), f32)
    for slot in range(slots):
        ids = ids_ref[slot : slot + 1, :]
        owner = jnp.where(lens > slot, ids >> RAW_BITS, -1)
        hit = owner_row == owner
        hit_f = jnp.where(hit, 1.0, 0.0)
        seen = dot(hit_f.astype(bf16), before) + base
        base = base + jnp.sum(hit_f, axis=1, keepdims=True)
        rank = jnp.sum(hit_f * seen, axis=0, keepdims=True).astype(i32)
        raw = ids & ((1 << RAW_BITS) - 1)
        planes = jnp.concatenate(
            [
                hit_f * (raw >> 7).astype(f32),
                hit_f * (raw & 127).astype(f32),
                hit_f * sample1,
            ],
            axis=0,
        ).astype(bf16)
        total = total + dot_last(planes, one_hot(rank_row == rank))
    hot = base > float(CAP)
    high, low, samp = total[:OWNERS], total[OWNERS : 2 * OWNERS], total[2 * OWNERS :]
    cold = jnp.where(hot, 0.0, 1.0)
    warm = 1.0 - cold
    raw_all = high * 128.0 + low
    req_ref[...] = ((samp * cold)[:, :CAP].astype(i32) << 16) + (raw_all * cold)[:, :CAP].astype(
        i32
    )
    hot_samp = jnp.sum(samp * warm, axis=0, keepdims=True).astype(i32)
    hot_raw = jnp.sum(raw_all * warm, axis=0, keepdims=True).astype(i32)
    index = jnp.sum(warm * iota((OWNERS, 1), 0).astype(f32), axis=0, keepdims=True)
    pad = jnp.broadcast_to(index.astype(i32), (1, HOT_LANES - HOT_CAP))
    hot_ref[...] = jnp.concatenate([(hot_samp << 16) + hot_raw, pad], axis=1)


def map_rows(code, map_t):
    lanes = code.shape[1]
    raw = code & 0xFFFF
    spread = one_hot(iota((64, lanes), 0) == (raw >> 7))
    both = dot(map_t, spread)
    wide = both[:128] * 64.0 + both[128:]
    return jnp.sum(
        jnp.where(iota((128, lanes), 0) == (raw & 127), wide, 0.0), axis=0, keepdims=True
    )


def as_column(row):
    return jnp.broadcast_to(row, (128, row.shape[1])).T


def low_one_hot(low):
    lane = iota(low.shape, 1)
    narrow = low.astype(f32).astype(bf16)
    return jnp.concatenate(
        [
            packed_hot(narrow == (lane + 128 * part).astype(f32).astype(bf16))
            for part in range(2)
        ],
        axis=1,
    )


def pick_rows(spread, high, table_pair, pairs):
    found = jnp.zeros((spread.shape[0], 128), f32)
    for pair in range(pairs):
        both = dot(spread, table_pair(pair))
        found = jnp.where(high == 2 * pair, both[:, :128], found)
        found = jnp.where(high == 2 * pair + 1, both[:, 128:], found)
    return found


def gather_kernel(req_ref, map_ref, table_ref, out_ref, spread_ref, high_ref):
    map_t = map_ref[...]
    chunks = req_ref.shape[0]

    @pl.loop(0, chunks // 4)
    def _(group):
        for part in range(4):
            chunk = group * 4 + part
            code = req_ref[pl.ds(chunk, 1), :]
            row = jnp.where(code >= 65536, map_rows(code, map_t), -1.0)
            column = as_column(row).astype(i32)
            place = pl.ds(pl.multiple_of(chunk * 128, 128), 128)
            spread_ref[place, :] = low_one_hot(column & 255)
            high_ref[place, :] = column >> 8

    block = 512

    @pl.loop(0, out_ref.shape[0] // block)
    def _(step):
        place = pl.ds(pl.multiple_of(step * block, block), block)

        def table_pair(pair):
            return jnp.concatenate(
                [
                    table_ref[pair * 512 : pair * 512 + 256, :],
                    table_ref[pair * 512 + 256 : pair * 512 + 512, :],
                ],
                axis=1,
            )

        out_ref[place, :] = pick_rows(
            spread_ref[place, :], high_ref[place, :], table_pair, 8
        ).astype(bf16)


def gather_call(asked, map_t, table):
    rows = asked.shape[0] * 128
    return pl.pallas_call(
        gather_kernel,
        out_shape=jax.ShapeDtypeStruct((rows, 128), bf16),
        in_specs=[VMEM] * 3,
        out_specs=VMEM,
        scratch_shapes=[pltpu.VMEM((rows, 256), bf16), pltpu.VMEM((rows, 128), i32)],
        cost_estimate=cost(9e9),
        compiler_params=params(16),
    )(asked, map_t, table)


def map_kernel(hot_ref, asked_ref, low_ref, high_ref, map_ref, after_ref, row_ref, samp_ref, code_ref):
    map_t = map_ref[...]
    blocks = asked_ref.shape[0]
    is_hot = hot_ref[0] == 1
    code_ref[0:blocks, :] = asked_ref[...]

    @pl.when(is_hot)
    def _():
        for chunk in range(3):
            all_ref = low_ref if chunk < 2 else high_ref
            even = all_ref[pl.ds(0, blocks, stride=16), :]
            odd = all_ref[pl.ds(8, blocks, stride=16), :]
            lanes = slice(chunk % 2 * 64, chunk % 2 * 64 + 64)
            code_ref[chunk * blocks : (chunk + 1) * blocks, :] = jnp.concatenate(
                [even[:, lanes], odd[:, lanes]], axis=1
            )

    @pl.loop(0, jnp.where(is_hot, 3 * blocks // 8, blocks // 8))
    def _(group):
        place = pl.ds(pl.multiple_of(group * 8, 8), 8)
        code = code_ref[place, :]
        samp_ref[place, :] = (code >> 16) - 1
        for half in range(2):
            wide = jnp.concatenate(
                [code[half * 4 + part : half * 4 + part + 1, :] for part in range(4)], axis=1
            )
            row = map_rows(wide, map_t).astype(i32)
            for part in range(4):
                row_ref[pl.ds(group * 8 + half * 4 + part, 1), :] = row[
                    :, part * 128 : part * 128 + 128
                ]


def cold_pool_kernel(req_ref, rows_ref, out_ref):
    samples = out_ref.shape[0]
    sample_col = iota((samples, 128), 0)
    summed = jnp.zeros((samples, 128), f32)
    for pair in range(req_ref.shape[0] // 2):
        parts = [
            one_hot(sample_col == (req_ref[2 * pair + half : 2 * pair + half + 1, :] >> 16) - 1)
            for half in range(2)
        ]
        summed = summed + dot(
            jnp.concatenate(parts, axis=1), rows_ref[pair * 256 : pair * 256 + 256, :]
        )
    out_ref[...] = summed


def pool_kernel(place_ref, summed_ref, hot_ref, own_ref, sib_ref, len_ref, out_ref):
    samples = out_ref.shape[0]
    across, core = place_ref[1], place_ref[2]

    def piece(index, start, size):
        half, slot = index // 4, (across - index % 4) & 3
        own = own_ref[slot, start : start + size, :].astype(f32)
        sib = sib_ref[slot, start : start + size, :].astype(f32)
        return jnp.where(core == half, own, sib)

    planes = [
        jnp.concatenate([piece(4 * plane + part, 512, 16) for part in range(4)], axis=0).T
        for plane in range(2)
    ]
    map_t = jnp.concatenate(planes, axis=0).astype(bf16)
    code = jnp.where(iota((1, HOT_LANES), 1) < HOT_CAP, hot_ref[...], 0)
    row = jnp.where(code >= 65536, map_rows(code, map_t), -1.0)
    column = as_column(row).astype(i32)

    def table_pair(pair):
        return jnp.concatenate(
            [piece(pair, 0, 256), piece(pair, 256, 256)], axis=1
        ).astype(bf16)

    hot_rows = pick_rows(low_one_hot(column & 255), column >> 8, table_pair, 8).astype(bf16)
    spread = one_hot(iota((samples, HOT_LANES), 0) == (code >> 16) - 1)
    summed = summed_ref[...] + dot(spread, hot_rows)
    out_ref[...] = (summed / len_ref[...].astype(f32)).astype(bf16)


def scatter_block(chunks, level, shifts, across, offset, row_ref, samp_ref, own_ref, sib_ref,
                  out_ref, wide_ref, spread_ref):
    lane = iota((128, 128), 1).astype(f32).astype(bf16)
    sub = iota((128, 128), 0).astype(f32).astype(bf16)
    span = 128 * chunks
    for order, shift in enumerate(shifts):
        block = level + ((across - shift) & 3)
        highs, picks = [], []
        for chunk in range(chunks):
            line = pl.ds(chunk * 32 + block, 1)
            row, samp = row_ref[line, :], samp_ref[line, :]
            samp = as_column(jnp.where(samp < 0, -1, samp + offset).astype(f32))
            low = row & (LOW_ROWS - 1)
            start = order * span + chunk * 128
            place = slice(start, start + 128)
            highs.append(as_column((row >> LOW_BITS).astype(f32)).astype(bf16))
            picks.append(
                jnp.concatenate(
                    [packed_hot((samp - 128.0 * part).astype(bf16) == lane) for part in range(4)],
                    axis=1,
                )
            )
            for part in range(LOW_ROWS // 128):
                shifted = (low - 128 * part).astype(f32)
                shifted = jnp.broadcast_to(shifted, (128, 128)).astype(bf16)
                spread_ref[part * 128 : part * 128 + 128, place] = packed_hot(shifted == sub)
        picked = jnp.concatenate(picks, axis=0) if chunks > 1 else picks[0]
        source = jnp.concatenate([own_ref[order], sib_ref[order]], axis=0)
        slots = dot(picked, source).astype(bf16)
        for chunk in range(chunks):
            start = order * span + chunk * 128
            part = slots[chunk * 128 : chunk * 128 + 128, :]
            for high in range(HIGHS):
                wide_ref[start : start + 128, high * 128 : high * 128 + 128] = jnp.where(
                    highs[chunk] == jnp.asarray(high, bf16), part, jnp.zeros((), bf16)
                )
    used = len(shifts) * span
    for pair in range(HIGHS // 2):
        both = dot(spread_ref[:, :used], wide_ref[:used, pair * 256 : pair * 256 + 256])
        start = 2 * pair * LOW_ROWS
        out_ref[start : start + LOW_ROWS, :] += both[:, :128]
        out_ref[start + LOW_ROWS : start + 2 * LOW_ROWS, :] += both[:, 128:]


def scatter_kernel(steps, place_ref, row_ref, samp_ref, *refs):
    count = len(steps)
    grads = refs[: 2 * count]
    if len(refs) == 2 * count + 3:
        out_ref, wide_ref, spread_ref = refs[2 * count :]
        out_ref[...] = jnp.zeros_like(out_ref)
    else:
        seen_ref, out_ref, wide_ref, spread_ref = refs[2 * count :]
        out_ref[...] = seen_ref[...]
    depth, across, core, chunks = place_ref[0], place_ref[1], place_ref[2], place_ref[3]
    offset = jnp.where(iota((1, 128), 1) < 64, core * 256, (1 - core) * 256)

    def every(count_chunks):
        for index, (step, shifts) in enumerate(steps):
            level = ((depth - step) & 7) * 4
            scatter_block(
                count_chunks, level, shifts, across, offset, row_ref, samp_ref,
                grads[2 * index], grads[2 * index + 1], out_ref, wide_ref, spread_ref,
            )

    @pl.when(chunks == 1)
    def _():
        every(1)

    @pl.when(chunks != 1)
    def _():
        every(3)


def scatter_call(steps, place, rows, samps, grads, seen, last=False):
    operands = [place, rows, samps, *grads]
    if seen is not None:
        operands.append(near_core(seen))
    return pl.pallas_call(
        functools.partial(scatter_kernel, steps),
        out_shape=(pltpu.HBM if last else pltpu.VMEM)((4096, 128), f32),
        in_specs=[SMEM] + [VMEM] * (len(operands) - 1),
        out_specs=VMEM,
        scratch_shapes=[
            pltpu.VMEM((1536, HIGHS * 128), bf16),
            pltpu.VMEM((LOW_ROWS, 1536), bf16),
        ],
        cost_estimate=cost(4e9 * len(steps)),
        compiler_params=params(16),
    )(*operands)


def feature_halves(task, core, felt_ref):
    first = (task - 2 * core) & 3
    own = jnp.concatenate([felt_ref[first], felt_ref[(first - 1) & 3]], axis=1)
    sib = jnp.concatenate([felt_ref[(first - 2) & 3], felt_ref[(first - 3) & 3]], axis=1)
    return own, sib


def activate(value, slope_ref):
    sig = sigmoid(value)
    out = value * sig
    slope_ref[...] = (sig + out * (1.0 - sig)).astype(bf16)
    return out.astype(bf16)


def mix_column(mix, index):
    return jnp.sum(jnp.where(iota(mix.shape, 1) == index, mix, 0.0), axis=1, keepdims=True)


def forward_kernel(place_ref, felt_ref, shared_own, shared_sib, tower_ref, gate_ref, sent_one,
                   sent_two, sent_three, partial_ref, proj_ref, mix_ref, shared_slope, acc_ref):
    step = pl.program_id(0)
    task, core = place_ref[0], place_ref[1]
    own, sib = feature_halves(task, core, felt_ref)

    @pl.when(step == 0)
    def _():
        acc_ref[...] = jnp.zeros_like(acc_ref)
        scores = dot(own, gate_ref[pl.ds(pl.multiple_of(core * 256, 256), 256), :]) + dot(
            sib, gate_ref[pl.ds(pl.multiple_of(256 - core * 256, 256), 256), :]
        )
        lane = iota(scores.shape, 1)
        raised = jnp.where(lane % 8 < 5, jnp.exp(scores), 0.0)
        bottom = jnp.ones_like(raised)
        for other in range(4):
            group = lane // 8 == other
            whole = jnp.sum(jnp.where(group, raised, 0.0), axis=1, keepdims=True)
            bottom = jnp.where(group, whole, bottom)
        mix_ref[...] = raised / bottom

    shared_out = activate(dot(own, shared_own[...]) + dot(sib, shared_sib[...]), shared_slope)
    for other in range(4):
        acc_ref[other] += dot(shared_out, tower_ref[other])

    @pl.when(step == pl.num_programs(0) - 1)
    def _():
        mix = mix_ref[...]
        proj_ref[...] = acc_ref[...]
        for shift in range(4):
            other = (task + shift) & 3
            part = mix_column(mix, other * 8 + 1 + task) * acc_ref[other]
            if shift == 0:
                partial_ref[...] = part
            else:
                (sent_one, sent_two, sent_three)[shift - 1][...] = part.astype(bf16)


def forward_spec_kernel(place_ref, felt_ref, spec_own, spec_sib, tower_ref, mix_ref, part_ref,
                        proj_ref, spec_slope, acc_ref):
    step = pl.program_id(0)
    task, core = place_ref[0], place_ref[1]
    own, sib = feature_halves(task, core, felt_ref)

    @pl.when(step == 0)
    def _():
        acc_ref[...] = jnp.zeros_like(acc_ref)

    spec_out = activate(dot(own, spec_own[...]) + dot(sib, spec_sib[...]), spec_slope)
    acc_ref[...] += dot(spec_out, tower_ref[0])

    @pl.when(step == pl.num_programs(0) - 1)
    def _():
        proj_ref[...] = acc_ref[...]
        part_ref[...] = mix_column(mix_ref[...], task * 8) * acc_ref[...]


def middle_kernel(partial_ref, spec_ref, one_ref, two_ref, three_ref, head_ref, label_ref, logit_ref,
                  pre_ref, balance_ref):
    value = (partial_ref[...] + spec_ref[...]) + (
        one_ref[...].astype(f32) + two_ref[...].astype(f32) + three_ref[...].astype(f32)
    )
    head = head_ref[...].astype(f32)
    sig = sigmoid(value)
    logit = jnp.sum(value * sig * head, axis=1, keepdims=True)
    logit_ref[...] = logit
    grad = loss_scale * (sigmoid(logit) - label_ref[...].astype(f32))
    pre = (grad * head * (sig * (1.0 + value * (1.0 - sig)))).astype(bf16)
    pre_ref[...] = pre
    balance_ref[...] = jnp.sum(pre.astype(f32) * value, axis=1, keepdims=True)


def backward_spec_kernel(place_ref, pre_ref, proj_ref, mix_ref, balance_ref, spec_own, spec_sib,
                         tower_ref, spec_slope, field_ref, score_ref, scaled_ref):
    step = pl.program_id(0)
    task = place_ref[0]

    @pl.when(step == 0)
    def _():
        field_ref[...] = jnp.zeros_like(field_ref)
        mix = mix_ref[...]
        lane = iota(mix.shape, 1)
        scaled = mix_column(mix, task * 8) * pre_ref[...].astype(f32)
        scaled_ref[...] = scaled.astype(bf16)
        gained = jnp.sum(scaled * proj_ref[...], axis=1, keepdims=True)
        score = jnp.where(lane // 8 == task, -mix * balance_ref[...], 0.0)
        score_ref[...] = score + jnp.where(lane == task * 8, gained, 0.0)

    back = dot_last(scaled_ref[...], tower_ref[0])
    inner = (back * spec_slope[...].astype(f32)).astype(bf16)
    field_ref[0] += dot_last(inner, spec_own[...])
    field_ref[1] += dot_last(inner, spec_sib[...])


def backward_kernel(place_ref, pre_own, pre_one, pre_two, pre_three, proj_ref, mix_ref,
                    gate_ref, start_ref, before_ref, shared_own, shared_sib, tower_ref,
                    shared_slope, sent_one, sent_two, sent_three, field_ref, scaled_ref, score_ref,
                    acc_ref):
    step = pl.program_id(0)
    task, core = place_ref[0], place_ref[1]

    @pl.when(step == 0)
    def _():
        acc_ref[...] = start_ref[...]
        mix = mix_ref[...]
        lane = iota(mix.shape, 1)
        score = before_ref[...]
        for shift, pre_ref in enumerate((pre_own, pre_one, pre_two, pre_three)):
            other = (task - shift) & 3
            index = other * 8 + 1 + task
            scaled = mix_column(mix, index) * pre_ref[...].astype(f32)
            scaled_ref[shift] = scaled.astype(bf16)
            gained = jnp.sum(scaled * proj_ref[other], axis=1, keepdims=True)
            score = score + jnp.where(lane == index, gained, 0.0)
        score_ref[...] = score

    shared_back = dot_last(scaled_ref[0], tower_ref[task])
    for shift in (1, 2, 3):
        shared_back = shared_back + dot_last(scaled_ref[shift], tower_ref[(task - shift) & 3])
    shared_inner = (shared_back * shared_slope[...].astype(f32)).astype(bf16)
    acc_ref[0] += dot_last(shared_inner, shared_own[...])
    acc_ref[1] += dot_last(shared_inner, shared_sib[...])

    @pl.when(step == pl.num_programs(0) - 1)
    def _():
        score = score_ref[...]
        parts = []
        for _ in range(3):
            parts.append(score.astype(bf16))
            score = score - parts[-1].astype(f32)
        for rel in range(2):
            half = core if rel == 0 else 1 - core
            gate = gate_ref[pl.ds(pl.multiple_of(half * 256, 256), 256), :]
            total = acc_ref[rel] + dot_last(parts[2], gate)
            total = total + dot_last(parts[1], gate) + dot_last(parts[0], gate)
            for side in range(2):
                block = total[:, side * 128 : side * 128 + 128]
                slot = (2 * half + side - task) & 3

                @pl.when(slot == 0)
                def _():
                    field_ref[...] = block

                for order, sent_ref in enumerate((sent_one, sent_two, sent_three)):

                    @pl.when(slot == order + 1)
                    def _():
                        sent_ref[...] = block.astype(bf16)


def tower_spec(tile):
    return pl.BlockSpec((1, tile, 256), lambda i, place: (place[0], i, 0))


def prefetched(spec):
    index = spec.index_map
    return pl.BlockSpec(spec.block_shape, lambda i, place: index(i))


def dense_specs(tile):
    weight = pl.BlockSpec((256, tile), lambda i: (0, i))
    tower = pl.BlockSpec((4, tile, 256), lambda i: (0, i, 0))
    return weight, tower


def whole_spec(*shape):
    return pl.BlockSpec(shape, lambda i: (0,) * len(shape))


def ring(size, shift):
    return [(i, (i + shift) % size) for i in range(size)]


def along_task(value, shift):
    return lax.ppermute(value, "task", ring(4, shift))


def across_core(value):
    return lax.ppermute(value, "fsdp", [(0, 1), (1, 0)])


def along_x(value, shift):
    return lax.ppermute(
        value, "table", [(z * 4 + x, z * 4 + (x + shift) % 4) for z in range(8) for x in range(4)]
    )


def along_z(value, shift):
    return lax.ppermute(
        value,
        "table",
        [(z * 4 + x, (z + shift) % 8 * 4 + x) for z in range(8) for x in range(4)],
    )


def at(stack, index):
    return lax.dynamic_index_in_dim(stack, index, 0, keepdims=False)


def local(
    raw_ids,
    bag_len,
    labels,
    emb_table,
    bucket_map,
    spec_weight,
    shared_weight,
    gate_weight,
    tower_weight,
    head_vector,
):
    task = lax.axis_index("task")
    core = lax.axis_index("fsdp")
    table_index = lax.axis_index("table")
    depth, across = table_index // 4, table_index % 4
    me = table_index * 2 + core
    samples = raw_ids.shape[0]
    lookups = OWNERS * CAP

    tower_all = lax.all_gather(tower_weight[0], ("task", "fsdp"), axis=0, tiled=True)
    tower_all = tower_all.reshape(4, 4096, 256)
    spec_sib = across_core(spec_weight[0])
    shared_sib = across_core(shared_weight[0])

    ids_t = raw_ids[:, 0, :].T
    req, hot_row = pl.pallas_call(
        bucket_kernel,
        out_shape=(
            jax.ShapeDtypeStruct((OWNERS, CAP), i32),
            jax.ShapeDtypeStruct((1, HOT_LANES), i32),
        ),
        in_specs=[VMEM] * 2,
        out_specs=(VMEM, VMEM),
        compiler_params=params(16),
    )(ids_t, bag_len.reshape(1, samples))
    hot_index = hot_row[0, HOT_CAP]
    hot_z, hot_x, hot_c = hot_index // 8, hot_index // 2 % 4, hot_index % 2
    away_z, away_x = (depth - hot_z) % 8, (across - hot_x) % 4

    row_map = bucket_map[0].reshape(64, 128)
    planes = jnp.concatenate([row_map >> 6, row_map & 63], axis=0).astype(bf16)
    map_t = jnp.concatenate([(row_map >> 6).T, (row_map & 63).T], axis=0).astype(bf16)
    shard_rows = emb_table[0]

    pieces = jnp.concatenate(
        [shard_rows.reshape(8, 512, 128), planes.reshape(8, 16, 128)], axis=1
    ).reshape(2, 4, PIECE_ROWS, 128)
    half = jnp.where(hot_c == core, at(pieces, core), across_core(at(pieces, 1 - core)))

    asked = lax.all_to_all(req, ("table", "fsdp"), split_axis=0, concat_axis=0, tiled=True)
    asked = asked.reshape(lookups // 128, 128)

    quarters = [at(half, across)] + [
        along_x(at(half, (across + shift) % 4), shift) for shift in (1, 2, 3)
    ]
    part = lax.select_n(away_x, *quarters)
    part = lax.select_n(
        jnp.where(away_z == 1, 1, jnp.where(away_z == 7, 2, 0)),
        part,
        along_z(part, 1),
        along_z(part, 7),
    )

    part, asked = lax.optimization_barrier((part, asked))
    part = lax.select_n(
        jnp.where((away_z >= 2) & (away_z <= 4), 1, jnp.where((away_z == 5) | (away_z == 6), 2, 0)),
        part,
        along_z(part, 3),
        along_z(part, 5),
    )
    fetched = gather_call(asked, map_t, shard_rows)
    fetched, part = lax.optimization_barrier((fetched, part))
    hot_own = jnp.stack([part] + [along_x(part, shift) for shift in (1, 2, 3)])
    returned = lax.all_to_all(
        fetched.reshape(OWNERS, CAP, 128),
        ("table", "fsdp"),
        split_axis=0,
        concat_axis=0,
        tiled=True,
    )
    gate_cat = jnp.pad(gate_weight, ((0, 0), (0, 0), (0, 3))).transpose(1, 0, 2)
    gate_cat = jnp.pad(gate_cat.reshape(512, 32), ((0, 0), (0, 96)))
    req_wide = req.reshape(lookups // 128, 128)
    returned, hot_own, gate_cat, req_wide = lax.optimization_barrier(
        (returned, hot_own, gate_cat, req_wide)
    )
    returned = returned.reshape(lookups, 128)
    hot_sib = across_core(hot_own)

    place = jnp.stack([depth, across, core]).astype(i32)
    summed = pl.pallas_call(
        cold_pool_kernel,
        out_shape=jax.ShapeDtypeStruct((samples, 128), f32),
        in_specs=[VMEM] * 2,
        out_specs=VMEM,
        cost_estimate=cost(1e9),
        compiler_params=params(16),
    )(req_wide, returned)
    pooled = pl.pallas_call(
        pool_kernel,
        out_shape=jax.ShapeDtypeStruct((samples, 128), bf16),
        in_specs=[SMEM] + [VMEM] * 5,
        out_specs=VMEM,
        compiler_params=params(16),
    )(place, summed, hot_row, hot_own, hot_sib, bag_len)

    hot_wide = jnp.pad(hot_row, ((0, 7), (0, 512 - HOT_LANES)))
    hot_all = lax.all_gather(hot_wide, ("table", "fsdp"), axis=0, tiled=True)
    is_hot = hot_index == me
    felt = jnp.stack([pooled] + [along_task(pooled, shift) for shift in (1, 2, 3)])
    dense_place = jnp.stack([task, core]).astype(i32)
    weight, tower = dense_specs(TILE)
    wide = spec_weight.shape[2]
    grid = (wide // TILE,)
    spec_pair = [hbm(spec_weight[0]), hbm(spec_sib)]
    shared_pair = [hbm(shared_weight[0]), hbm(shared_sib)]
    towers, felt, gate_cat = hbm(tower_all), hbm(felt), hbm(gate_cat)
    flat = pltpu.HBM((samples, 256), f32)
    flat_spec = whole_spec(samples, 256)
    mix_spec = whole_spec(samples, 128)
    *sent, partial, proj, mix, shared_slope = pl.pallas_call(
        forward_kernel,
        grid=grid,
        out_shape=(
            *[pltpu.HBM((samples, 256), bf16)] * 3,
            flat,
            pltpu.HBM((4, samples, 256), f32),
            pltpu.HBM((samples, 128), f32),
            pltpu.HBM((samples, wide), bf16),
        ),
        in_specs=[SMEM, whole_spec(4, samples, 128), weight, weight, tower, whole_spec(512, 128)],
        out_specs=(
            *[flat_spec] * 4,
            whole_spec(4, samples, 256),
            mix_spec,
            weight,
        ),
        scratch_shapes=[pltpu.VMEM((4, samples, 256), f32)],
        compiler_params=params(28),
    )(dense_place, felt, *shared_pair, towers, gate_cat)
    received = [along_task(sent[shift - 1], shift) for shift in (1, 2, 3)]
    spec_part, spec_proj, spec_slope = pl.pallas_call(
        forward_spec_kernel,
        grid_spec=pltpu.PrefetchScalarGridSpec(
            num_scalar_prefetch=1,
            grid=grid,
            in_specs=[
                prefetched(spec)
                for spec in (whole_spec(4, samples, 128), weight, weight)
            ]
            + [tower_spec(TILE), prefetched(mix_spec)],
            out_specs=[prefetched(spec) for spec in (flat_spec, flat_spec, weight)],
            scratch_shapes=[pltpu.VMEM((samples, 256), f32)],
        ),
        out_shape=(flat, flat, pltpu.HBM((samples, wide), bf16)),
        cost_estimate=cost(2e9),
        compiler_params=params(28),
    )(dense_place, felt, *spec_pair, towers, hbm(mix))
    logit_own, pre_grad, balance = pl.pallas_call(
        middle_kernel,
        out_shape=(
            pltpu.HBM((samples, 1), f32),
            pltpu.HBM((samples, 256), bf16),
            pltpu.HBM((samples, 1), f32),
        ),
        in_specs=[VMEM] * 7,
        out_specs=(VMEM,) * 3,
        compiler_params=params(16),
    )(hbm(partial), hbm(spec_part), *received, head_vector, labels)
    others = [along_task(pre_grad, shift) for shift in (1, 2, 3)]
    start, score = pl.pallas_call(
        backward_spec_kernel,
        grid_spec=pltpu.PrefetchScalarGridSpec(
            num_scalar_prefetch=1,
            grid=grid,
            in_specs=[
                prefetched(spec)
                for spec in (
                    flat_spec, flat_spec, mix_spec, whole_spec(samples, 1), weight, weight,
                )
            ]
            + [tower_spec(TILE), prefetched(weight)],
            out_specs=[prefetched(spec) for spec in (whole_spec(2, samples, 256), mix_spec)],
            scratch_shapes=[pltpu.VMEM((samples, 256), bf16)],
        ),
        out_shape=(pltpu.HBM((2, samples, 256), f32), pltpu.HBM((samples, 128), f32)),
        cost_estimate=cost(2e9),
        compiler_params=params(28),
    )(dense_place, hbm(pre_grad), hbm(spec_proj), hbm(mix), hbm(balance), *spec_pair, towers,
      hbm(spec_slope))
    *sent_blocks, field_grad = pl.pallas_call(
        backward_kernel,
        grid=grid,
        out_shape=(
            *[pltpu.HBM((samples, 128), bf16)] * 3,
            pltpu.HBM((samples, 128), f32),
        ),
        in_specs=[SMEM]
        + [flat_spec] * 4
        + [
            whole_spec(4, samples, 256),
            mix_spec,
            whole_spec(512, 128),
            whole_spec(2, samples, 256),
            mix_spec,
        ]
        + [weight, weight, tower, weight],
        out_specs=(mix_spec,) * 4,
        scratch_shapes=[
            pltpu.VMEM((4, samples, 256), bf16),
            pltpu.VMEM((samples, 128), f32),
            pltpu.VMEM((2, samples, 256), f32),
        ],
        compiler_params=params(28),
    )(dense_place, hbm(pre_grad), *others, hbm(proj), hbm(mix), gate_cat, hbm(start), hbm(score),
      *shared_pair, towers, hbm(shared_slope))
    rows, samps = pl.pallas_call(
        map_kernel,
        grid=(1,),
        out_shape=(jax.ShapeDtypeStruct((96, 128), i32),) * 2,
        in_specs=[
            SMEM,
            whole_spec(*asked.shape),
            pl.BlockSpec((8 * OWNERS, 128), lambda i: (0, 0)),
            pl.BlockSpec((8 * OWNERS, 128), lambda i: (0, 1)),
            whole_spec(*map_t.shape),
            pl.BlockSpec(memory_space=pl.ANY),
        ],
        out_specs=(whole_spec(96, 128),) * 2,
        scratch_shapes=[pltpu.VMEM((96, 128), i32)],
        cost_estimate=cost(4e9),
        compiler_params=params(16),
    )(is_hot.astype(i32).reshape(1), asked, hbm(hot_all), hbm(hot_all), map_t, hbm(field_grad))
    blocks = [along_task(sent_blocks[shift - 1], shift).astype(f32) for shift in (1, 2, 3)]
    field_grad = field_grad + (blocks[0] + blocks[1] + blocks[2])
    lookup_grad = (field_grad / bag_len.astype(f32)).astype(bf16)
    lookup_grad, rows, samps = lax.optimization_barrier((lookup_grad, rows, samps))

    place4 = jnp.stack([depth, across, core, jnp.where(is_hot, 3, 1)]).astype(i32)
    near = jnp.stack([lookup_grad] + [along_x(lookup_grad, shift) for shift in (1, 2, 3)])
    near_sib = across_core(near)
    table_grad = None
    up, down = near, near
    every = (0, 1, 2, 3)
    steps, ready = ((0, every),), [near, near_sib]
    for step in (1, 2, 3):
        up, down = along_z(up, 1), along_z(down, 7)
        table_grad = scatter_call(steps, place4, rows, samps, ready, table_grad)
        table_grad, up, down = lax.optimization_barrier((table_grad, up, down))
        steps = ((step, every), (-step, every))
        ready = [up, across_core(up), down, across_core(down)]
    far = [along_z(up[:2], 1), along_z(down[2:], 7)]
    table_grad = scatter_call(steps, place4, rows, samps, ready, table_grad)
    table_grad, *far = lax.optimization_barrier((table_grad, *far))
    table_grad = scatter_call(
        ((4, (0, 1)), (4, (2, 3))),
        place4,
        rows,
        samps,
        [far[0], across_core(far[0]), far[1], across_core(far[1])],
        table_grad,
        last=True,
    )
    return (logit_own, table_grad[None])


def solution(mesh):
    return jax.shard_map(
        local,
        mesh=mesh,
        in_specs=(
            P(("table", "fsdp"), "task", None),
            P(("table", "fsdp"), "task"),
            P(("table", "fsdp"), "task"),
            P("task", ("table", "fsdp"), None),
            P("task", ("table", "fsdp")),
            P("task", "fsdp", None),
            P("task", "fsdp", None),
            P(),
            P("task", "fsdp", None),
            P("task", None),
        ),
        out_specs=(P(("table", "fsdp"), "task"), P("task", ("table", "fsdp"), None)),
        check_vma=False,
    )
```
